32 devices in a mesh: dp: 8 (over z, x), chan: 4 (over y, core).
Axes of the slice: x: 2, y: 2, z: 4, core: 2. Of those that a mesh axis runs over, the one named last changes fastest.
Arguments:
- tokens: bfloat16 [32768, 768], P('dp', 'chan'), may hold values from -6 to 6
- norm1_gain: bfloat16 [768], P('chan'), may hold values from 0.099609375 to 1.8984375
- norm1_bias: bfloat16 [768], P('chan'), may hold values from -3 to 3
- qkv_weight: bfloat16 [3, 768, 768], P(None, None, 'chan'), may hold values from -0.21875 to 0.21875
- qv_bias: bfloat16 [2, 768], P(None, 'chan'), may hold values from -3 to 3
- pair_bias: bfloat16 [1024, 1024], replicated, may hold values from 0 to 4
- out_weight: bfloat16 [768, 768], P('chan'), may hold values from -2.5 to 2.5
- out_bias: bfloat16 [768], P('chan'), may hold values from -2 to 2
- norm2_gain: bfloat16 [768], P('chan'), may hold values from 0.099609375 to 1.8984375
- norm2_bias: bfloat16 [768], P('chan'), may hold values from -3 to 3
- up_weight: bfloat16 [768, 3072], P(None, 'chan'), may hold values from -0.21875 to 0.21875
- up_bias: bfloat16 [3072], P('chan'), may hold values from -3 to 3
- down_weight: bfloat16 [3072, 768], P('chan'), may hold values from -0.109375 to 0.109375
- down_bias: bfloat16 [768], P('chan'), may hold values from -2 to 2
- lengths: int32 [16], P('dp'), may hold values from 64 to 2048, as said below
- cotangent: bfloat16 [32768, 768], P('dp', 'chan'), may hold values from -6 to 6
Outputs:
- layer_out: bfloat16 [32768, 768], P('dp', 'chan')
- input_grad: bfloat16 [32768, 768], P('dp', 'chan')
- norm1_gain_grad: float32 [768], P('chan')
- norm1_bias_grad: float32 [768], P('chan')
- qkv_weight_grad: float32 [3, 768, 768], P(None, None, 'chan')
- qv_bias_grad: float32 [2, 768], P(None, 'chan')
- pair_bias_grad: float32 [1024, 1024], replicated
- out_weight_grad: float32 [768, 768], P('chan')
- out_bias_grad: float32 [768], P('chan')
- norm2_gain_grad: float32 [768], P('chan')
- norm2_bias_grad: float32 [768], P('chan')
- up_weight_grad: float32 [768, 3072], P(None, 'chan')
- up_bias_grad: float32 [3072], P('chan')
- down_weight_grad: float32 [3072, 768], P('chan')
- down_bias_grad: float32 [768], P('chan')
The draws below stay inside these ranges and needn't reach their ends.
Inputs may be any that keep to these rules, and one draw needn't show every extreme that they name: `lengths`: each index of dp holds 2 whole sequences in a row, padded to 2048 rows each; in every such group one sequence is exactly 2048 long.
All inputs are finite; a program needn't handle non-finite values.
Results may differ from the reference program's by a relative error of at most 0.0089.
Values may be sent and summed in bfloat16 or wider, within the bound.
No kernel may reach another device: no remote copies, remote signals or barrier semaphores. Data moves between devices by JAX's collectives and lax.ppermute only.
A program may use at most 256 MiB of HBM per device.

```python
import jax
import jax.numpy as jnp
from jax import lax

D = 768
FF = 3072
PAIR = 1024
WIN = 256
BLOCK = 512
LEN = 2048
MINLEN = 64
SEQ_DEV = 2
SEQS = 16
TOKENS = 32768


def draw_lengths(key, part):
    key = jax.random.fold_in(key, 7)
    first_key, second_key = jax.random.split(key)
    ranks = jax.random.randint(first_key, (SEQS,), 0, 64)
    base_len = MINLEN + (LEN - MINLEN) * ranks * ranks // 3969
    chosen = jax.random.randint(second_key, (SEQS // SEQ_DEV,), 0, SEQ_DEV)
    position = jnp.arange(SEQS, dtype=jnp.int32) % SEQ_DEV
    full_row = position == jnp.repeat(chosen, SEQ_DEV)
    return jnp.where(full_row, LEN, base_len).astype(jnp.int32)


def levels(own_key, dims, pieces, smallest, top_value):
    loudness = 1.0
    for dim, shards_of in pieces:
        heights = jax.random.uniform(jax.random.fold_in(jax.random.fold_in(own_key, 6), dim), (shards_of,), jnp.float32, smallest / len(pieces), top_value / len(pieces))
        loudness = loudness * jnp.repeat(jnp.exp(heights), dims[dim] // shards_of).reshape((-1,) + (1,) * (len(dims) - 1 - dim))
    return loudness


def bell_draw(stream_key, shape, scale, most, cuts=(), held_as=jnp.bfloat16):
    values = jax.random.normal(stream_key, shape, jnp.float32) * scale
    if len(cuts) > 0:
        values = levels(stream_key, shape, cuts, -0.22, 0.18) * values
    return jnp.clip(values, min=-most, max=most).astype(held_as)


def setup_inputs(seed: int = 0) -> dict:
    keys = jax.random.split(jax.random.key(seed), 17)
    return {
        "tokens": bell_draw(keys[0], (TOKENS, D), 1.0, 6.0, ((0, 8), (1, 4))),
        "norm1_gain": jnp.clip(1.0 + 0.18 * jax.random.normal(keys[1], (D,), jnp.float32), 0.099609375, 1.8984375).astype(jnp.bfloat16),
        "norm1_bias": bell_draw(keys[2], (D,), 0.5, 3.0, ((0, 4),)),
        "qkv_weight": bell_draw(keys[3], (3, D, D), D ** -0.5, 0.21875, ((2, 4),)),
        "qv_bias": bell_draw(keys[4], (2, D), 0.5, 3.0, ((1, 4),)),
        "pair_bias": jnp.clip(jax.random.uniform(keys[5], (PAIR, PAIR), jnp.float32, 0.0, 4.0), 0.0, 4.0).astype(jnp.bfloat16),
        "out_weight": bell_draw(keys[6], (D, D), (max(1, D * 16 // LEN)) ** -0.5, 2.5, ((0, 4),)),
        "out_bias": bell_draw(keys[7], (D,), 0.3, 2.0, ((0, 4),)),
        "norm2_gain": jnp.clip(1.0 + 0.18 * jax.random.normal(keys[8], (D,), jnp.float32), 0.099609375, 1.8984375).astype(jnp.bfloat16),
        "norm2_bias": bell_draw(keys[9], (D,), 0.5, 3.0, ((0, 4),)),
        "up_weight": bell_draw(keys[10], (D, FF), D ** -0.5, 0.21875, ((1, 4),)),
        "up_bias": bell_draw(keys[11], (FF,), 0.5, 3.0, ((0, 4),)),
        "down_weight": bell_draw(keys[12], (FF, D), FF ** -0.5, 0.109375, ((0, 4),)),
        "down_bias": bell_draw(keys[13], (D,), 0.3, 2.0, ((0, 4),)),
        "lengths": draw_lengths(jax.random.fold_in(keys[16], 71), 0),
        "cotangent": bell_draw(keys[15], (TOKENS, D), 1.0, 6.0, ((0, 8), (1, 4))),
    }


@jax.custom_vjp
def low(v):
    return lax.optimization_barrier(v.astype(jnp.bfloat16)).astype(jnp.float32)

@jax.custom_vjp
def low_back(v):
    return v

def low_keep(v):
    return (low(v), None)

def low_pass(kept, grad):
    return (grad,)

def back_keep(v):
    return (v, None)

def back_low(kept, grad):
    return (low(grad),)
low.defvjp(low_keep, low_pass)
low_back.defvjp(back_keep, back_low)
EPSILON = 1e-05

def layer_norm(values, gain_vals, shift_vals):
    row_mean = lax.optimization_barrier(jnp.mean(values, axis=-1, keepdims=True))
    spread = lax.optimization_barrier(jnp.mean(values * values, axis=-1, keepdims=True)) - row_mean * row_mean
    return (values - row_mean) * lax.rsqrt(spread + EPSILON) * gain_vals + shift_vals

def band_rows():
    row_ids = lax.broadcasted_iota(jnp.int32, (BLOCK, PAIR), 0)
    col_ids = lax.broadcasted_iota(jnp.int32, (BLOCK, PAIR), 1)
    return (jnp.abs(row_ids + WIN - col_ids) < WIN).astype(jnp.float32)

def window_sums(stacked, pair_vals):
    padded = jnp.pad(stacked, ((WIN, WIN), (0, 0)))
    band_mask = band_rows()
    anchor = jnp.int32(0)

    def one_block(block_id):
        row_start = block_id * BLOCK
        rows_of = lax.dynamic_slice(pair_vals, (row_start % PAIR, anchor), (BLOCK, PAIR))
        shifted = jnp.roll(rows_of, WIN - row_start, axis=1)
        weights = low(band_mask * (jnp.exp(shifted) - 1.0))
        extent = lax.dynamic_slice(padded, (row_start, anchor), (PAIR, stacked.shape[1]))
        return jnp.dot(weights, extent, precision=lax.Precision.HIGHEST)
    blocks = lax.map(jax.checkpoint(one_block), jnp.arange(LEN // BLOCK, dtype=jnp.int32))
    return blocks.reshape(LEN, stacked.shape[1])

def sequence_layer(params, rows_in, length):
    norm1_gain, norm1_bias, qkv_weight, qv_bias, pair_bias, out_weight, out_bias, norm2_gain, norm2_bias, up_weight, up_bias, down_weight, down_bias = params
    live_rows = (jnp.arange(LEN, dtype=jnp.int32) < length).astype(jnp.float32)[:, None]
    normed = low(layer_norm(rows_in, norm1_gain, norm1_bias))
    projected = jnp.einsum('td,kdc->ktc', normed, qkv_weight, precision=lax.Precision.HIGHEST)
    queries = low_back(projected[0] + qv_bias[0])
    key_proj = low_back(projected[1])
    value_proj = low_back(projected[2] + qv_bias[1])
    exp_keys = live_rows * jnp.exp(key_proj)
    carried = exp_keys * value_proj
    stacked = low(jnp.concatenate([carried, exp_keys], axis=1))
    windowed = low_back(window_sums(stacked, pair_bias))
    numerator = lax.optimization_barrier(jnp.sum(carried, axis=0)) + windowed[:, :D]
    denominator = lax.optimization_barrier(jnp.sum(exp_keys, axis=0)) + windowed[:, D:]
    mix_ratio = numerator / denominator
    gate_vals = jax.nn.sigmoid(queries)
    mixed_rows = low(live_rows * gate_vals * mix_ratio)
    branch = low_back(jnp.dot(mixed_rows, out_weight, precision=lax.Precision.HIGHEST) + out_bias)
    residual = rows_in + live_rows * branch
    normed_two = low(layer_norm(residual, norm2_gain, norm2_bias))
    hidden = low_back(jnp.dot(normed_two, up_weight, precision=lax.Precision.HIGHEST) + up_bias)
    activated = low(jax.nn.gelu(hidden, approximate=True))
    down_out = low_back(jnp.dot(activated, down_weight, precision=lax.Precision.HIGHEST) + down_bias)
    return residual + live_rows * down_out

def reference(tokens, norm1_gain, norm1_bias, qkv_weight, qv_bias, pair_bias, out_weight, out_bias, norm2_gain, norm2_bias, up_weight, up_bias, down_weight, down_bias, lengths, cotangent):
    params = tuple((member.astype(jnp.float32) for member in (norm1_gain, norm1_bias, qkv_weight, qv_bias, pair_bias, out_weight, out_bias, norm2_gain, norm2_bias, up_weight, up_bias, down_weight, down_bias)))
    layer_step = jax.checkpoint(sequence_layer)

    def forward(params_in, flat_rows):
        sequences = flat_rows.reshape(SEQS, LEN, D)

        def advance(scan_state, member):
            return (scan_state, layer_step(params_in, member[0], member[1]))
        _, outputs = lax.scan(advance, jnp.zeros((), jnp.float32), (sequences, lengths))
        return outputs.reshape(TOKENS, D)
    result, pull_back = jax.vjp(forward, params, tokens.astype(jnp.float32))
    gradients, input_grad = pull_back(cotangent.astype(jnp.float32))
    return (result.astype(jnp.bfloat16), input_grad.astype(jnp.bfloat16), gradients[0], gradients[1], gradients[2], gradients[3], gradients[4], gradients[5], gradients[6], gradients[7], gradients[8], gradients[9], gradients[10], gradients[11], gradients[12])
```

```python
import jax
import jax.numpy as jnp
from jax import lax
from jax.sharding import PartitionSpec as P

D = 768
PAIR = 1024
WIN = 256
LEN = 2048
CHAN = 4
EPSILON = 1e-05
BF = jnp.bfloat16
F32 = jnp.float32


def flip(values, axis, mask):
    size = lax.axis_size(axis)
    return lax.ppermute(values, axis, [(i, i ^ mask) for i in range(size)])


def dot_f32(left, right, dims):
    return lax.dot_general(left, right, (dims, ((), ())), preferred_element_type=F32)


def mm(left, right):
    return dot_f32(left, right, ((1,), (0,)))


def mm_t(left, right):
    return dot_f32(left, right, ((1,), (1,)))


def t_mm(left, right):
    return dot_f32(left, right, ((0,), (0,)))


def pick(pieces, index):
    low, high = index % 2 == 1, index // 2 == 1
    a, b, c, d = pieces
    a, b = jnp.where(low, b, a), jnp.where(low, a, b)
    c, d = jnp.where(low, d, c), jnp.where(low, c, d)
    a, c = jnp.where(high, c, a), jnp.where(high, a, c)
    b, d = jnp.where(high, d, b), jnp.where(high, b, d)
    return [a, b, c, d]


def rows_in(values, me):
    rows = values.shape[0] // CHAN
    pieces = [lax.dynamic_slice_in_dim(values, (me ^ r) * rows, rows, 0) for r in range(CHAN)]
    pieces = pieces[:1] + [flip(pieces[r], "chan", r) for r in range(1, CHAN)]
    return jnp.concatenate(pick(pieces, me), axis=1)


def rows_out(values, me):
    cols = values.shape[1] // CHAN
    rows = values.shape[0]
    pieces = pick([values[:, r * cols : (r + 1) * cols] for r in range(CHAN)], me)
    pieces = pieces[:1] + [flip(pieces[r], "chan", r) for r in range(1, CHAN)]
    out = jnp.zeros((CHAN * rows, cols), values.dtype)
    for r in range(CHAN):
        out = lax.dynamic_update_slice_in_dim(out, pieces[r], (me ^ r) * rows, 0)
    return out


def shards(weight):
    near = flip(weight, "chan", 1)
    far = flip(weight, "chan", 2)
    return [weight, near, far, flip(far, "chan", 1)]


def dp_stages():
    size = lax.axis_size("dp")
    stages, mask = [[1]], 2
    while mask < size:
        if mask * 2 < size:
            stages.append([mask, mask * 2, mask * 3])
            mask *= 4
        else:
            stages.append([mask])
            mask *= 2
    return stages


def group_index(index, masks):
    return (index // masks[0]) % (len(masks) + 1)


def dp_sum(values):
    me = lax.axis_index("dp")
    stages = dp_stages()
    for masks in stages:
        own = group_index(me, masks)
        parts = len(masks) + 1
        rows = values.shape[0] // parts
        got = [
            flip(
                lax.dynamic_slice_in_dim(values, (own ^ k) * rows, rows, 0), "dp", masks[0] * k
            )
            for k in range(1, parts)
        ]
        total = lax.dynamic_slice_in_dim(values, own * rows, rows, 0).astype(F32)
        for g in got:
            total = total + g.astype(F32)
        values = total.astype(BF)
    for masks in reversed(stages):
        own = group_index(me, masks)
        parts = len(masks) + 1
        rows = values.shape[0]
        out = jnp.zeros((parts * rows, values.shape[1]), values.dtype)
        out = lax.dynamic_update_slice_in_dim(out, values, own * rows, 0)
        for k in range(1, parts):
            got = flip(values, "dp", masks[0] * k)
            out = lax.dynamic_update_slice_in_dim(out, got, (own ^ k) * rows, 0)
        values = out
    return values


def weight_sum(grads):
    far = grads[2] + flip(grads[3].astype(BF), "chan", 1).astype(F32)
    near = grads[0] + flip(grads[1].astype(BF), "chan", 1).astype(F32)
    own = near + flip(far.astype(BF), "chan", 2).astype(F32)
    return dp_sum(own.astype(BF)).astype(F32)


def all_sum(values):
    for k in (1, 2):
        values = values + flip(values, "chan", k)
    for masks in dp_stages():
        got = [flip(values, "dp", m) for m in masks]
        for g in got:
            values = values + g
    return values


def pair_sum_all(values):
    me = lax.axis_index("chan")
    for bit in (1, 2):
        rows = values.shape[0] // 2
        own = (me // bit) % 2
        got = flip(lax.dynamic_slice_in_dim(values, (1 - own) * rows, rows, 0), "chan", bit)
        kept = lax.dynamic_slice_in_dim(values, own * rows, rows, 0)
        values = (kept.astype(F32) + got.astype(F32)).astype(BF)
    values = dp_sum(values)
    for bit in (2, 1):
        own = (me // bit) % 2
        got = flip(values, "chan", bit)
        first = jnp.where(own == 0, values, got)
        second = jnp.where(own == 0, got, values)
        values = jnp.concatenate([first, second], axis=0)
    return values


def norm_forward(values, gain_vals, shift_vals):
    row_mean = jnp.mean(values, axis=1, keepdims=True)
    spread = jnp.mean(values * values, axis=1, keepdims=True) - row_mean * row_mean
    inv_scale = lax.rsqrt(spread + EPSILON)
    centred = (values - row_mean) * inv_scale
    return centred, inv_scale, (centred * gain_vals + shift_vals).astype(BF)


def norm_backward(grad_out, centred, inv_scale, gain_vals):
    scaled = grad_out * gain_vals
    plain = jnp.mean(scaled, axis=1, keepdims=True)
    crossed = jnp.mean(scaled * centred, axis=1, keepdims=True)
    grad_in = inv_scale * (scaled - plain - centred * crossed)
    return grad_in, jnp.sum(grad_out * centred, axis=0), jnp.sum(grad_out, axis=0)


def gelu_pair(u):
    c0, c1 = 0.7978845608, 0.044715
    sq = u * u
    t = jnp.tanh(c0 * u * (1.0 + c1 * sq))
    half = 0.5 * (1.0 + t)
    slope = half + 0.5 * u * (1.0 - t * t) * (c0 * (1.0 + 3.0 * c1 * sq))
    return u * half, slope


def body(
    tokens,
    norm1_gain,
    norm1_bias,
    qkv_weight,
    qv_bias,
    pair_bias,
    out_weight,
    out_bias,
    norm2_gain,
    norm2_bias,
    up_weight,
    up_bias,
    down_weight,
    down_bias,
    lengths,
    cotangent,
):
    me = lax.axis_index("chan")
    half = me % 2
    rows = tokens.shape[0] // CHAN
    blocks = rows // WIN
    width = D // CHAN
    length = lax.dynamic_index_in_dim(lengths, me // 2, 0, keepdims=False)
    place = lax.broadcasted_iota(jnp.int32, (rows, 1), 0) + half * rows
    live = (place < length).astype(F32)

    small = jnp.stack(
        [norm1_gain, norm1_bias, qv_bias[0], qv_bias[1], out_bias, norm2_gain, norm2_bias, down_bias]
    )
    small = jnp.concatenate([small, up_bias.reshape(CHAN, width)], axis=0)
    small_rel = [small] + [flip(small, "chan", r) for r in range(1, CHAN)]
    small_abs = jnp.concatenate(pick(small_rel, me), axis=1).astype(F32)
    gain_one, shift_one = small_abs[0], small_abs[1]
    out_shift, gain_two, shift_two, down_shift = (
        small_abs[4],
        small_abs[5],
        small_abs[6],
        small_abs[7],
    )
    q_shift = jnp.concatenate(pick([s[2] for s in small_rel], half)).astype(F32)
    v_shift = jnp.concatenate(pick([s[3] for s in small_rel], half)).astype(F32)
    up_shift = [s[8:].reshape(-1).astype(F32) for s in small_rel]

    x_rows = rows_in(tokens, me).astype(F32)
    qkv_t = jnp.concatenate(pick(shards(jnp.swapaxes(qkv_weight, 1, 2)), half), axis=1)
    out_w = jnp.concatenate(pick(shards(out_weight), half), axis=0)
    up_w = shards(up_weight)
    down_w = shards(down_weight)
    cot = rows_in(cotangent, me).astype(F32)

    pair = pair_bias.astype(F32)
    row_ids = lax.broadcasted_iota(jnp.int32, (WIN, WIN), 0)
    col_ids = lax.broadcasted_iota(jnp.int32, (WIN, WIN), 1)
    masks = [col_ids > row_ids, col_ids >= 0, col_ids < row_ids]

    def pair_block(b, k):
        col = (b - 1 + k) % blocks
        return jnp.exp(pair[b * WIN : (b + 1) * WIN, col * WIN : (col + 1) * WIN])

    terms = [
        jnp.concatenate(
            [jnp.where(masks[k], pair_block(b, k) - 1.0, 0.0).astype(BF) for k in range(3)], axis=1
        )
        for b in range(blocks)
    ]
    terms_t = [
        jnp.concatenate(
            [terms[(s - 1 + k) % blocks][:, (2 - k) * WIN : (3 - k) * WIN] for k in range(3)], axis=0
        )
        for s in range(blocks)
    ]

    def extend(values):
        edge = lax.dynamic_slice_in_dim(values, (1 - half) * (rows - WIN), WIN, 0)
        halo = flip(edge, "chan", 1)
        none = jnp.zeros_like(halo)
        return jnp.concatenate(
            [jnp.where(half == 1, halo, none), values, jnp.where(half == 1, none, halo)], axis=0
        )

    def both_halves(values):
        return values + flip(values, "chan", 1)

    cent_one, inv_one, normed_one = norm_forward(x_rows, gain_one, shift_one)
    queries = mm_t(normed_one, qkv_t[0]) + q_shift
    key_proj = mm_t(normed_one, qkv_t[1])
    value_proj = mm_t(normed_one, qkv_t[2]) + v_shift
    exp_keys = live * jnp.exp(key_proj)
    carried = exp_keys * value_proj
    joined = jnp.concatenate([carried, exp_keys], axis=1)
    totals = both_halves(jnp.sum(joined, axis=0, keepdims=True))
    data_ext = extend(joined.astype(BF))
    windowed = jnp.concatenate(
        [mm(terms[b], data_ext[b * WIN : (b + 3) * WIN]) for b in range(blocks)], axis=0
    )
    merged = totals + windowed
    denominator = merged[:, D:]
    mix_ratio = merged[:, :D] / denominator
    gate = jax.nn.sigmoid(queries)
    mixed = (live * gate * mix_ratio).astype(BF)
    residual = x_rows + live * (mm(mixed, out_w) + out_shift)
    cent_two, inv_two, normed_two = norm_forward(residual, gain_two, shift_two)

    down_grad = (live * cot).astype(BF)
    down_out = jnp.zeros((rows, D), F32)
    norm_two_in = jnp.zeros((rows, D), F32)
    up_grads, down_grads, up_shift_grads = [None] * CHAN, [None] * CHAN, [None] * CHAN
    for r in (0, 1, 3, 2):
        hidden = mm(normed_two, up_w[r]) + up_shift[r]
        act, slope = gelu_pair(hidden)
        act = act.astype(BF)
        down_out = down_out + mm(act, down_w[r])
        hidden_grad = (mm_t(down_grad, down_w[r]) * slope).astype(BF)
        down_grads[r] = t_mm(act, down_grad)
        up_grads[r] = t_mm(normed_two, hidden_grad)
        up_shift_grads[r] = jnp.sum(hidden_grad.astype(F32), axis=0)
        norm_two_in = norm_two_in + mm_t(hidden_grad, up_w[r])
    layer_out = (residual + live * (down_out + down_shift)).astype(BF)
    layer_out = rows_out(layer_out, me)
    down_weight_grad = weight_sum(down_grads)
    up_weight_grad = weight_sum(up_grads)

    back_two, gain_two_grad, shift_two_grad = norm_backward(
        norm_two_in, cent_two, inv_two, gain_two
    )
    res_grad = cot + back_two
    branch_grad = (live * res_grad).astype(BF)
    out_grad = t_mm(mixed, branch_grad)
    out_weight_grad = weight_sum(
        pick([out_grad[r * width : (r + 1) * width] for r in range(CHAN)], half)
    )
    mixed_grad = live * mm_t(branch_grad, out_w)
    query_grad = (mixed_grad * mix_ratio * gate * (1.0 - gate)).astype(BF)
    num_grad = mixed_grad * gate / denominator
    den_grad = -num_grad * mix_ratio
    joined_grad = jnp.concatenate([num_grad, den_grad], axis=1)
    grad_totals = both_halves(jnp.sum(joined_grad, axis=0, keepdims=True))
    grad_low = joined_grad.astype(BF)
    grad_ext = extend(grad_low)
    tri = []
    for b in range(blocks):
        prod = mm_t(grad_low[b * WIN : (b + 1) * WIN], data_ext[b * WIN : (b + 3) * WIN])
        side = jnp.where(masks[0], prod[:, :WIN], 0.0) + jnp.where(
            masks[2], prod[:, 2 * WIN :], 0.0
        )
        tri.append(jnp.concatenate([prod[:, WIN : 2 * WIN], side], axis=1))
    packed = pair_sum_all(jnp.concatenate(tri, axis=0).astype(BF)).astype(F32)
    lines = []
    for b in range(blocks):
        own, side = packed[b * WIN : (b + 1) * WIN, :WIN], packed[b * WIN : (b + 1) * WIN, WIN:]
        squares = [jnp.zeros((WIN, WIN), F32)] * blocks
        squares[b] = own * pair_block(b, 1)
        squares[(b - 1) % blocks] = jnp.where(masks[0], side * pair_block(b, 0), 0.0)
        squares[(b + 1) % blocks] = jnp.where(masks[2], side * pair_block(b, 2), 0.0)
        lines.append(jnp.concatenate(squares, axis=1))
    pair_bias_grad = jnp.concatenate(lines, axis=0)

    pulled = grad_totals + jnp.concatenate(
        [t_mm(terms_t[s], grad_ext[s * WIN : (s + 3) * WIN]) for s in range(blocks)], axis=0
    )
    carried_grad, exp_grad = pulled[:, :D], pulled[:, D:]
    value_grad = (carried_grad * exp_keys).astype(BF)
    key_grad = ((exp_grad + carried_grad * value_proj) * exp_keys).astype(BF)
    qkv_grads = [query_grad, key_grad, value_grad]
    qkv_full = jnp.stack([t_mm(g, normed_one) for g in qkv_grads])
    qkv_sum = weight_sum(
        pick([qkv_full[:, r * width : (r + 1) * width].reshape(-1, D) for r in range(CHAN)], half)
    )
    qkv_weight_grad = jnp.swapaxes(qkv_sum.reshape(3, width, D), 1, 2)
    norm_one_in = mm(query_grad, qkv_t[0]) + mm(key_grad, qkv_t[1]) + mm(value_grad, qkv_t[2])
    back_one, gain_one_grad, shift_one_grad = norm_backward(
        norm_one_in, cent_one, inv_one, gain_one
    )
    input_grad = rows_out((res_grad + back_one).astype(BF), me)

    def rel(vector):
        pieces = pick([vector[r * width : (r + 1) * width] for r in range(CHAN)], half)
        return jnp.stack(pick(pieces, me))

    def col_sum(values):
        return jnp.sum(values.astype(F32), axis=0)

    def absolute(vector):
        return vector.reshape(CHAN, width)

    pieces = jnp.stack(
        [
            absolute(gain_one_grad),
            absolute(shift_one_grad),
            rel(col_sum(query_grad)),
            rel(col_sum(value_grad)),
            absolute(col_sum(branch_grad)),
            absolute(gain_two_grad),
            absolute(shift_two_grad),
            absolute(jnp.sum(live * cot, axis=0)),
        ],
        axis=1,
    )
    ups = jnp.stack(pick([g.reshape(CHAN, width) for g in up_shift_grads], me))
    pieces = all_sum(jnp.concatenate([pieces, ups], axis=1))
    mine = lax.dynamic_index_in_dim(pieces, me, 0, keepdims=False)
    return (
        layer_out,
        input_grad,
        mine[0],
        mine[1],
        qkv_weight_grad,
        mine[2:4],
        pair_bias_grad,
        out_weight_grad,
        mine[4],
        mine[5],
        mine[6],
        up_weight_grad,
        mine[8:].reshape(-1),
        down_weight_grad,
        mine[7],
    )


def solution(mesh):
    in_specs = (
        P("dp", "chan"),
        P("chan"),
        P("chan"),
        P(None, None, "chan"),
        P(None, "chan"),
        P(),
        P("chan", None),
        P("chan"),
        P("chan"),
        P("chan"),
        P(None, "chan"),
        P("chan"),
        P("chan", None),
        P("chan"),
        P("dp"),
        P("dp", "chan"),
    )
    out_specs = (
        P("dp", "chan"),
        P("dp", "chan"),
        P("chan"),
        P("chan"),
        P(None, None, "chan"),
        P(None, "chan"),
        P(),
        P("chan", None),
        P("chan"),
        P("chan"),
        P("chan"),
        P(None, "chan"),
        P("chan"),
        P("chan", None),
        P("chan"),
    )
    return jax.shard_map(body, mesh=mesh, in_specs=in_specs, out_specs=out_specs, check_vma=False)
```

```python
import functools

import jax
import jax.numpy as jnp
from jax import lax
from jax.experimental import pallas as pl
from jax.experimental.pallas import tpu as pltpu
from jax.sharding import PartitionSpec as P

D = 768
PAIR = 1024
WIN = 256
LEN = 2048
CHAN = 4
EPSILON = 1e-05
BF = jnp.bfloat16
F32 = jnp.float32
SMEM = pltpu.SMEM
MIB = 1024 * 1024
RB = 512
INPUT_COST = 72


def flip(values, axis, mask):
    size = lax.axis_size(axis)
    return lax.ppermute(values, axis, [(i, i ^ mask) for i in range(size)])


def dot_f32(left, right, dims):
    return lax.dot_general(left, right, (dims, ((), ())), preferred_element_type=F32)


def mm(left, right):
    return dot_f32(left, right, ((1,), (0,)))


def mm_t(left, right):
    return dot_f32(left, right, ((1,), (1,)))


def t_mm(left, right):
    return dot_f32(left, right, ((0,), (0,)))


def pick(pieces, index):
    low, high = index % 2 == 1, index // 2 == 1
    a, b, c, d = pieces
    a, b = jnp.where(low, b, a), jnp.where(low, a, b)
    c, d = jnp.where(low, d, c), jnp.where(low, c, d)
    a, c = jnp.where(high, c, a), jnp.where(high, a, c)
    b, d = jnp.where(high, d, b), jnp.where(high, b, d)
    return [a, b, c, d]


def call(
    kernel, steps, views, out_views, out_shape, scratch=(), flops=0, heavy=0, mem=18, tokens=()
):
    vm = pl.BlockSpec(memory_space=pltpu.VMEM)
    specs = [pl.BlockSpec(memory_space=SMEM) if v is None else vm for v in views]
    every = list(views) + list(out_views)
    first_out, count = len(views) + len(tokens), len(out_views)

    def unrolled(*refs):
        used = refs[: len(views)] + refs[first_out : first_out + count]
        refs[first_out + count][...] = jnp.zeros((8, 128), F32)
        for step in range(steps):
            parts = [r if v is None else v(r, step) for v, r in zip(every, used)]
            kernel(step, steps, *parts, *refs[first_out + count + 1 :])

    run = pl.pallas_call(
        unrolled,
        in_specs=specs + [vm] * len(tokens),
        out_specs=[vm] * (count + 1),
        out_shape=list(out_shape) + [shape_of((8, 128), F32)],
        scratch_shapes=list(scratch),
        compiler_params=pltpu.CompilerParams(vmem_limit_bytes=mem * MIB),
        cost_estimate=pl.CostEstimate(
            flops=flops, bytes_accessed=flops // 300, transcendentals=heavy
        ),
    )
    return lambda *operands: run(*operands, *tokens)


def whole(ref, step):
    return ref


def rows_of(size):
    return lambda ref, step: ref.at[step * size : (step + 1) * size]


def cols_of(size):
    return lambda ref, step: ref.at[:, step * size : (step + 1) * size]


def shape_of(shape, dtype):
    return jax.ShapeDtypeStruct(shape, dtype)


def live_block(info_ref, step, size):
    ids = lax.broadcasted_iota(jnp.int32, (size, 1), 0) + step * size
    return (ids < info_ref[0]).astype(F32)


def normalize(values):
    row_mean = jnp.mean(values, axis=1, keepdims=True)
    spread = jnp.mean(values * values, axis=1, keepdims=True) - row_mean * row_mean
    inv_scale = lax.rsqrt(spread + EPSILON)
    return (values - row_mean) * inv_scale, inv_scale


def norm_back(grad_out, centred, inv_scale, gain_vals):
    scaled = grad_out * gain_vals
    plain = jnp.mean(scaled, axis=1, keepdims=True)
    crossed = jnp.mean(scaled * centred, axis=1, keepdims=True)
    return inv_scale * (scaled - plain - centred * crossed)


def col_sum(values):
    return jnp.sum(values, axis=0, keepdims=True)


def gelu_pair(u):
    c0, c1 = 0.7978845608, 0.044715
    sq = u * u
    half = 0.5 + 0.5 * jnp.tanh(u * (c0 + c0 * c1 * sq))
    slope = half * (1.0 + (1.0 - half) * (u * (2.0 * c0 + 6.0 * c0 * c1 * sq)))
    return u * half, slope


def add_into(ref, step, values):
    ref[...] = values if step == 0 else ref[...] + values


def vector_kernel(step, count, info, small_ref, vec_ref, up_ref):
    width, me = D // CHAN, info[2]
    for k in range(CHAN):
        cols = slice(k * width, (k + 1) * width)
        own = small_ref[me ^ k].astype(F32)
        pair = small_ref[k - k % 2 + (k % 2 + info[1]) % 2].astype(F32)
        vec_ref[0:2, cols] = own[0:2]
        vec_ref[2:4, cols] = pair[2:4]
        vec_ref[4:8, cols] = own[4:8]
        ups = small_ref[k].astype(F32)
        for t in range(CHAN):
            up_ref[k : k + 1, t * width : (t + 1) * width] = ups[8 + t : 9 + t]


def vectors(info, small, tokens=()):
    return call(
        vector_kernel,
        1,
        [None, whole],
        [whole, whole],
        [shape_of((8, D), F32), shape_of((CHAN, D), F32)],
        mem=16,
        tokens=tokens,
    )(info, small)


def chan_row(info, r):
    return (r - r % 2) + (r % 2 + info[1]) % 2


def project_kernel(
    step, count, info, x_ref, vec, w_0, w_1, w_2, w_3, n_ref, gate_ref, v_ref, s_ref, tot_ref, w_ref
):
    width = D // CHAN
    if step == 0:
        for r, ref in enumerate((w_0, w_1, w_2, w_3)):
            row = pl.multiple_of(chan_row(info, r) * width, width)
            for k in range(3):
                w_ref[k, pl.ds(row, width)] = ref[k * width : (k + 1) * width]
    live = live_block(info, step, RB)
    centred, _ = normalize(x_ref[...].astype(F32).T)
    normed = (centred * vec[0:1] + vec[1:2]).astype(BF)
    n_ref[...] = normed
    gate_ref[...] = jax.nn.sigmoid(mm_t(normed, w_ref[0]) + vec[2:3]).astype(BF)
    keys = live * jnp.exp(mm_t(normed, w_ref[1]))
    vals = mm_t(normed, w_ref[2]) + vec[3:4]
    carried = keys * vals
    v_ref[...] = vals.astype(BF)
    s_ref[:, :D] = carried.astype(BF)
    s_ref[:, D:] = keys.astype(BF)
    add_into(tot_ref, step, jnp.concatenate([col_sum(carried), col_sum(keys)], axis=1))


def project(info, x_t, vec, weights, tokens=()):
    rows = x_t.shape[1]
    return call(
        project_kernel,
        rows // RB,
        [None, cols_of(RB)] + [whole] * 5,
        [rows_of(RB)] * 4 + [whole] * 2,
        [shape_of((rows, D), BF)] * 3
        + [shape_of((rows, 2 * D), BF), shape_of((1, 2 * D), F32), shape_of((3, D, D), BF)],
        flops=6 * rows * D * D,
        heavy=rows * D * 2,
        tokens=tokens,
    )(info, x_t, vec, *weights)


def side_masks():
    row_ids = lax.broadcasted_iota(jnp.int32, (WIN, WIN), 0)
    col_ids = lax.broadcasted_iota(jnp.int32, (WIN, WIN), 1)
    return col_ids > row_ids, col_ids < row_ids


def neighbours(info, step, count, ref, halo_ref):
    half = info[1]
    if step == 0:
        left = jnp.where(half == 1, halo_ref[:WIN], jnp.zeros_like(halo_ref[:WIN]))
    else:
        left = ref[(step - 1) * WIN : step * WIN]
    if step == count - 1:
        right = jnp.where(half == 0, halo_ref[:WIN], jnp.zeros_like(halo_ref[:WIN]))
    else:
        right = ref[(step + 1) * WIN : (step + 2) * WIN]
    return left, ref[step * WIN : (step + 1) * WIN], right


def pair_total(tot_ref, far_ref):
    far = far_ref[WIN : WIN + 16].astype(F32)
    return tot_ref[...] + (far[0:1] + far[1:2])


def pair_cols(ref, step, count, side):
    col = (step + side) % count
    return ref[step * WIN : (step + 1) * WIN, col * WIN : (col + 1) * WIN]


def mix_kernel(
    step, count, info, pair_ref, s_ref, far_ref, tot_ref, gate_ref, x_ref, vec,
    w_0, w_1, w_2, w_3, term_ref, ratio_ref, inv_ref, mixed_ref, res_ref, n_ref, w_ref,
):
    width = D // CHAN
    if step == 0:
        for r, ref in enumerate((w_0, w_1, w_2, w_3)):
            row = pl.multiple_of(chan_row(info, r) * width, width)
            w_ref[pl.ds(row, width)] = ref[3 * width :]
    live = live_block(info, step, WIN)
    before, after_own = side_masks()
    left, own, right = neighbours(info, step, count, s_ref, far_ref)
    grow = [jnp.exp(pair_cols(pair_ref, step, count, k).astype(F32)) - 1.0 for k in (-1, 0, 1)]
    term_l = jnp.where(before, grow[0], 0.0).astype(BF)
    term_o = grow[1].astype(BF)
    term_r = jnp.where(after_own, grow[2], 0.0).astype(BF)
    term_ref[:, :WIN] = term_l
    term_ref[:, WIN : 2 * WIN] = term_o
    term_ref[:, 2 * WIN :] = term_r
    merged = mm(term_l, left) + mm(term_o, own) + mm(term_r, right)
    merged = merged + pair_total(tot_ref, far_ref)
    inverse = 1.0 / merged[:, D:]
    ratio = merged[:, :D] * inverse
    mixed = (live * gate_ref[...].astype(F32) * ratio).astype(BF)
    ratio_ref[...] = ratio.astype(BF)
    inv_ref[...] = inverse
    mixed_ref[...] = mixed
    residual = x_ref[...].astype(F32).T + live * (mm(mixed, w_ref[...]) + vec[4:5])
    res_ref[...] = residual
    centred, _ = normalize(residual)
    n_ref[...] = (centred * vec[5:6] + vec[6:7]).astype(BF)


def mix(info, pair_bias, stacked, message, totals, gate, x_t, vec, weights, tokens=()):
    rows = x_t.shape[1]
    return call(
        mix_kernel,
        rows // WIN,
        [None, whole, whole, whole, whole, rows_of(WIN), cols_of(WIN)] + [whole] * 5,
        [rows_of(WIN)] * 6 + [whole],
        [
            shape_of((rows, 3 * WIN), BF),
            shape_of((rows, D), BF),
            shape_of((rows, D), F32),
            shape_of((rows, D), BF),
            shape_of((rows, D), F32),
            shape_of((rows, D), BF),
            shape_of((D, D), BF),
        ],
        flops=2 * rows * D * (6 * WIN + D),
        heavy=rows * D * 2,
        tokens=tokens,
    )(info, pair_bias, stacked, message, totals, gate, x_t, vec, *weights)


def feed_kernel(first, final, extra, step, count, info, n_ref, cot_ref, shift_ref, w_ref, *rest):
    rest = list(rest)
    state = [rest.pop(0), rest.pop(0)] if not first else None
    final_refs = [rest.pop(0), rest.pop(0)] if final else None
    extra_ref = rest.pop(0) if extra else None
    sum_ref, into_ref, ups_ref = rest.pop(0), rest.pop(0), rest.pop(0)
    weight_grad = rest.pop(0)
    if first:
        rest.pop(0)[...] = (cot := cot_ref[...].T)
    else:
        cot = cot_ref[...]
    grad_sc, act_sc, hidden_sc = rest
    live = lax.broadcasted_iota(jnp.int32, (n_ref.shape[0], 1), 0) < info[0]
    grad_sc[...] = jnp.where(live, cot, jnp.zeros_like(cot))
    grad = grad_sc[...]
    for f in range(0, D, WIN):
        cols, low = slice(f, f + WIN), slice(D + f, D + f + WIN)
        hidden = mm(n_ref[...], w_ref[:D, cols]) + shift_ref[:, cols]
        act, slope = gelu_pair(hidden)
        act = act.astype(BF)
        hidden_grad = (mm_t(grad, w_ref[low]) * slope).astype(BF)
        act_sc[:, cols] = act
        hidden_sc[:, cols] = hidden_grad
        ups_ref[:, cols] = col_sum(hidden_grad.astype(F32))
        of_up = t_mm(n_ref[...], hidden_grad)
        of_down = t_mm(act, grad)
        if extra:
            of_up = of_up + extra_ref[:D, cols].astype(F32)
            of_down = of_down + extra_ref[low].astype(F32)
        weight_grad[:D, cols] = of_up.astype(BF)
        weight_grad[low] = of_down.astype(BF)
    total = mm(act_sc[...], w_ref[D:])
    into = mm_t(hidden_sc[...], w_ref[:D])
    if not first:
        total, into = total + state[0][...], into + state[1][...]
    into_ref[...] = into
    if final:
        res_ref, vec = final_refs
        out = res_ref[...] + jnp.where(live, total + vec[7:8], 0.0)
        sum_ref[...] = out.T.astype(BF)
    else:
        sum_ref[...] = total


def feed(info, normed, cot, shift, weights, state=None, final=None, extra=None, tokens=()):
    rows = normed.shape[0]
    operands = [info, normed, cot, shift, weights]
    operands += list(state or ()) + list(final or ()) + ([] if extra is None else [extra])
    out_shape = [
        shape_of((rows, D), F32) if final is None else shape_of((D, rows), BF),
        shape_of((rows, D), F32),
        shape_of((1, D), F32),
    ]
    out_shape.append(shape_of((2 * D, D), BF))
    if state is None:
        out_shape.append(shape_of((rows, D), BF))
    flags = (state is None, final is not None, extra is not None)
    return call(
        functools.partial(feed_kernel, *flags),
        1,
        [None] + [whole] * (len(operands) - 1),
        [whole] * len(out_shape),
        out_shape,
        scratch=[pltpu.VMEM((rows, D), BF)] * 3,
        flops=12 * rows * D * D,
        heavy=rows * D,
        mem=18,
        tokens=tokens,
    )(*operands)


def branch_kernel(
    step, count, info, into_ref, res_ref, cot_ref, vec, w_ref, ratio_ref, inv_ref, gate_ref,
    resg_ref, branch_ref, qg_ref, g_ref, tot_ref, cols_ref,
):
    live = live_block(info, step, RB)
    upstream = into_ref[...]
    centred, inv_scale = normalize(res_ref[...])
    cot = cot_ref[...].astype(F32)
    res_grad = cot + norm_back(upstream, centred, inv_scale, vec[5:6])
    resg_ref[...] = res_grad
    branch = (live * res_grad).astype(BF)
    branch_ref[...] = branch
    mixed_grad = live * mm_t(branch, w_ref[...])
    gate, ratio = gate_ref[...].astype(F32), ratio_ref[...].astype(F32)
    pulled = mixed_grad * gate
    qg_ref[...] = (pulled * ratio * (1.0 - gate)).astype(BF)
    num = pulled * inv_ref[...]
    den = -num * ratio
    g_ref[:, :D] = num.astype(BF)
    g_ref[:, D:] = den.astype(BF)
    add_into(tot_ref, step, jnp.concatenate([col_sum(num), col_sum(den)], axis=1))
    cols = [
        col_sum(upstream * centred),
        col_sum(upstream),
        col_sum(branch.astype(F32)),
        col_sum(live * cot),
        jnp.zeros((4, D), F32),
    ]
    add_into(cols_ref, step, jnp.concatenate(cols, axis=0))


def branch_back(info, into, residual, cot, vec, out_w, ratio, inverse, gate, tokens=()):
    rows = cot.shape[0]
    wide = rows_of(RB)
    return call(
        branch_kernel,
        rows // RB,
        [None, wide, wide, wide, whole, whole, wide, wide, wide],
        [wide, wide, wide, wide, whole, whole],
        [
            shape_of((rows, D), F32),
            shape_of((rows, D), BF),
            shape_of((rows, D), BF),
            shape_of((rows, 2 * D), BF),
            shape_of((1, 2 * D), F32),
            shape_of((8, D), F32),
        ],
        flops=2 * rows * D * D,
        tokens=tokens,
    )(info, into, residual, cot, vec, out_w, ratio, inverse, gate)


def window_kernel(
    step, count, info, t_ref, g_ref, gfar_ref, tot_ref, s_ref, sfar_ref, v_ref,
    kg_ref, vg_ref, pair_ref,
):
    before, after_own = side_masks()
    left, own, right = neighbours(info, step, count, g_ref, gfar_ref)

    def term(block, part):
        block = block % count
        return t_ref[block * WIN : (block + 1) * WIN, part * WIN : (part + 1) * WIN]

    pulled = t_mm(term(step - 1, 2), left) + t_mm(term(step, 1), own)
    pulled = pulled + t_mm(term(step + 1, 0), right) + pair_total(tot_ref, gfar_ref)
    carried_grad, exp_grad = pulled[:, :D], pulled[:, D:]
    left, data, right = neighbours(info, step, count, s_ref, sfar_ref)
    keys = data[:, D:].astype(F32)
    vg_ref[...] = (carried_grad * keys).astype(BF)
    kg_ref[...] = ((exp_grad + carried_grad * v_ref[...].astype(F32)) * keys).astype(BF)
    pair_ref[:, :WIN] = mm_t(own, data).astype(BF)
    side = jnp.where(before, mm_t(own, left), 0.0) + jnp.where(after_own, mm_t(own, right), 0.0)
    pair_ref[:, WIN:] = side.astype(BF)


def window_back(info, terms, grads, grad_message, grad_totals, stacked, message, vals, tokens=()):
    rows = vals.shape[0]
    return call(
        window_kernel,
        rows // WIN,
        [None, whole, whole, whole, whole, whole, whole, rows_of(WIN)],
        [rows_of(WIN)] * 3,
        [shape_of((rows, D), BF), shape_of((rows, D), BF), shape_of((rows, 2 * WIN), BF)],
        flops=8 * rows * D * 3 * WIN,
        tokens=tokens,
    )(info, terms, grads, grad_message, grad_totals, stacked, message, vals)


def mixing_grads_kernel(
    step, count, info, q_ref, k_ref, v_ref, m_ref, n_ref, b_ref, pair_ref, two_ref, ups_ref,
    keep_near, keep_far, send_ref, pack_ref,
):
    half, me = info[1], info[2]
    width = D // CHAN
    keep_refs = (keep_near, keep_far)
    products = [t_mm(ref[...], n_ref[...]).astype(BF) for ref in (q_ref, k_ref, v_ref)]
    products.append(t_mm(m_ref[...], b_ref[...]).astype(BF))

    def store(core, far, rows, values):
        @pl.when(half == core)
        def _():
            keep_refs[far][rows] = values

        @pl.when(half != core)
        def _():
            send_ref[far, rows] = values

    for k, product in enumerate(products):
        for far in range(2):
            for core in range(2):
                b = 2 * far + core
                rows = slice(k * width, (k + 1) * width)
                store(core, far, rows, product[b * width : (b + 1) * width])

    sums = [col_sum(q_ref[...].astype(F32)), col_sum(v_ref[...].astype(F32))]
    turned = [jnp.concatenate([t[:, D // 2 :], t[:, : D // 2]], axis=1) for t in sums]
    pack_ref[0:2] = jnp.zeros((2, D), F32)
    pack_ref[2:6] = two_ref[0:4]
    for k in range(2):
        pack_ref[6 + k : 7 + k] = jnp.where(me // 2 == 1, turned[k], sums[k])
    for r in range(CHAN):
        pack_ref[pl.ds(8 + (me ^ r), 1)] = ups_ref[r : r + 1]
    pack_ref[12:16] = jnp.zeros((4, D), F32)

    for r in range(CHAN):
        target = keep_refs[r // 2] if r % 2 == 0 else send_ref.at[r // 2]
        block = me ^ r
        rows = slice(D, D + WIN)
        target[rows, : 2 * WIN] = pair_ref[pl.ds(pl.multiple_of(block * WIN, WIN), WIN)]
        lines = [pack_ref[pl.ds(3 * block + i, 1)] for i in range(3)]
        lines = [line[:, t * WIN : (t + 1) * WIN] for line in lines for t in range(3)]
        lines = jnp.concatenate(lines + [jnp.zeros((WIN - 9, WIN), F32)], axis=0)
        target[rows, 2 * WIN :] = lines.astype(BF)


def mixing_grads(info, q_grad, k_grad, v_grad, mixed, normed, branch, pair_grad, two, ups, tokens=()):
    rows = normed.shape[0]
    return call(
        mixing_grads_kernel,
        1,
        [None] + [whole] * 9,
        [whole] * 3,
        [shape_of((D + WIN, D), BF)] * 2 + [shape_of((2, D + WIN, D), BF)],
        scratch=[pltpu.VMEM((16, D), F32)],
        flops=8 * rows * D * D,
        mem=18,
        tokens=tokens,
    )(info, q_grad, k_grad, v_grad, mixed, normed, branch, pair_grad, two, ups)


def input_kernel(step, count, q_ref, k_ref, v_ref, w_ref, x_ref, vec, resg_ref, out_ref, cols_ref):
    upstream = mm(q_ref[...], w_ref[0]) + mm(k_ref[...], w_ref[1]) + mm(v_ref[...], w_ref[2])
    centred, inv_scale = normalize(x_ref[...].astype(F32).T)
    grad = resg_ref[...] + norm_back(upstream, centred, inv_scale, vec[0:1])
    out_ref[...] = grad.T.astype(BF)
    cols = [col_sum(upstream * centred), col_sum(upstream), jnp.zeros((6, D), F32)]
    add_into(cols_ref, step, jnp.concatenate(cols, axis=0))


def input_back(q_grad, k_grad, v_grad, weights, x_t, vec, res_grad, tokens=()):
    rows = res_grad.shape[0]
    wide = rows_of(RB)
    return call(
        input_kernel,
        rows // RB,
        [wide, wide, wide, whole, cols_of(RB), whole, wide],
        [cols_of(RB), whole],
        [shape_of((D, rows), BF), shape_of((8, D), F32)],
        flops=INPUT_COST * rows * D * D,
        tokens=tokens,
    )(q_grad, k_grad, v_grad, weights, x_t, vec, res_grad)


def sync(*arrays):
    return lax.optimization_barrier(arrays)


def row_pieces(values, rows):
    return values.reshape(-1, CHAN, rows).swapaxes(0, 1)


def to_rows(pieces):
    pieces = lax.all_to_all(pieces, "chan", 0, 0, tiled=True)
    return pieces.reshape(-1, pieces.shape[2])


def exchange_near(pieces):
    return flip(jnp.stack([pieces[1], pieces[3]]), "chan", 1)


def exchange_far(pieces, near):
    return flip(jnp.stack([pieces[2], near[1]]), "chan", 2)


def columns(pieces, near, far, me):
    return jnp.concatenate(pick([pieces[0], near[0], far[0], far[1]], me), axis=1).T


def split_rows(values, count):
    size = values.shape[0] // count
    return [values[k * size : (k + 1) * size] for k in range(count)]


def take(values, index, size, axis=0):
    return lax.dynamic_slice_in_dim(values, index * size, size, axis)


def unpack_kernel(step, count, info, packed_ref, pair_ref, out_ref, small_ref, *vectors):
    before, after_own = side_masks()
    grow = [jnp.exp(pair_cols(pair_ref, step, count, k).astype(F32)) for k in (-1, 0, 1)]
    own = packed_ref[step, :, :WIN].astype(F32)
    side = packed_ref[step, :, WIN : 2 * WIN].astype(F32)
    squares = [jnp.zeros((WIN, WIN), F32)] * count
    squares[step] = own * grow[1]
    squares[(step - 1) % count] = jnp.where(before, side * grow[0], 0.0)
    squares[(step + 1) % count] = jnp.where(after_own, side * grow[2], 0.0)
    for k in range(count):
        out_ref[:, k * WIN : (k + 1) * WIN] = squares[k]
    if step == count - 1:
        me, width = info[2], D // CHAN
        lines = []
        for b in range(CHAN):
            part = packed_ref[b, :16, 2 * WIN :].astype(F32)
            for i in range(3):
                lines.append(
                    jnp.concatenate([part[3 * i + t : 3 * i + t + 1] for t in range(3)], axis=1)
                )
        every = jnp.concatenate(lines, axis=0)
        mine = every[:8, :width]
        for k in range(1, CHAN):
            mine = jnp.where(me == k, every[:8, k * width : (k + 1) * width], mine)
        ups = every[8:9]
        for k in range(1, CHAN):
            ups = jnp.where(me == k, every[8 + k : 9 + k], ups)
        small_ref[:, :width] = mine
        small_ref[:, width:] = jnp.zeros((8, D - width), F32)
        vectors[0][...] = ups


def unpack_pairs(info, packed, pair_bias, tokens=()):
    size = pair_bias.shape[0]
    return call(
        unpack_kernel,
        size // WIN,
        [None, whole, whole],
        [rows_of(WIN), whole, whole],
        [shape_of((size, size), F32), shape_of((8, D), F32), shape_of((1, D), F32)],
        heavy=size * WIN * 3,
        tokens=tokens,
    )(info, packed, pair_bias)


def dp_stages():
    size = lax.axis_size("dp")
    stages, mask = [[1]], 2
    while mask < size:
        if mask * 2 < size:
            stages.append([mask, mask * 2, mask * 3])
            mask *= 4
        else:
            stages.append([mask])
            mask *= 2
    return stages


def add(first, second):
    return first.astype(F32) + second.astype(F32)


def dp_groups(masks):
    size = lax.axis_size("dp")
    low, count = masks[0], len(masks) + 1
    starts = [i for i in range(size) if (i // low) % count == 0]
    return [[i + low * k for k in range(count)] for i in starts]


def own_share(masks):
    return (lax.axis_index("dp") // masks[0]) % (len(masks) + 1)


def scatter_start(values, masks):
    count = len(masks) + 1
    n, rows, cols = values.shape[0], values.shape[1] // count, values.shape[2]
    if count == 2:
        return flip(take(values, 1 - own_share(masks), rows, 1), "dp", masks[0])
    parts = values.reshape(n, count, rows, cols).swapaxes(0, 1)
    return lax.all_to_all(parts, "dp", 0, 0, axis_index_groups=dp_groups(masks), tiled=True)


def scatter_end(values, got, masks):
    count = len(masks) + 1
    if count == 2:
        return add(take(values, own_share(masks), values.shape[1] // 2, 1), got).astype(BF)
    total = got[0].astype(F32)
    for k in range(1, count):
        total = total + got[k].astype(F32)
    return total.astype(BF)


def gather_start(values, masks):
    count = len(masks) + 1
    if count == 2:
        return flip(values, "dp", masks[0])
    parts = jnp.broadcast_to(values[None], (count, *values.shape))
    return lax.all_to_all(parts, "dp", 0, 0, axis_index_groups=dp_groups(masks), tiled=True)


def gather_end(values, got, masks):
    if len(masks) == 1:
        own = own_share(masks)
        pieces = [jnp.where(own == 1, got, values), jnp.where(own == 1, values, got)]
        return jnp.concatenate(pieces, axis=1)
    return got.swapaxes(0, 1).reshape(values.shape[0], -1, values.shape[2])


def scatter_rest(values, stages):
    for masks in stages:
        values = scatter_end(values, scatter_start(values, masks), masks)
    return values


def gather_rest(values, stages):
    for masks in reversed(stages):
        values = gather_end(values, gather_start(values, masks), masks)
    return values


def body(
    tokens,
    norm1_gain,
    norm1_bias,
    qkv_weight,
    qv_bias,
    pair_bias,
    out_weight,
    out_bias,
    norm2_gain,
    norm2_bias,
    up_weight,
    up_bias,
    down_weight,
    down_bias,
    lengths,
    cotangent,
):
    me = lax.axis_index("chan")
    place = lax.axis_index("dp") % 4
    half = me % 2
    rows = tokens.shape[0] // CHAN
    width = D // CHAN
    length = lax.dynamic_index_in_dim(lengths, me // 2, 0, keepdims=False)
    info = jnp.stack([jnp.clip(length - half * rows, 0, rows), half, me]).astype(jnp.int32)
    along, across, *others = dp_stages()

    mixing = jnp.concatenate([jnp.swapaxes(qkv_weight, 1, 2).reshape(-1, D), out_weight], axis=0)
    mix_q0 = flip(take(mixing, place, D // 4), "chan", 2)
    mix_near = flip(mixing, "chan", 1)
    feeding = jnp.concatenate([up_weight, down_weight], axis=0)
    feed_near = flip(feeding, "chan", 1)
    token_pieces = row_pieces(tokens.T, rows)
    mix_q0, token_pieces = sync(mix_q0, token_pieces)
    x_t = to_rows(token_pieces)
    mix_q1 = flip(mix_q0, "dp", 1)
    mix_q2 = flip(mix_q0, "dp", 2)
    small = jnp.stack(
        [norm1_gain, norm1_bias, qv_bias[0], qv_bias[1], out_bias, norm2_gain, norm2_bias, down_bias]
    )
    small = jnp.concatenate([small, up_bias.reshape(CHAN, width)], axis=0)
    small = jnp.pad(small, ((0, 4), (0, 0)))
    small = jnp.stack([small] + [flip(small, "chan", r) for r in range(1, CHAN)])
    mix_q1, mix_q2, feeding = sync(mix_q1, mix_q2, feeding)
    mix_q3 = flip(mix_q2, "dp", 1)
    vec, up_shift, tok = vectors(info, small)
    mix_q3, x_t, feeding, tok = sync(mix_q3, x_t, feeding, tok)
    mix_far = jnp.concatenate(pick([mix_q0, mix_q1, mix_q2, mix_q3], place), axis=0)
    mixing = [mixing, mix_near, mix_far, flip(mix_far, "chan", 1)]
    feed_q0 = flip(take(feeding, place, D // 2), "chan", 2)

    def message(values, totals):
        edge = lax.dynamic_slice_in_dim(values, (1 - half) * (rows - WIN), WIN, 0)
        high = totals.astype(BF)
        low = (totals - high.astype(F32)).astype(BF)
        rest = jnp.zeros((14, values.shape[1]), BF)
        return flip(jnp.concatenate([edge, high, low, rest], axis=0), "chan", 1)

    normed_one, gate, vals, stacked, totals, qkv_t, tok = project(
        info, x_t, vec, mixing, tokens=[tok]
    )
    cot_pieces = row_pieces(cotangent.T, rows)
    feed_q0, totals, cot_pieces, tok = sync(feed_q0, totals, cot_pieces, tok)
    halo = message(stacked, totals)
    feed_q1 = flip(feed_q0, "dp", 1)
    feed_q2 = flip(feed_q0, "dp", 2)
    cot_t = to_rows(cot_pieces)
    terms, ratio, inverse, mixed, residual, normed_two, out_w, tok = mix(
        info, pair_bias, stacked, halo, totals, gate, x_t, vec, mixing, tokens=[tok]
    )
    feed_q1, feed_q2, cot_t, tok = sync(feed_q1, feed_q2, cot_t, tok)
    feed_q3 = flip(feed_q2, "dp", 1)

    total, into, ups_1, grad_1, cot, tok = feed(
        info, normed_two, cot_t, up_shift[1:2], feed_near, tokens=[tok]
    )
    got_1 = flip(grad_1, "chan", 1)
    feed_q3, tok = sync(feed_q3, tok)
    feed_far = jnp.concatenate(pick([feed_q0, feed_q1, feed_q2, feed_q3], place), axis=0)
    feed_both = flip(feed_far, "chan", 1)
    total, into, ups_3, grad_3, tok = feed(
        info, normed_two, cot, up_shift[3:4], feed_both, (total, into), tokens=[tok]
    )
    got_3 = flip(grad_3, "chan", 1)
    total, into, ups_0, near, tok = feed(
        info, normed_two, cot, up_shift[0:1], feeding, (total, into), extra=got_1, tokens=[tok]
    )
    near = near.reshape(2, D, D)
    near_x = scatter_start(near, along)
    layer_t, into, ups_2, far, tok = feed(
        info,
        normed_two,
        cot,
        up_shift[2:3],
        feed_far,
        (total, into),
        (residual, vec),
        got_3,
        tokens=[tok],
    )
    far = far.reshape(2, D, D)
    res_grad, branch, q_grad, grads, grad_totals, cols_two, tok = branch_back(
        info, into, residual, cot, vec, out_w, ratio, inverse, gate, tokens=[tok]
    )
    near_x, tok = sync(near_x, tok)
    near = scatter_end(near, near_x, along)
    near_z = scatter_start(near, across)
    far_x = scatter_start(far, along)
    grad_halo = message(grads, grad_totals)
    k_grad, v_grad, pair_grad, tok = window_back(
        info, terms, grads, grad_halo, grad_totals, stacked, halo, vals, tokens=[tok]
    )
    ups = jnp.concatenate([ups_0, ups_1, ups_2, ups_3], axis=0)
    m_near, m_far, send, tok = mixing_grads(
        info, q_grad, k_grad, v_grad, mixed, normed_one, branch, pair_grad, cols_two, ups, tokens=[tok]
    )
    got = flip(send, "chan", 1)
    input_t, cols_one, tok = input_back(
        q_grad, k_grad, v_grad, qkv_t, x_t, vec, res_grad, tokens=[tok]
    )

    cols_one = cols_one[:2] + flip(cols_one[:2], "chan", 1)
    got, tok = sync(got, tok)

    def with_norm(values, there):
        lines = jnp.where(there, cols_one, 0.0).reshape(6, WIN)
        return values + jnp.pad(lines, ((D, WIN - 6), (2 * WIN, 0)))

    m_far = flip(with_norm(add(m_far, got[1]), me == 2).astype(BF), "chan", 2)
    m_near = with_norm(add(m_near, got[0]), me == 0)
    near_z, far_x, tok = sync(near_z, far_x, tok)
    near = scatter_end(near, near_z, across)
    far = scatter_end(far, far_x, along)
    far_z = scatter_start(far, across)
    layer_parts = pick(split_rows(layer_t, CHAN), me)
    input_parts = pick(split_rows(input_t, CHAN), me)
    layer_near = exchange_near(layer_parts)
    input_near = exchange_near(input_parts)
    far_z, m_near, tok = sync(far_z, m_near, tok)
    f_near = scatter_rest(near, others)
    f_far = scatter_rest(scatter_end(far, far_z, across), others)
    f_y = flip(f_far, "chan", 2)
    m_far, f_y, tok = sync(m_far, f_y, tok)
    f = gather_rest(add(f_near, f_y).astype(BF), others)
    f_z = [flip(f, "dp", k) for k in across]
    m = add(m_near, m_far).astype(BF)[None]
    m_x = scatter_start(m, along)
    m_x, f, layer_near, tok = sync(m_x, f, layer_near, tok)
    m = scatter_end(m, m_x, along)
    layer_far = exchange_far(layer_parts, layer_near)
    *f_z, m, tok = sync(*f_z, m, tok)
    m_z = scatter_start(m, across)
    f = jnp.concatenate(pick([f, *f_z], own_share(across)), axis=1)
    f_x = gather_start(f, along)
    m_z, f_x, layer_far, input_near, f = sync(m_z, f_x, layer_far, input_near, f)
    m = scatter_rest(scatter_end(m, m_z, across), others)
    m = gather_rest(m, others)
    m_z = gather_start(m, across)
    f = gather_end(f, f_x, along).astype(F32)
    layer_out = columns(layer_parts, layer_near, layer_far, me)
    input_far = exchange_far(input_parts, input_near)
    m_z, f, layer_out, input_far = sync(m_z, f, layer_out, input_far)
    m = gather_end(m, m_z, across)
    m_x = gather_start(m, along)
    input_grad = columns(input_parts, input_near, input_far, me)
    m_x, input_grad, f = sync(m_x, input_grad, f)
    m = gather_end(m, m_x, along)[0]
    block = m[D:]
    other = flip(block, "chan", 2)
    qkv_out = jnp.swapaxes(m[: 3 * width].reshape(3, width, D).astype(F32), 1, 2)
    out_out = m[3 * width : D].astype(F32)
    other, qkv_out, out_out, tok = sync(other, qkv_out, out_out, tok)
    pair = jnp.stack([block, other])
    beside = flip(pair, "chan", 1)
    table = jnp.stack(pick([pair[0], beside[0], pair[1], beside[1]], me))
    pair_out, small_out, ups_out, tok = unpack_pairs(info, table, pair_bias, tokens=[tok])
    vector = [small_out[k, :width] for k in range(8)]
    return (
        layer_out,
        input_grad,
        vector[0],
        vector[1],
        qkv_out,
        jnp.stack(vector[6:8]),
        pair_out,
        out_out,
        vector[4],
        vector[2],
        vector[3],
        f[0],
        ups_out.reshape(-1),
        f[1],
        vector[5],
    )


def solution(mesh):
    in_specs = (
        P("dp", "chan"),
        P("chan"),
        P("chan"),
        P(None, None, "chan"),
        P(None, "chan"),
        P(),
        P("chan", None),
        P("chan"),
        P("chan"),
        P("chan"),
        P(None, "chan"),
        P("chan"),
        P("chan", None),
        P("chan"),
        P("dp"),
        P("dp", "chan"),
    )
    out_specs = (
        P("dp", "chan"),
        P("dp", "chan"),
        P("chan"),
        P("chan"),
        P(None, None, "chan"),
        P(None, "chan"),
        P(),
        P("chan", None),
        P("chan"),
        P("chan"),
        P("chan"),
        P(None, "chan"),
        P("chan"),
        P("chan", None),
        P("chan"),
    )
    return jax.shard_map(body, mesh=mesh, in_specs=in_specs, out_specs=out_specs, check_vma=False)
```

```python
import functools

import jax
import jax.numpy as jnp
from jax import lax
from jax.experimental import pallas as pl
from jax.experimental.pallas import tpu as pltpu
from jax.sharding import PartitionSpec as P

D = 768
PAIR = 1024
WIN = 256
LEN = 2048
CHAN = 4
EPSILON = 1e-05
BF = jnp.bfloat16
F32 = jnp.float32
SMEM = pltpu.SMEM
MIB = 1024 * 1024
RB = 512
INPUT_COST = 72
WINDOW_COST = 1000


def flip(values, axis, mask):
    size = lax.axis_size(axis)
    return lax.ppermute(values, axis, [(i, i ^ mask) for i in range(size)])


def dot_f32(left, right, dims):
    return lax.dot_general(left, right, (dims, ((), ())), preferred_element_type=F32)


def mm(left, right):
    return dot_f32(left, right, ((1,), (0,)))


def mm_t(left, right):
    return dot_f32(left, right, ((1,), (1,)))


def t_mm(left, right):
    return dot_f32(left, right, ((0,), (0,)))


def pick(pieces, index):
    low, high = index % 2 == 1, index // 2 == 1
    a, b, c, d = pieces
    a, b = jnp.where(low, b, a), jnp.where(low, a, b)
    c, d = jnp.where(low, d, c), jnp.where(low, c, d)
    a, c = jnp.where(high, c, a), jnp.where(high, a, c)
    b, d = jnp.where(high, d, b), jnp.where(high, b, d)
    return [a, b, c, d]


def call(
    kernel, steps, views, out_views, out_shape, scratch=(), flops=0, heavy=0, mem=18, tokens=()
):
    vm = pl.BlockSpec(memory_space=pltpu.VMEM)
    specs = [pl.BlockSpec(memory_space=SMEM) if v is None else vm for v in views]
    every = list(views) + list(out_views)
    first_out, count = len(views) + len(tokens), len(out_views)

    def unrolled(*refs):
        used = refs[: len(views)] + refs[first_out : first_out + count]
        refs[first_out + count][...] = jnp.zeros((8, 128), F32)
        for step in range(steps):
            parts = [r if v is None else v(r, step) for v, r in zip(every, used)]
            kernel(step, steps, *parts, *refs[first_out + count + 1 :])

    run = pl.pallas_call(
        unrolled,
        in_specs=specs + [vm] * len(tokens),
        out_specs=[vm] * (count + 1),
        out_shape=list(out_shape) + [shape_of((8, 128), F32)],
        scratch_shapes=list(scratch),
        compiler_params=pltpu.CompilerParams(vmem_limit_bytes=mem * MIB),
        cost_estimate=pl.CostEstimate(
            flops=flops, bytes_accessed=flops // 300, transcendentals=heavy
        ),
    )
    return lambda *operands: run(*operands, *tokens)


def whole(ref, step):
    return ref


def rows_of(size):
    return lambda ref, step: ref.at[step * size : (step + 1) * size]


def cols_of(size):
    return lambda ref, step: ref.at[:, step * size : (step + 1) * size]


def shape_of(shape, dtype):
    return jax.ShapeDtypeStruct(shape, dtype)


def live_block(info_ref, step, size):
    ids = lax.broadcasted_iota(jnp.int32, (size, 1), 0) + step * size
    return (ids < info_ref[0]).astype(F32)


def normalize(values):
    row_mean = jnp.mean(values, axis=1, keepdims=True)
    spread = jnp.mean(values * values, axis=1, keepdims=True) - row_mean * row_mean
    inv_scale = lax.rsqrt(spread + EPSILON)
    return (values - row_mean) * inv_scale, inv_scale


def norm_back(grad_out, centred, inv_scale, gain_vals):
    scaled = grad_out * gain_vals
    plain = jnp.mean(scaled, axis=1, keepdims=True)
    crossed = jnp.mean(scaled * centred, axis=1, keepdims=True)
    return inv_scale * (scaled - plain - centred * crossed)


def col_sum(values):
    return jnp.sum(values, axis=0, keepdims=True)


def gelu_pair(u):
    c0, c1 = 0.7978845608, 0.044715
    sq = u * u
    half = 0.5 + 0.5 * jnp.tanh(u * (c0 + c0 * c1 * sq))
    slope = half * (1.0 + (1.0 - half) * (u * (2.0 * c0 + 6.0 * c0 * c1 * sq)))
    return u * half, slope


def add_into(ref, step, values):
    ref[...] = values if step == 0 else ref[...] + values


def vector_kernel(step, count, info, small_ref, vec_ref, up_ref):
    width, me = D // CHAN, info[2]
    for k in range(CHAN):
        cols = slice(k * width, (k + 1) * width)
        own = small_ref[me ^ k].astype(F32)
        pair = small_ref[k - k % 2 + (k % 2 + info[1]) % 2].astype(F32)
        vec_ref[0:2, cols] = own[0:2]
        vec_ref[2:4, cols] = pair[2:4]
        vec_ref[4:8, cols] = own[4:8]
        ups = small_ref[k].astype(F32)
        for t in range(CHAN):
            up_ref[k : k + 1, t * width : (t + 1) * width] = ups[8 + t : 9 + t]


def vectors(info, small, tokens=()):
    return call(
        vector_kernel,
        1,
        [None, whole],
        [whole, whole],
        [shape_of((8, D), F32), shape_of((CHAN, D), F32)],
        mem=16,
        tokens=tokens,
    )(info, small)


def chan_row(info, r):
    return (r - r % 2) + (r % 2 + info[1]) % 2


def project_kernel(
    step, count, info, x_ref, vec, w_0, w_1, w_2, w_3, n_ref, gate_ref, v_ref, s_ref, tot_ref, w_ref
):
    width = D // CHAN
    if step == 0:
        for r, ref in enumerate((w_0, w_1, w_2, w_3)):
            row = pl.multiple_of(chan_row(info, r) * width, width)
            for k in range(3):
                w_ref[k, pl.ds(row, width)] = ref[k * width : (k + 1) * width]
    live = live_block(info, step, RB)
    centred, _ = normalize(x_ref[...].astype(F32).T)
    normed = (centred * vec[0:1] + vec[1:2]).astype(BF)
    n_ref[...] = normed
    gate_ref[...] = jax.nn.sigmoid(mm_t(normed, w_ref[0]) + vec[2:3]).astype(BF)
    keys = live * jnp.exp(mm_t(normed, w_ref[1]))
    vals = mm_t(normed, w_ref[2]) + vec[3:4]
    carried = keys * vals
    v_ref[...] = vals.astype(BF)
    s_ref[:, :D] = carried.astype(BF)
    s_ref[:, D:] = keys.astype(BF)
    add_into(tot_ref, step, jnp.concatenate([col_sum(carried), col_sum(keys)], axis=1))


def project(info, x_t, vec, weights, tokens=()):
    rows = x_t.shape[1]
    return call(
        project_kernel,
        rows // RB,
        [None, cols_of(RB)] + [whole] * 5,
        [rows_of(RB)] * 4 + [whole] * 2,
        [shape_of((rows, D), BF)] * 3
        + [shape_of((rows, 2 * D), BF), shape_of((1, 2 * D), F32), shape_of((3, D, D), BF)],
        flops=6 * rows * D * D,
        heavy=rows * D * 2,
        tokens=tokens,
    )(info, x_t, vec, *weights)


def side_masks():
    row_ids = lax.broadcasted_iota(jnp.int32, (WIN, WIN), 0)
    col_ids = lax.broadcasted_iota(jnp.int32, (WIN, WIN), 1)
    return col_ids > row_ids, col_ids < row_ids


def neighbours(info, step, count, ref, halo_ref):
    half = info[1]
    if step == 0:
        left = jnp.where(half == 1, halo_ref[:WIN], jnp.zeros_like(halo_ref[:WIN]))
    else:
        left = ref[(step - 1) * WIN : step * WIN]
    if step == count - 1:
        right = jnp.where(half == 0, halo_ref[:WIN], jnp.zeros_like(halo_ref[:WIN]))
    else:
        right = ref[(step + 1) * WIN : (step + 2) * WIN]
    return left, ref[step * WIN : (step + 1) * WIN], right


def pair_total(tot_ref, far_ref):
    far = far_ref[WIN : WIN + 16].astype(F32)
    return tot_ref[...] + (far[0:1] + far[1:2])


def pair_cols(ref, step, count, side):
    col = (step + side) % count
    return ref[step * WIN : (step + 1) * WIN, col * WIN : (col + 1) * WIN]


def mix_kernel(
    step, count, info, pair_ref, s_ref, far_ref, tot_ref, gate_ref, x_ref, vec,
    w_0, w_1, w_2, w_3, term_ref, ratio_ref, inv_ref, mixed_ref, res_ref, n_ref, w_ref,
):
    width = D // CHAN
    if step == 0:
        for r, ref in enumerate((w_0, w_1, w_2, w_3)):
            row = pl.multiple_of(chan_row(info, r) * width, width)
            w_ref[pl.ds(row, width)] = ref[3 * width :]
    live = live_block(info, step, WIN)
    before, after_own = side_masks()
    left, own, right = neighbours(info, step, count, s_ref, far_ref)
    grow = [jnp.exp(pair_cols(pair_ref, step, count, k).astype(F32)) - 1.0 for k in (-1, 0, 1)]
    term_l = jnp.where(before, grow[0], 0.0).astype(BF)
    term_o = grow[1].astype(BF)
    term_r = jnp.where(after_own, grow[2], 0.0).astype(BF)
    term_ref[:, :WIN] = term_l
    term_ref[:, WIN : 2 * WIN] = term_o
    term_ref[:, 2 * WIN :] = term_r
    merged = mm(term_l, left) + mm(term_o, own) + mm(term_r, right)
    merged = merged + pair_total(tot_ref, far_ref)
    inverse = 1.0 / merged[:, D:]
    ratio = merged[:, :D] * inverse
    mixed = (live * gate_ref[...].astype(F32) * ratio).astype(BF)
    ratio_ref[...] = ratio.astype(BF)
    inv_ref[...] = inverse
    mixed_ref[...] = mixed
    residual = x_ref[...].astype(F32).T + live * (mm(mixed, w_ref[...]) + vec[4:5])
    res_ref[...] = residual
    centred, _ = normalize(residual)
    n_ref[...] = (centred * vec[5:6] + vec[6:7]).astype(BF)


def mix(info, pair_bias, stacked, message, totals, gate, x_t, vec, weights, tokens=()):
    rows = x_t.shape[1]
    return call(
        mix_kernel,
        rows // WIN,
        [None, whole, whole, whole, whole, rows_of(WIN), cols_of(WIN)] + [whole] * 5,
        [rows_of(WIN)] * 6 + [whole],
        [
            shape_of((rows, 3 * WIN), BF),
            shape_of((rows, D), BF),
            shape_of((rows, D), F32),
            shape_of((rows, D), BF),
            shape_of((rows, D), F32),
            shape_of((rows, D), BF),
            shape_of((D, D), BF),
        ],
        flops=2 * rows * D * (6 * WIN + D),
        heavy=rows * D * 2,
        tokens=tokens,
    )(info, pair_bias, stacked, message, totals, gate, x_t, vec, *weights)


def feed_kernel(first, final, extra, step, count, info, n_ref, cot_ref, shift_ref, w_ref, *rest):
    rest = list(rest)
    state = [rest.pop(0), rest.pop(0)] if not first else None
    final_refs = [rest.pop(0), rest.pop(0)] if final else None
    extra_ref = rest.pop(0) if extra else None
    sum_ref, into_ref, ups_ref = rest.pop(0), rest.pop(0), rest.pop(0)
    weight_grad = rest.pop(0)
    if first:
        rest.pop(0)[...] = (cot := cot_ref[...].T)
    else:
        cot = cot_ref[...]
    grad_sc, act_sc, hidden_sc = rest
    live = lax.broadcasted_iota(jnp.int32, (n_ref.shape[0], 1), 0) < info[0]
    grad_sc[...] = jnp.where(live, cot, jnp.zeros_like(cot))
    grad = grad_sc[...]
    for f in range(0, D, WIN):
        cols, low = slice(f, f + WIN), slice(D + f, D + f + WIN)
        hidden = mm(n_ref[...], w_ref[:D, cols]) + shift_ref[:, cols]
        act, slope = gelu_pair(hidden)
        act = act.astype(BF)
        hidden_grad = (mm_t(grad, w_ref[low]) * slope).astype(BF)
        act_sc[:, cols] = act
        hidden_sc[:, cols] = hidden_grad
        ups_ref[:, cols] = col_sum(hidden_grad.astype(F32))
        of_up = t_mm(n_ref[...], hidden_grad)
        of_down = t_mm(act, grad)
        if extra:
            of_up = of_up + extra_ref[:D, cols].astype(F32)
            of_down = of_down + extra_ref[low].astype(F32)
        weight_grad[:D, cols] = of_up.astype(BF)
        weight_grad[low] = of_down.astype(BF)
    total = mm(act_sc[...], w_ref[D:])
    into = mm_t(hidden_sc[...], w_ref[:D])
    if not first:
        total, into = total + state[0][...], into + state[1][...]
    into_ref[...] = into
    if final:
        res_ref, vec = final_refs
        out = res_ref[...] + jnp.where(live, total + vec[7:8], 0.0)
        sum_ref[...] = out.T.astype(BF)
    else:
        sum_ref[...] = total


def feed(info, normed, cot, shift, weights, state=None, final=None, extra=None, tokens=()):
    rows = normed.shape[0]
    operands = [info, normed, cot, shift, weights]
    operands += list(state or ()) + list(final or ()) + ([] if extra is None else [extra])
    out_shape = [
        shape_of((rows, D), F32) if final is None else shape_of((D, rows), BF),
        shape_of((rows, D), F32),
        shape_of((1, D), F32),
    ]
    out_shape.append(shape_of((2 * D, D), BF))
    if state is None:
        out_shape.append(shape_of((rows, D), BF))
    flags = (state is None, final is not None, extra is not None)
    return call(
        functools.partial(feed_kernel, *flags),
        1,
        [None] + [whole] * (len(operands) - 1),
        [whole] * len(out_shape),
        out_shape,
        scratch=[pltpu.VMEM((rows, D), BF)] * 3,
        flops=12 * rows * D * D,
        heavy=rows * D,
        mem=18,
        tokens=tokens,
    )(*operands)


def branch_kernel(
    step, count, info, into_ref, res_ref, cot_ref, vec, w_ref, ratio_ref, inv_ref, gate_ref,
    resg_ref, branch_ref, qg_ref, g_ref, tot_ref, cols_ref,
):
    live = live_block(info, step, RB)
    upstream = into_ref[...]
    centred, inv_scale = normalize(res_ref[...])
    cot = cot_ref[...].astype(F32)
    res_grad = cot + norm_back(upstream, centred, inv_scale, vec[5:6])
    resg_ref[...] = res_grad
    branch = (live * res_grad).astype(BF)
    branch_ref[...] = branch
    mixed_grad = live * mm_t(branch, w_ref[...])
    gate, ratio = gate_ref[...].astype(F32), ratio_ref[...].astype(F32)
    pulled = mixed_grad * gate
    qg_ref[...] = (pulled * ratio * (1.0 - gate)).astype(BF)
    num = pulled * inv_ref[...]
    den = -num * ratio
    g_ref[:, :D] = num.astype(BF)
    g_ref[:, D:] = den.astype(BF)
    add_into(tot_ref, step, jnp.concatenate([col_sum(num), col_sum(den)], axis=1))
    cols = [
        col_sum(upstream * centred),
        col_sum(upstream),
        col_sum(branch.astype(F32)),
        col_sum(live * cot),
        jnp.zeros((4, D), F32),
    ]
    add_into(cols_ref, step, jnp.concatenate(cols, axis=0))


def branch_back(info, into, residual, cot, vec, out_w, ratio, inverse, gate, tokens=()):
    rows = cot.shape[0]
    wide = rows_of(RB)
    return call(
        branch_kernel,
        rows // RB,
        [None, wide, wide, wide, whole, whole, wide, wide, wide],
        [wide, wide, wide, wide, whole, whole],
        [
            shape_of((rows, D), F32),
            shape_of((rows, D), BF),
            shape_of((rows, D), BF),
            shape_of((rows, 2 * D), BF),
            shape_of((1, 2 * D), F32),
            shape_of((8, D), F32),
        ],
        flops=2 * rows * D * D,
        tokens=tokens,
    )(info, into, residual, cot, vec, out_w, ratio, inverse, gate)


def window_kernel(
    step, count, info, t_ref, g_ref, gfar_ref, tot_ref, s_ref, sfar_ref, v_ref,
    kg_ref, vg_ref, pair_ref,
):
    before, after_own = side_masks()
    left, own, right = neighbours(info, step, count, g_ref, gfar_ref)

    def term(block, part):
        block = block % count
        return t_ref[block * WIN : (block + 1) * WIN, part * WIN : (part + 1) * WIN]

    pulled = t_mm(term(step - 1, 2), left) + t_mm(term(step, 1), own)
    pulled = pulled + t_mm(term(step + 1, 0), right) + pair_total(tot_ref, gfar_ref)
    carried_grad, exp_grad = pulled[:, :D], pulled[:, D:]
    left, data, right = neighbours(info, step, count, s_ref, sfar_ref)
    keys = data[:, D:].astype(F32)
    vg_ref[...] = (carried_grad * keys).astype(BF)
    kg_ref[...] = ((exp_grad + carried_grad * v_ref[...].astype(F32)) * keys).astype(BF)
    r = info[2] ^ step
    slot = (r % 2) * 2 + r // 2
    pair_ref[slot, :, :WIN] = mm_t(own, data).astype(BF)
    side = jnp.where(before, mm_t(own, left), 0.0) + jnp.where(after_own, mm_t(own, right), 0.0)
    pair_ref[slot, :, WIN:] = side.astype(BF)


def window_back(info, terms, grads, grad_message, grad_totals, stacked, message, vals, tokens=()):
    rows = vals.shape[0]
    return call(
        window_kernel,
        rows // WIN,
        [None, whole, whole, whole, whole, whole, whole, rows_of(WIN)],
        [rows_of(WIN), rows_of(WIN), whole],
        [shape_of((rows, D), BF)] * 2 + [shape_of((rows // WIN, WIN, 2 * WIN), BF)],
        flops=WINDOW_COST,
        tokens=tokens,
    )(info, terms, grads, grad_message, grad_totals, stacked, message, vals)


def mixing_grads_kernel(
    step, count, info, q_ref, k_ref, v_ref, m_ref, n_ref, b_ref, two_ref, ups_ref,
    keep_near, keep_far, send_ref, pack_ref,
):
    half, me = info[1], info[2]
    keep_refs = (keep_near, keep_far)
    width = D // CHAN
    products = [t_mm(ref[...], n_ref[...]).astype(BF) for ref in (q_ref, k_ref, v_ref)]
    products.append(t_mm(m_ref[...], b_ref[...]).astype(BF))

    def store(core, far, rows, values):
        @pl.when(half == core)
        def _():
            keep_refs[far][rows] = values

        @pl.when(half != core)
        def _():
            send_ref[far, rows] = values

    for k, product in enumerate(products):
        for far in range(2):
            for core in range(2):
                b = 2 * far + core
                rows = slice(k * width, (k + 1) * width)
                store(core, far, rows, product[b * width : (b + 1) * width])

    sums = [col_sum(q_ref[...].astype(F32)), col_sum(v_ref[...].astype(F32))]
    turned = [jnp.concatenate([t[:, D // 2 :], t[:, : D // 2]], axis=1) for t in sums]
    pack_ref[0:2] = jnp.zeros((2, D), F32)
    pack_ref[2:6] = two_ref[0:4]
    for k in range(2):
        pack_ref[6 + k : 7 + k] = jnp.where(me // 2 == 1, turned[k], sums[k])
    for r in range(CHAN):
        pack_ref[pl.ds(8 + (me ^ r), 1)] = ups_ref[r : r + 1]
    pack_ref[12:16] = jnp.zeros((4, D), F32)


def mixing_grads(info, q_grad, k_grad, v_grad, mixed, normed, branch, two, ups, tokens=()):
    rows = normed.shape[0]
    return call(
        mixing_grads_kernel,
        1,
        [None] + [whole] * 8,
        [whole] * 4,
        [shape_of((D, D), BF)] * 2 + [shape_of((2, D, D), BF), shape_of((16, D), F32)],
        flops=8 * rows * D * D,
        mem=18,
        tokens=tokens,
    )(info, q_grad, k_grad, v_grad, mixed, normed, branch, two, ups)


def input_kernel(
    step, count, q_ref, k_ref, v_ref, w_ref, x_ref, vec, resg_ref, pack_ref, out_ref, cols_ref
):
    upstream = mm(q_ref[...], w_ref[0]) + mm(k_ref[...], w_ref[1]) + mm(v_ref[...], w_ref[2])
    centred, inv_scale = normalize(x_ref[...].astype(F32).T)
    grad = resg_ref[...] + norm_back(upstream, centred, inv_scale, vec[0:1])
    out_ref[...] = grad.T.astype(BF)
    if step == 0:
        cols_ref[...] = pack_ref[...]
    cols_ref[0:1] += col_sum(upstream * centred)
    cols_ref[1:2] += col_sum(upstream)


def input_back(q_grad, k_grad, v_grad, weights, x_t, vec, res_grad, pack, tokens=()):
    rows = res_grad.shape[0]
    wide = rows_of(RB)
    return call(
        input_kernel,
        rows // RB,
        [wide, wide, wide, whole, cols_of(RB), whole, wide, whole],
        [cols_of(RB), whole],
        [shape_of((D, rows), BF), shape_of((16, D), F32)],
        flops=INPUT_COST * rows * D * D,
        tokens=tokens,
    )(q_grad, k_grad, v_grad, weights, x_t, vec, res_grad, pack)


def sync(*arrays):
    return lax.optimization_barrier(arrays)


def row_pieces(values, rows):
    return values.reshape(-1, CHAN, rows).swapaxes(0, 1)


def to_rows(pieces):
    pieces = lax.all_to_all(pieces, "chan", 0, 0, tiled=True)
    return pieces.reshape(-1, pieces.shape[2])


def exchange_near(pieces):
    return flip(jnp.stack([pieces[1], pieces[3]]), "chan", 1)


def exchange_far(pieces, near):
    return flip(jnp.stack([pieces[2], near[1]]), "chan", 2)


def columns(pieces, near, far, me):
    return jnp.concatenate(pick([pieces[0], near[0], far[0], far[1]], me), axis=1).T


def split_rows(values, count):
    size = values.shape[0] // count
    return [values[k * size : (k + 1) * size] for k in range(count)]


def take(values, index, size, axis=0):
    return lax.dynamic_slice_in_dim(values, index * size, size, axis)


def unpack_kernel(step, count, info, packed_ref, pair_ref, out_ref, small_ref, ups_ref):
    before, after_own = side_masks()
    grow = [jnp.exp(pair_cols(pair_ref, step, count, k).astype(F32)) for k in (-1, 0, 1)]
    own = packed_ref[step, :WIN, :WIN].astype(F32)
    side = packed_ref[step, :WIN, WIN:].astype(F32)
    squares = [jnp.zeros((WIN, WIN), F32)] * count
    squares[step] = own * grow[1]
    squares[(step - 1) % count] = jnp.where(before, side * grow[0], 0.0)
    squares[(step + 1) % count] = jnp.where(after_own, side * grow[2], 0.0)
    for k in range(count):
        out_ref[:, k * WIN : (k + 1) * WIN] = squares[k]
    if step == count - 1:
        me, width = info[2], D // CHAN
        every = 0.0
        for b in range(CHAN):
            part = packed_ref[b, WIN : WIN + 32].astype(F32)
            every = every + jnp.concatenate([part[:16], part[16:, :WIN]], axis=1)
        mine = every[:8, :width]
        for k in range(1, CHAN):
            mine = jnp.where(me == k, every[:8, k * width : (k + 1) * width], mine)
        ups = every[8:9]
        for k in range(1, CHAN):
            ups = jnp.where(me == k, every[8 + k : 9 + k], ups)
        small_ref[:, :width] = mine
        small_ref[:, width:] = jnp.zeros((8, D - width), F32)
        ups_ref[...] = ups


def unpack_pairs(info, packed, pair_bias, tokens=()):
    size = pair_bias.shape[0]
    return call(
        unpack_kernel,
        size // WIN,
        [None, whole, whole],
        [rows_of(WIN), whole, whole],
        [shape_of((size, size), F32), shape_of((8, D), F32), shape_of((1, D), F32)],
        heavy=size * WIN * 3,
        tokens=tokens,
    )(info, packed, pair_bias)


def dp_stages():
    size = lax.axis_size("dp")
    stages, mask = [[1]], 2
    while mask < size:
        if mask * 2 < size:
            stages.append([mask, mask * 2, mask * 3])
            mask *= 4
        else:
            stages.append([mask])
            mask *= 2
    return stages


def add(first, second):
    return first.astype(F32) + second.astype(F32)


def dp_groups(masks):
    size = lax.axis_size("dp")
    low, count = masks[0], len(masks) + 1
    starts = [i for i in range(size) if (i // low) % count == 0]
    return [[i + low * k for k in range(count)] for i in starts]


def own_share(masks):
    return (lax.axis_index("dp") // masks[0]) % (len(masks) + 1)


def scatter_start(values, masks):
    count = len(masks) + 1
    n, rows, cols = values.shape[0], values.shape[1] // count, values.shape[2]
    if count == 2:
        return flip(take(values, 1 - own_share(masks), rows, 1), "dp", masks[0])
    parts = values.reshape(n, count, rows, cols).swapaxes(0, 1)
    return lax.all_to_all(parts, "dp", 0, 0, axis_index_groups=dp_groups(masks), tiled=True)


def scatter_end(values, got, masks):
    count = len(masks) + 1
    if count == 2:
        return add(take(values, own_share(masks), values.shape[1] // 2, 1), got).astype(BF)
    total = got[0].astype(F32)
    for k in range(1, count):
        total = total + got[k].astype(F32)
    return total.astype(BF)


def gather_start(values, masks):
    count = len(masks) + 1
    if count == 2:
        return flip(values, "dp", masks[0])
    parts = jnp.broadcast_to(values[None], (count, *values.shape))
    return lax.all_to_all(parts, "dp", 0, 0, axis_index_groups=dp_groups(masks), tiled=True)


def gather_end(values, got, masks):
    if len(masks) == 1:
        own = own_share(masks)
        pieces = [jnp.where(own == 1, got, values), jnp.where(own == 1, values, got)]
        return jnp.concatenate(pieces, axis=1)
    return got.swapaxes(0, 1).reshape(values.shape[0], -1, values.shape[2])


def scatter_all(values):
    parts = values.reshape(lax.axis_size("dp"), -1, values.shape[1])
    return lax.all_to_all(parts, "dp", 0, 0, tiled=True)


def sum_all(got):
    total = got[0].astype(F32)
    for k in range(1, got.shape[0]):
        total = total + got[k].astype(F32)
    return total.astype(BF)


def gather_all(values):
    parts = jnp.broadcast_to(values[None], (lax.axis_size("dp"), *values.shape))
    return lax.all_to_all(parts, "dp", 0, 0, tiled=True)


def scatter_rest(values, stages):
    for masks in stages:
        values = scatter_end(values, scatter_start(values, masks), masks)
    return values


def gather_rest(values, stages):
    for masks in reversed(stages):
        values = gather_end(values, gather_start(values, masks), masks)
    return values


def body(
    tokens,
    norm1_gain,
    norm1_bias,
    qkv_weight,
    qv_bias,
    pair_bias,
    out_weight,
    out_bias,
    norm2_gain,
    norm2_bias,
    up_weight,
    up_bias,
    down_weight,
    down_bias,
    lengths,
    cotangent,
):
    me = lax.axis_index("chan")
    place = lax.axis_index("dp") % 4
    half = me % 2
    rows = tokens.shape[0] // CHAN
    width = D // CHAN
    length = lax.dynamic_index_in_dim(lengths, me // 2, 0, keepdims=False)
    info = jnp.stack([jnp.clip(length - half * rows, 0, rows), half, me]).astype(jnp.int32)
    along, across, *others = dp_stages()

    mixing = jnp.concatenate([jnp.swapaxes(qkv_weight, 1, 2).reshape(-1, D), out_weight], axis=0)
    mix_q0 = flip(take(mixing, place, D // 4), "chan", 2)
    mix_near = flip(mixing, "chan", 1)
    feeding = jnp.concatenate([up_weight, down_weight], axis=0)
    feed_near = flip(feeding, "chan", 1)
    token_pieces = row_pieces(tokens.T, rows)
    mix_q0, token_pieces = sync(mix_q0, token_pieces)
    x_t = to_rows(token_pieces)
    mix_q1 = flip(mix_q0, "dp", 1)
    mix_q2 = flip(mix_q0, "dp", 2)
    small = jnp.stack(
        [norm1_gain, norm1_bias, qv_bias[0], qv_bias[1], out_bias, norm2_gain, norm2_bias, down_bias]
    )
    small = jnp.concatenate([small, up_bias.reshape(CHAN, width)], axis=0)
    small = jnp.pad(small, ((0, 4), (0, 0)))
    small = jnp.stack([small] + [flip(small, "chan", r) for r in range(1, CHAN)])
    mix_q1, mix_q2, feeding = sync(mix_q1, mix_q2, feeding)
    mix_q3 = flip(mix_q2, "dp", 1)
    vec, up_shift, tok = vectors(info, small)
    mix_q3, x_t, feeding, tok = sync(mix_q3, x_t, feeding, tok)
    mix_far = jnp.concatenate(pick([mix_q0, mix_q1, mix_q2, mix_q3], place), axis=0)
    mixing = [mixing, mix_near, mix_far, flip(mix_far, "chan", 1)]
    feed_q0 = flip(take(feeding, place, D // 2), "chan", 2)

    def message(values, totals):
        edge = lax.dynamic_slice_in_dim(values, (1 - half) * (rows - WIN), WIN, 0)
        high = totals.astype(BF)
        low = (totals - high.astype(F32)).astype(BF)
        rest = jnp.zeros((14, values.shape[1]), BF)
        return flip(jnp.concatenate([edge, high, low, rest], axis=0), "chan", 1)

    normed_one, gate, vals, stacked, totals, qkv_t, tok = project(
        info, x_t, vec, mixing, tokens=[tok]
    )
    cot_pieces = row_pieces(cotangent.T, rows)
    feed_q0, totals, cot_pieces, tok = sync(feed_q0, totals, cot_pieces, tok)
    halo = message(stacked, totals)
    feed_q1 = flip(feed_q0, "dp", 1)
    feed_q2 = flip(feed_q0, "dp", 2)
    cot_t = to_rows(cot_pieces)
    terms, ratio, inverse, mixed, residual, normed_two, out_w, tok = mix(
        info, pair_bias, stacked, halo, totals, gate, x_t, vec, mixing, tokens=[tok]
    )
    feed_q1, feed_q2, cot_t, tok = sync(feed_q1, feed_q2, cot_t, tok)
    feed_q3 = flip(feed_q2, "dp", 1)

    total, into, ups_1, grad_1, cot, tok = feed(
        info, normed_two, cot_t, up_shift[1:2], feed_near, tokens=[tok]
    )
    got_1 = flip(grad_1, "chan", 1)
    feed_q3, tok = sync(feed_q3, tok)
    feed_far = jnp.concatenate(pick([feed_q0, feed_q1, feed_q2, feed_q3], place), axis=0)
    feed_both = flip(feed_far, "chan", 1)
    total, into, ups_3, grad_3, tok = feed(
        info, normed_two, cot, up_shift[3:4], feed_both, (total, into), tokens=[tok]
    )
    got_3 = flip(grad_3, "chan", 1)
    total, into, ups_0, near, tok = feed(
        info, normed_two, cot, up_shift[0:1], feeding, (total, into), extra=got_1, tokens=[tok]
    )
    near = near.reshape(2, D, D)
    near_x = scatter_start(near, along)
    layer_t, into, ups_2, far, tok = feed(
        info,
        normed_two,
        cot,
        up_shift[2:3],
        feed_far,
        (total, into),
        (residual, vec),
        got_3,
        tokens=[tok],
    )
    far = far.reshape(2, D, D)
    far_u, far_d = far[:1], far[1:]
    far_uy = flip(far_u, "chan", 2)
    far_dx = scatter_start(far_d, along)
    res_grad, branch, q_grad, grads, grad_totals, cols_two, tok = branch_back(
        info, into, residual, cot, vec, out_w, ratio, inverse, gate, tokens=[tok]
    )
    grad_halo = message(grads, grad_totals)
    k_grad, v_grad, pair_grad, tok = window_back(
        info, terms, grads, grad_halo, grad_totals, stacked, halo, vals, tokens=[tok]
    )
    t_got = flip(pair_grad[2:], "chan", 1)
    ups = jnp.concatenate([ups_0, ups_1, ups_2, ups_3], axis=0)
    m_near, m_far, send, pack, tok = mixing_grads(
        info, q_grad, k_grad, v_grad, mixed, normed_one, branch, cols_two, ups, tokens=[tok]
    )
    got = flip(send, "chan", 1)
    near_x, far_uy, far_dx, t_got, tok = sync(near_x, far_uy, far_dx, t_got, tok)
    t = add(pair_grad[:2], t_got).astype(BF)
    t_near, t_far = t[:1], flip(t[1:], "chan", 2)
    near = scatter_end(near, near_x, along)
    far_dy = flip(scatter_end(far_d, far_dx, along), "chan", 2)
    far_ux = scatter_start(far_uy, along)
    input_t, pack, tok = input_back(
        q_grad, k_grad, v_grad, qkv_t, x_t, vec, res_grad, pack, tokens=[tok]
    )

    got, tok = sync(got, tok)
    m_far = add(m_far, got[1]).astype(BF)
    far_ux, far_dy, m_far, t_far, tok = sync(far_ux, far_dy, m_far, t_far, tok)
    m_far = flip(m_far, "chan", 2)
    f_u = add(near[:1], scatter_end(far_uy, far_ux, along)).astype(BF)
    f_d = add(near[1:], far_dy).astype(BF)
    f = jnp.concatenate([f_u, f_d], axis=0)
    f_z = scatter_start(f, across)
    m_near = add(m_near, got[0]).astype(BF)
    half_cols = 2 * WIN
    rest = jnp.pad(pack[:, half_cols:], ((0, 0), (0, half_cols - WIN)))
    pack = jnp.pad(jnp.concatenate([pack[:, :half_cols], rest], axis=0), ((0, 96), (0, 0)))
    t = jnp.concatenate([add(t_near, t_far)[0].astype(BF), pack.astype(BF)], axis=0)
    t_all = scatter_all(t)
    layer_parts = pick(split_rows(layer_t, CHAN), me)
    input_parts = pick(split_rows(input_t, CHAN), me)
    layer_near = exchange_near(layer_parts)
    input_near = exchange_near(input_parts)
    m_far, f_z, layer_near, tok = sync(m_far, f_z, layer_near, tok)
    m = add(m_near, m_far).astype(BF)[None]
    m_x = scatter_start(m, along)
    f = gather_rest(scatter_rest(scatter_end(f, f_z, across), others), others)
    f_z = [flip(f, "dp", k) for k in across]
    layer_far = exchange_far(layer_parts, layer_near)
    m_x, t_all, f, tok = sync(m_x, t_all, f, tok)
    m = scatter_end(m, m_x, along)
    m_z = scatter_start(m, across)
    t = sum_all(t_all)
    *f_z, layer_far, m = sync(*f_z, layer_far, m)
    f = jnp.concatenate(pick([f, *f_z], own_share(across)), axis=1)
    f_x = gather_start(f, along)
    m_z, t, input_near, f = sync(m_z, t, input_near, f)
    m = gather_rest(scatter_rest(scatter_end(m, m_z, across), others), others)
    m_z = gather_start(m, across)
    layer_out = columns(layer_parts, layer_near, layer_far, me)
    input_far = exchange_far(input_parts, input_near)
    f_x, m, t, layer_out = sync(f_x, m, t, layer_out)
    t_all = gather_all(t)
    f_u = gather_end(f[:1], f_x[:1], along)[0].astype(F32)
    f_d = gather_end(f[1:], f_x[1:], along)[0].astype(F32)
    m_z, f_u, f_d, tok = sync(m_z, f_u, f_d, tok)
    m = gather_end(m, m_z, across)
    m_x = gather_start(m, along)
    t_all, input_far, tok = sync(t_all, input_far, tok)
    t = t_all.reshape(-1, half_cols)
    t_y = flip(t, "chan", 2)
    input_grad = columns(input_parts, input_near, input_far, me)
    m_x, t_y, input_grad = sync(m_x, t_y, input_grad)
    pair = jnp.stack([t, t_y])
    beside = flip(pair, "chan", 1)
    m = gather_end(m, m_x, along)[0]
    qkv_out = jnp.swapaxes(m[: 3 * width].reshape(3, width, D).astype(F32), 1, 2)
    out_out = m[3 * width :].astype(F32)
    beside, qkv_out, out_out, tok = sync(beside, qkv_out, out_out, tok)
    table = jnp.stack(pick([pair[0], beside[0], pair[1], beside[1]], me))
    pair_out, small_out, ups_out, tok = unpack_pairs(info, table, pair_bias, tokens=[tok])
    vector = [small_out[k, :width] for k in range(8)]
    return (
        layer_out,
        input_grad,
        vector[0],
        vector[1],
        qkv_out,
        jnp.stack(vector[6:8]),
        pair_out,
        out_out,
        vector[4],
        vector[2],
        vector[3],
        f_u,
        ups_out.reshape(-1),
        f_d,
        vector[5],
    )


def solution(mesh):
    in_specs = (
        P("dp", "chan"),
        P("chan"),
        P("chan"),
        P(None, None, "chan"),
        P(None, "chan"),
        P(),
        P("chan", None),
        P("chan"),
        P("chan"),
        P("chan"),
        P(None, "chan"),
        P("chan"),
        P("chan", None),
        P("chan"),
        P("dp"),
        P("dp", "chan"),
    )
    out_specs = (
        P("dp", "chan"),
        P("dp", "chan"),
        P("chan"),
        P("chan"),
        P(None, None, "chan"),
        P(None, "chan"),
        P(),
        P("chan", None),
        P("chan"),
        P("chan"),
        P("chan"),
        P(None, "chan"),
        P("chan"),
        P("chan", None),
        P("chan"),
    )
    return jax.shard_map(body, mesh=mesh, in_specs=in_specs, out_specs=out_specs, check_vma=False)
```

```python
import functools

import jax
import jax.numpy as jnp
from jax import lax
from jax.experimental import pallas as pl
from jax.experimental.pallas import tpu as pltpu
from jax.sharding import PartitionSpec as P

D = 768
PAIR = 1024
WIN = 256
LEN = 2048
CHAN = 4
EPSILON = 1e-05
BF = jnp.bfloat16
F32 = jnp.float32
SMEM = pltpu.SMEM
MIB = 1024 * 1024
RB = 512
INPUT_COST = 72
CUT = 512
WINDOW_COST = 1000


def flip(values, axis, mask):
    size = lax.axis_size(axis)
    return lax.ppermute(values, axis, [(i, i ^ mask) for i in range(size)])


def dot_f32(left, right, dims):
    return lax.dot_general(left, right, (dims, ((), ())), preferred_element_type=F32)


def mm(left, right):
    return dot_f32(left, right, ((1,), (0,)))


def mm_t(left, right):
    return dot_f32(left, right, ((1,), (1,)))


def t_mm(left, right):
    return dot_f32(left, right, ((0,), (0,)))


def pick(pieces, index):
    low, high = index % 2 == 1, index // 2 == 1
    a, b, c, d = pieces
    a, b = jnp.where(low, b, a), jnp.where(low, a, b)
    c, d = jnp.where(low, d, c), jnp.where(low, c, d)
    a, c = jnp.where(high, c, a), jnp.where(high, a, c)
    b, d = jnp.where(high, d, b), jnp.where(high, b, d)
    return [a, b, c, d]


def call(
    kernel, steps, views, out_views, out_shape, scratch=(), flops=0, heavy=0, mem=18, tokens=()
):
    vm = pl.BlockSpec(memory_space=pltpu.VMEM)
    specs = [pl.BlockSpec(memory_space=SMEM) if v is None else vm for v in views]
    every = list(views) + list(out_views)
    first_out, count = len(views) + len(tokens), len(out_views)

    def unrolled(*refs):
        used = refs[: len(views)] + refs[first_out : first_out + count]
        refs[first_out + count][...] = jnp.zeros((8, 128), F32)
        for step in range(steps):
            parts = [r if v is None else v(r, step) for v, r in zip(every, used)]
            kernel(step, steps, *parts, *refs[first_out + count + 1 :])

    run = pl.pallas_call(
        unrolled,
        in_specs=specs + [vm] * len(tokens),
        out_specs=[vm] * (count + 1),
        out_shape=list(out_shape) + [shape_of((8, 128), F32)],
        scratch_shapes=list(scratch),
        compiler_params=pltpu.CompilerParams(vmem_limit_bytes=mem * MIB),
        cost_estimate=pl.CostEstimate(
            flops=flops, bytes_accessed=flops // 300, transcendentals=heavy
        ),
    )
    return lambda *operands: run(*operands, *tokens)


def whole(ref, step):
    return ref


def rows_of(size):
    return lambda ref, step: ref.at[step * size : (step + 1) * size]


def cols_of(size):
    return lambda ref, step: ref.at[:, step * size : (step + 1) * size]


def shape_of(shape, dtype):
    return jax.ShapeDtypeStruct(shape, dtype)


def live_block(info_ref, step, size):
    ids = lax.broadcasted_iota(jnp.int32, (size, 1), 0) + step * size
    return (ids < info_ref[0]).astype(F32)


def normalize(values):
    row_mean = jnp.mean(values, axis=1, keepdims=True)
    spread = jnp.mean(values * values, axis=1, keepdims=True) - row_mean * row_mean
    inv_scale = lax.rsqrt(spread + EPSILON)
    return (values - row_mean) * inv_scale, inv_scale


def norm_back(grad_out, centred, inv_scale, gain_vals):
    scaled = grad_out * gain_vals
    plain = jnp.mean(scaled, axis=1, keepdims=True)
    crossed = jnp.mean(scaled * centred, axis=1, keepdims=True)
    return inv_scale * (scaled - plain - centred * crossed)


def col_sum(values):
    return jnp.sum(values, axis=0, keepdims=True)


def gelu_pair(u):
    c0, c1 = 0.7978845608, 0.044715
    sq = u * u
    half = 0.5 + 0.5 * jnp.tanh(u * (c0 + c0 * c1 * sq))
    slope = half * (1.0 + (1.0 - half) * (u * (2.0 * c0 + 6.0 * c0 * c1 * sq)))
    return u * half, slope


def add_into(ref, step, values):
    ref[...] = values if step == 0 else ref[...] + values


def vector_kernel(step, count, info, small_ref, vec_ref, up_ref):
    width, me = D // CHAN, info[2]
    for k in range(CHAN):
        cols = slice(k * width, (k + 1) * width)
        own = small_ref[me ^ k].astype(F32)
        pair = small_ref[k - k % 2 + (k % 2 + info[1]) % 2].astype(F32)
        vec_ref[0:2, cols] = own[0:2]
        vec_ref[2:4, cols] = pair[2:4]
        vec_ref[4:8, cols] = own[4:8]
        ups = small_ref[k].astype(F32)
        for t in range(CHAN):
            up_ref[k : k + 1, t * width : (t + 1) * width] = ups[8 + t : 9 + t]


def vectors(info, small, tokens=()):
    return call(
        vector_kernel,
        1,
        [None, whole],
        [whole, whole],
        [shape_of((8, D), F32), shape_of((CHAN, D), F32)],
        mem=16,
        tokens=tokens,
    )(info, small)


def chan_row(info, r):
    return (r - r % 2) + (r % 2 + info[1]) % 2


def project_kernel(
    step, count, info, x_ref, vec, w_0, w_1, w_2, w_3, n_ref, gate_ref, v_ref, s_ref, tot_ref, w_ref
):
    width = D // CHAN
    if step == 0:
        for r, ref in enumerate((w_0, w_1, w_2, w_3)):
            row = pl.multiple_of(chan_row(info, r) * width, width)
            for k in range(3):
                w_ref[k, pl.ds(row, width)] = ref[k * width : (k + 1) * width]
    live = live_block(info, step, RB)
    centred, _ = normalize(x_ref[...].astype(F32).T)
    normed = (centred * vec[0:1] + vec[1:2]).astype(BF)
    n_ref[...] = normed
    gate_ref[...] = jax.nn.sigmoid(mm_t(normed, w_ref[0]) + vec[2:3]).astype(BF)
    keys = live * jnp.exp(mm_t(normed, w_ref[1]))
    vals = mm_t(normed, w_ref[2]) + vec[3:4]
    carried = keys * vals
    v_ref[...] = vals.astype(BF)
    s_ref[:, :D] = carried.astype(BF)
    s_ref[:, D:] = keys.astype(BF)
    add_into(tot_ref, step, jnp.concatenate([col_sum(carried), col_sum(keys)], axis=1))


def project(info, x_t, vec, weights, tokens=()):
    rows = x_t.shape[1]
    return call(
        project_kernel,
        rows // RB,
        [None, cols_of(RB)] + [whole] * 5,
        [rows_of(RB)] * 4 + [whole] * 2,
        [shape_of((rows, D), BF)] * 3
        + [shape_of((rows, 2 * D), BF), shape_of((1, 2 * D), F32), shape_of((3, D, D), BF)],
        flops=6 * rows * D * D,
        heavy=rows * D * 2,
        tokens=tokens,
    )(info, x_t, vec, *weights)


def side_masks():
    row_ids = lax.broadcasted_iota(jnp.int32, (WIN, WIN), 0)
    col_ids = lax.broadcasted_iota(jnp.int32, (WIN, WIN), 1)
    return col_ids > row_ids, col_ids < row_ids


def neighbours(info, step, count, ref, halo_ref):
    half = info[1]
    if step == 0:
        left = jnp.where(half == 1, halo_ref[:WIN], jnp.zeros_like(halo_ref[:WIN]))
    else:
        left = ref[(step - 1) * WIN : step * WIN]
    if step == count - 1:
        right = jnp.where(half == 0, halo_ref[:WIN], jnp.zeros_like(halo_ref[:WIN]))
    else:
        right = ref[(step + 1) * WIN : (step + 2) * WIN]
    return left, ref[step * WIN : (step + 1) * WIN], right


def pair_total(tot_ref, far_ref):
    far = far_ref[WIN : WIN + 16].astype(F32)
    return tot_ref[...] + (far[0:1] + far[1:2])


def pair_cols(ref, step, count, side):
    col = (step + side) % count
    return ref[step * WIN : (step + 1) * WIN, col * WIN : (col + 1) * WIN]


def mix_kernel(
    step, count, info, pair_ref, s_ref, far_ref, tot_ref, gate_ref, x_ref, vec,
    w_0, w_1, w_2, w_3, term_ref, ratio_ref, inv_ref, mixed_ref, res_ref, n_ref, w_ref,
):
    width = D // CHAN
    if step == 0:
        for r, ref in enumerate((w_0, w_1, w_2, w_3)):
            row = pl.multiple_of(chan_row(info, r) * width, width)
            w_ref[pl.ds(row, width)] = ref[3 * width :]
    live = live_block(info, step, WIN)
    before, after_own = side_masks()
    left, own, right = neighbours(info, step, count, s_ref, far_ref)
    grow = [jnp.exp(pair_cols(pair_ref, step, count, k).astype(F32)) - 1.0 for k in (-1, 0, 1)]
    term_l = jnp.where(before, grow[0], 0.0).astype(BF)
    term_o = grow[1].astype(BF)
    term_r = jnp.where(after_own, grow[2], 0.0).astype(BF)
    term_ref[:, :WIN] = term_l
    term_ref[:, WIN : 2 * WIN] = term_o
    term_ref[:, 2 * WIN :] = term_r
    merged = mm(term_l, left) + mm(term_o, own) + mm(term_r, right)
    merged = merged + pair_total(tot_ref, far_ref)
    inverse = 1.0 / merged[:, D:]
    ratio = merged[:, :D] * inverse
    mixed = (live * gate_ref[...].astype(F32) * ratio).astype(BF)
    ratio_ref[...] = ratio.astype(BF)
    inv_ref[...] = inverse
    mixed_ref[...] = mixed
    residual = x_ref[...].astype(F32).T + live * (mm(mixed, w_ref[...]) + vec[4:5])
    res_ref[...] = residual
    centred, _ = normalize(residual)
    n_ref[...] = (centred * vec[5:6] + vec[6:7]).astype(BF)


def mix(info, pair_bias, stacked, message, totals, gate, x_t, vec, weights, tokens=()):
    rows = x_t.shape[1]
    return call(
        mix_kernel,
        rows // WIN,
        [None, whole, whole, whole, whole, rows_of(WIN), cols_of(WIN)] + [whole] * 5,
        [rows_of(WIN)] * 6 + [whole],
        [
            shape_of((rows, 3 * WIN), BF),
            shape_of((rows, D), BF),
            shape_of((rows, D), F32),
            shape_of((rows, D), BF),
            shape_of((rows, D), F32),
            shape_of((rows, D), BF),
            shape_of((D, D), BF),
        ],
        flops=2 * rows * D * (6 * WIN + D),
        heavy=rows * D * 2,
        tokens=tokens,
    )(info, pair_bias, stacked, message, totals, gate, x_t, vec, *weights)


def feed_kernel(first, final, extra, step, count, info, n_ref, cot_ref, shift_ref, w_ref, *rest):
    rest = list(rest)
    state = [rest.pop(0), rest.pop(0)] if not first else None
    final_refs = [rest.pop(0), rest.pop(0)] if final else None
    extra_ref = rest.pop(0) if extra else None
    sum_ref, into_ref, ups_ref = rest.pop(0), rest.pop(0), rest.pop(0)
    weight_grad = rest.pop(0)
    if first:
        rest.pop(0)[...] = (cot := cot_ref[...].T)
    else:
        cot = cot_ref[...]
    grad_sc, act_sc, hidden_sc = rest
    live = lax.broadcasted_iota(jnp.int32, (n_ref.shape[0], 1), 0) < info[0]
    grad_sc[...] = jnp.where(live, cot, jnp.zeros_like(cot))
    grad = grad_sc[...]
    for f in range(0, D, WIN):
        cols, low = slice(f, f + WIN), slice(D + f, D + f + WIN)
        hidden = mm(n_ref[...], w_ref[:D, cols]) + shift_ref[:, cols]
        act, slope = gelu_pair(hidden)
        act = act.astype(BF)
        hidden_grad = (mm_t(grad, w_ref[low]) * slope).astype(BF)
        act_sc[:, cols] = act
        hidden_sc[:, cols] = hidden_grad
        ups_ref[:, cols] = col_sum(hidden_grad.astype(F32))
        of_up = t_mm(n_ref[...], hidden_grad)
        of_down = t_mm(act, grad)
        if extra:
            of_up = of_up + extra_ref[:D, cols].astype(F32)
            of_down = of_down + extra_ref[low].astype(F32)
        weight_grad[:D, cols] = of_up.astype(BF)
        weight_grad[low] = of_down.astype(BF)
    total = mm(act_sc[...], w_ref[D:])
    into = mm_t(hidden_sc[...], w_ref[:D])
    if not first:
        total, into = total + state[0][...], into + state[1][...]
    into_ref[...] = into
    if final:
        res_ref, vec = final_refs
        out = res_ref[...] + jnp.where(live, total + vec[7:8], 0.0)
        sum_ref[...] = out.T.astype(BF)
    else:
        sum_ref[...] = total


def feed(info, normed, cot, shift, weights, state=None, final=None, extra=None, tokens=()):
    rows = normed.shape[0]
    operands = [info, normed, cot, shift, weights]
    operands += list(state or ()) + list(final or ()) + ([] if extra is None else [extra])
    out_shape = [
        shape_of((rows, D), F32) if final is None else shape_of((D, rows), BF),
        shape_of((rows, D), F32),
        shape_of((1, D), F32),
    ]
    out_shape.append(shape_of((2 * D, D), BF))
    if state is None:
        out_shape.append(shape_of((rows, D), BF))
    flags = (state is None, final is not None, extra is not None)
    return call(
        functools.partial(feed_kernel, *flags),
        1,
        [None] + [whole] * (len(operands) - 1),
        [whole] * len(out_shape),
        out_shape,
        scratch=[pltpu.VMEM((rows, D), BF)] * 3,
        flops=12 * rows * D * D,
        heavy=rows * D,
        mem=18,
        tokens=tokens,
    )(*operands)


def branch_kernel(
    step, count, info, into_ref, res_ref, cot_ref, vec, w_ref, ratio_ref, inv_ref, gate_ref,
    resg_ref, branch_ref, qg_ref, g_ref, tot_ref, cols_ref,
):
    live = live_block(info, step, RB)
    upstream = into_ref[...]
    centred, inv_scale = normalize(res_ref[...])
    cot = cot_ref[...].astype(F32)
    res_grad = cot + norm_back(upstream, centred, inv_scale, vec[5:6])
    resg_ref[...] = res_grad
    branch = (live * res_grad).astype(BF)
    branch_ref[...] = branch
    mixed_grad = live * mm_t(branch, w_ref[...])
    gate, ratio = gate_ref[...].astype(F32), ratio_ref[...].astype(F32)
    pulled = mixed_grad * gate
    qg_ref[...] = (pulled * ratio * (1.0 - gate)).astype(BF)
    num = pulled * inv_ref[...]
    den = -num * ratio
    g_ref[:, :D] = num.astype(BF)
    g_ref[:, D:] = den.astype(BF)
    add_into(tot_ref, step, jnp.concatenate([col_sum(num), col_sum(den)], axis=1))
    cols = [
        col_sum(upstream * centred),
        col_sum(upstream),
        col_sum(branch.astype(F32)),
        col_sum(live * cot),
        jnp.zeros((4, D), F32),
    ]
    add_into(cols_ref, step, jnp.concatenate(cols, axis=0))


def branch_back(info, into, residual, cot, vec, out_w, ratio, inverse, gate, tokens=()):
    rows = cot.shape[0]
    wide = rows_of(RB)
    return call(
        branch_kernel,
        rows // RB,
        [None, wide, wide, wide, whole, whole, wide, wide, wide],
        [wide, wide, wide, wide, whole, whole],
        [
            shape_of((rows, D), F32),
            shape_of((rows, D), BF),
            shape_of((rows, D), BF),
            shape_of((rows, 2 * D), BF),
            shape_of((1, 2 * D), F32),
            shape_of((8, D), F32),
        ],
        flops=2 * rows * D * D,
        tokens=tokens,
    )(info, into, residual, cot, vec, out_w, ratio, inverse, gate)


def window_kernel(
    step, count, info, t_ref, g_ref, gfar_ref, tot_ref, s_ref, sfar_ref, v_ref,
    kg_ref, vg_ref, pair_ref,
):
    before, after_own = side_masks()
    left, own, right = neighbours(info, step, count, g_ref, gfar_ref)

    def term(block, part):
        block = block % count
        return t_ref[block * WIN : (block + 1) * WIN, part * WIN : (part + 1) * WIN]

    pulled = t_mm(term(step - 1, 2), left) + t_mm(term(step, 1), own)
    pulled = pulled + t_mm(term(step + 1, 0), right) + pair_total(tot_ref, gfar_ref)
    carried_grad, exp_grad = pulled[:, :D], pulled[:, D:]
    left, data, right = neighbours(info, step, count, s_ref, sfar_ref)
    keys = data[:, D:].astype(F32)
    vg_ref[...] = (carried_grad * keys).astype(BF)
    kg_ref[...] = ((exp_grad + carried_grad * v_ref[...].astype(F32)) * keys).astype(BF)
    r = info[2] ^ step
    slot = (r % 2) * 2 + r // 2
    pair_ref[slot, :, :WIN] = mm_t(own, data).astype(BF)
    side = jnp.where(before, mm_t(own, left), 0.0) + jnp.where(after_own, mm_t(own, right), 0.0)
    pair_ref[slot, :, WIN:] = side.astype(BF)


def window_back(info, terms, grads, grad_message, grad_totals, stacked, message, vals, tokens=()):
    rows = vals.shape[0]
    return call(
        window_kernel,
        rows // WIN,
        [None, whole, whole, whole, whole, whole, whole, rows_of(WIN)],
        [rows_of(WIN), rows_of(WIN), whole],
        [shape_of((rows, D), BF)] * 2 + [shape_of((rows // WIN, WIN, 2 * WIN), BF)],
        flops=WINDOW_COST,
        tokens=tokens,
    )(info, terms, grads, grad_message, grad_totals, stacked, message, vals)


def mixing_grads_kernel(
    step, count, info, q_ref, k_ref, v_ref, m_ref, n_ref, b_ref, two_ref, ups_ref,
    keep_near, keep_far, send_ref, pack_ref,
):
    half, me = info[1], info[2]
    keep_refs = (keep_near, keep_far)
    width = D // CHAN
    products = [t_mm(ref[...], n_ref[...]).astype(BF) for ref in (q_ref, k_ref, v_ref)]
    products.append(t_mm(m_ref[...], b_ref[...]).astype(BF))

    def store(core, far, rows, values):
        @pl.when(half == core)
        def _():
            keep_refs[far][rows] = values

        @pl.when(half != core)
        def _():
            send_ref[far, rows] = values

    for k, product in enumerate(products):
        for far in range(2):
            for core in range(2):
                b = 2 * far + core
                rows = slice(k * width, (k + 1) * width)
                store(core, far, rows, product[b * width : (b + 1) * width])

    sums = [col_sum(q_ref[...].astype(F32)), col_sum(v_ref[...].astype(F32))]
    turned = [jnp.concatenate([t[:, D // 2 :], t[:, : D // 2]], axis=1) for t in sums]
    pack_ref[0:2] = jnp.zeros((2, D), F32)
    pack_ref[2:6] = two_ref[0:4]
    for k in range(2):
        pack_ref[6 + k : 7 + k] = jnp.where(me // 2 == 1, turned[k], sums[k])
    for r in range(CHAN):
        pack_ref[pl.ds(8 + (me ^ r), 1)] = ups_ref[r : r + 1]
    pack_ref[12:16] = jnp.zeros((4, D), F32)


def mixing_grads(info, q_grad, k_grad, v_grad, mixed, normed, branch, two, ups, tokens=()):
    rows = normed.shape[0]
    return call(
        mixing_grads_kernel,
        1,
        [None] + [whole] * 8,
        [whole] * 4,
        [shape_of((D, D), BF)] * 2 + [shape_of((2, D, D), BF), shape_of((16, D), F32)],
        flops=8 * rows * D * D,
        mem=18,
        tokens=tokens,
    )(info, q_grad, k_grad, v_grad, mixed, normed, branch, two, ups)


def input_kernel(
    step, count, q_ref, k_ref, v_ref, w_ref, x_ref, vec, resg_ref, pack_ref, out_ref, cols_ref
):
    upstream = mm(q_ref[...], w_ref[0]) + mm(k_ref[...], w_ref[1]) + mm(v_ref[...], w_ref[2])
    centred, inv_scale = normalize(x_ref[...].astype(F32).T)
    grad = resg_ref[...] + norm_back(upstream, centred, inv_scale, vec[0:1])
    out_ref[...] = grad.T.astype(BF)
    if step == 0:
        cols_ref[...] = pack_ref[...]
    cols_ref[0:1] += col_sum(upstream * centred)
    cols_ref[1:2] += col_sum(upstream)


def input_back(q_grad, k_grad, v_grad, weights, x_t, vec, res_grad, pack, tokens=()):
    rows = res_grad.shape[0]
    wide = rows_of(RB)
    return call(
        input_kernel,
        rows // RB,
        [wide, wide, wide, whole, cols_of(RB), whole, wide, whole],
        [cols_of(RB), whole],
        [shape_of((D, rows), BF), shape_of((16, D), F32)],
        flops=INPUT_COST * rows * D * D,
        tokens=tokens,
    )(q_grad, k_grad, v_grad, weights, x_t, vec, res_grad, pack)


def sync(*arrays):
    return lax.optimization_barrier(arrays)


def row_pieces(values, rows):
    return values.reshape(-1, CHAN, rows).swapaxes(0, 1)


def to_rows(pieces):
    pieces = lax.all_to_all(pieces, "chan", 0, 0, tiled=True)
    return pieces.reshape(-1, pieces.shape[2])


def exchange_near(pieces):
    return flip(jnp.stack([pieces[1], pieces[3]]), "chan", 1)


def exchange_far(pieces, near):
    return flip(jnp.stack([pieces[2], near[1]]), "chan", 2)


def columns(pieces, near, far, me):
    return jnp.concatenate(pick([pieces[0], near[0], far[0], far[1]], me), axis=1).T


def split_rows(values, count):
    size = values.shape[0] // count
    return [values[k * size : (k + 1) * size] for k in range(count)]


def take(values, index, size, axis=0):
    return lax.dynamic_slice_in_dim(values, index * size, size, axis)


def unpack_kernel(step, count, info, packed_ref, pair_ref, out_ref, small_ref, ups_ref):
    before, after_own = side_masks()
    grow = [jnp.exp(pair_cols(pair_ref, step, count, k).astype(F32)) for k in (-1, 0, 1)]
    own = packed_ref[step, :WIN, :WIN].astype(F32)
    side = packed_ref[step, :WIN, WIN:].astype(F32)
    squares = [jnp.zeros((WIN, WIN), F32)] * count
    squares[step] = own * grow[1]
    squares[(step - 1) % count] = jnp.where(before, side * grow[0], 0.0)
    squares[(step + 1) % count] = jnp.where(after_own, side * grow[2], 0.0)
    for k in range(count):
        out_ref[:, k * WIN : (k + 1) * WIN] = squares[k]
    if step == count - 1:
        me, width = info[2], D // CHAN
        every = 0.0
        for b in range(CHAN):
            part = packed_ref[b, WIN : WIN + 32].astype(F32)
            every = every + jnp.concatenate([part[:16], part[16:, :WIN]], axis=1)
        mine = every[:8, :width]
        for k in range(1, CHAN):
            mine = jnp.where(me == k, every[:8, k * width : (k + 1) * width], mine)
        ups = every[8:9]
        for k in range(1, CHAN):
            ups = jnp.where(me == k, every[8 + k : 9 + k], ups)
        small_ref[:, :width] = mine
        small_ref[:, width:] = jnp.zeros((8, D - width), F32)
        ups_ref[...] = ups


def unpack_pairs(info, packed, pair_bias, tokens=()):
    size = pair_bias.shape[0]
    return call(
        unpack_kernel,
        size // WIN,
        [None, whole, whole],
        [rows_of(WIN), whole, whole],
        [shape_of((size, size), F32), shape_of((8, D), F32), shape_of((1, D), F32)],
        heavy=size * WIN * 3,
        tokens=tokens,
    )(info, packed, pair_bias)


def dp_stages():
    size = lax.axis_size("dp")
    stages, mask = [[1]], 2
    while mask < size:
        if mask * 2 < size:
            stages.append([mask, mask * 2, mask * 3])
            mask *= 4
        else:
            stages.append([mask])
            mask *= 2
    return stages


def add(first, second):
    return first.astype(F32) + second.astype(F32)


def dp_groups(masks):
    size = lax.axis_size("dp")
    low, count = masks[0], len(masks) + 1
    starts = [i for i in range(size) if (i // low) % count == 0]
    return [[i + low * k for k in range(count)] for i in starts]


def own_share(masks):
    return (lax.axis_index("dp") // masks[0]) % (len(masks) + 1)


def scatter_start(values, masks):
    count = len(masks) + 1
    n, rows, cols = values.shape[0], values.shape[1] // count, values.shape[2]
    if count == 2:
        return flip(take(values, 1 - own_share(masks), rows, 1), "dp", masks[0])
    parts = values.reshape(n, count, rows, cols).swapaxes(0, 1)
    return lax.all_to_all(parts, "dp", 0, 0, axis_index_groups=dp_groups(masks), tiled=True)


def scatter_end(values, got, masks):
    count = len(masks) + 1
    if count == 2:
        return add(take(values, own_share(masks), values.shape[1] // 2, 1), got).astype(BF)
    total = got[0].astype(F32)
    for k in range(1, count):
        total = total + got[k].astype(F32)
    return total.astype(BF)


def gather_start(values, masks):
    count = len(masks) + 1
    if count == 2:
        return flip(values, "dp", masks[0])
    parts = jnp.broadcast_to(values[None], (count, *values.shape))
    return lax.all_to_all(parts, "dp", 0, 0, axis_index_groups=dp_groups(masks), tiled=True)


def gather_end(values, got, masks):
    if len(masks) == 1:
        own = own_share(masks)
        pieces = [jnp.where(own == 1, got, values), jnp.where(own == 1, values, got)]
        return jnp.concatenate(pieces, axis=1)
    return got.swapaxes(0, 1).reshape(values.shape[0], -1, values.shape[2])


def scatter_all(values):
    parts = values.reshape(lax.axis_size("dp"), -1, values.shape[1])
    return lax.all_to_all(parts, "dp", 0, 0, tiled=True)


def sum_all(got):
    total = got[0].astype(F32)
    for k in range(1, got.shape[0]):
        total = total + got[k].astype(F32)
    return total.astype(BF)


def gather_all(values):
    parts = jnp.broadcast_to(values[None], (lax.axis_size("dp"), *values.shape))
    return lax.all_to_all(parts, "dp", 0, 0, tiled=True)


def scatter_rest(values, stages):
    for masks in stages:
        values = scatter_end(values, scatter_start(values, masks), masks)
    return values


def gather_rest(values, stages):
    for masks in reversed(stages):
        values = gather_end(values, gather_start(values, masks), masks)
    return values


def body(
    tokens,
    norm1_gain,
    norm1_bias,
    qkv_weight,
    qv_bias,
    pair_bias,
    out_weight,
    out_bias,
    norm2_gain,
    norm2_bias,
    up_weight,
    up_bias,
    down_weight,
    down_bias,
    lengths,
    cotangent,
):
    me = lax.axis_index("chan")
    place = lax.axis_index("dp") % 4
    half = me % 2
    rows = tokens.shape[0] // CHAN
    width = D // CHAN
    length = lax.dynamic_index_in_dim(lengths, me // 2, 0, keepdims=False)
    info = jnp.stack([jnp.clip(length - half * rows, 0, rows), half, me]).astype(jnp.int32)
    along, across, *others = dp_stages()

    mixing = jnp.concatenate([jnp.swapaxes(qkv_weight, 1, 2).reshape(-1, D), out_weight], axis=0)
    mix_q0 = flip(take(mixing, place, D // 4), "chan", 2)
    mix_near = flip(mixing, "chan", 1)
    feeding = jnp.concatenate([up_weight, down_weight], axis=0)
    feed_near = flip(feeding, "chan", 1)
    token_pieces = row_pieces(tokens.T, rows)
    mix_q0, token_pieces = sync(mix_q0, token_pieces)
    x_t = to_rows(token_pieces)
    mix_q1 = flip(mix_q0, "dp", 1)
    mix_q2 = flip(mix_q0, "dp", 2)
    small = jnp.stack(
        [norm1_gain, norm1_bias, qv_bias[0], qv_bias[1], out_bias, norm2_gain, norm2_bias, down_bias]
    )
    small = jnp.concatenate([small, up_bias.reshape(CHAN, width)], axis=0)
    small = jnp.pad(small, ((0, 4), (0, 0)))
    small = jnp.stack([small] + [flip(small, "chan", r) for r in range(1, CHAN)])
    mix_q1, mix_q2, feeding = sync(mix_q1, mix_q2, feeding)
    mix_q3 = flip(mix_q2, "dp", 1)
    vec, up_shift, tok = vectors(info, small)
    mix_q3, x_t, feeding, tok = sync(mix_q3, x_t, feeding, tok)
    mix_far = jnp.concatenate(pick([mix_q0, mix_q1, mix_q2, mix_q3], place), axis=0)
    mixing = [mixing, mix_near, mix_far, flip(mix_far, "chan", 1)]
    feed_q0 = flip(take(feeding, place, D // 2), "chan", 2)

    def message(values, totals):
        edge = lax.dynamic_slice_in_dim(values, (1 - half) * (rows - WIN), WIN, 0)
        high = totals.astype(BF)
        low = (totals - high.astype(F32)).astype(BF)
        rest = jnp.zeros((14, values.shape[1]), BF)
        return flip(jnp.concatenate([edge, high, low, rest], axis=0), "chan", 1)

    normed_one, gate, vals, stacked, totals, qkv_t, tok = project(
        info, x_t, vec, mixing, tokens=[tok]
    )
    cot_pieces = row_pieces(cotangent.T, rows)
    feed_q0, totals, cot_pieces, tok = sync(feed_q0, totals, cot_pieces, tok)
    halo = message(stacked, totals)
    feed_q1 = flip(feed_q0, "dp", 1)
    feed_q2 = flip(feed_q0, "dp", 2)
    cot_t = to_rows(cot_pieces)
    terms, ratio, inverse, mixed, residual, normed_two, out_w, tok = mix(
        info, pair_bias, stacked, halo, totals, gate, x_t, vec, mixing, tokens=[tok]
    )
    feed_q1, feed_q2, cot_t, tok = sync(feed_q1, feed_q2, cot_t, tok)
    feed_q3 = flip(feed_q2, "dp", 1)

    total, into, ups_1, grad_1, cot, tok = feed(
        info, normed_two, cot_t, up_shift[1:2], feed_near, tokens=[tok]
    )
    got_1 = flip(grad_1, "chan", 1)
    feed_q3, tok = sync(feed_q3, tok)
    feed_far = jnp.concatenate(pick([feed_q0, feed_q1, feed_q2, feed_q3], place), axis=0)
    feed_both = flip(feed_far, "chan", 1)
    total, into, ups_3, grad_3, tok = feed(
        info, normed_two, cot, up_shift[3:4], feed_both, (total, into), tokens=[tok]
    )
    got_3 = flip(grad_3, "chan", 1)
    total, into, ups_2, grad_2, tok = feed(
        info, normed_two, cot, up_shift[2:3], feed_far, (total, into), tokens=[tok]
    )
    far_p = add(grad_2[:CUT], got_3[:CUT]).astype(BF)
    far_q = add(grad_2[CUT:], got_3[CUT:]).astype(BF)[None]
    far_py = flip(far_p, "chan", 2)
    far_qx = scatter_start(far_q, along)
    layer_t, into, ups_0, near, tok = feed(
        info,
        normed_two,
        cot,
        up_shift[0:1],
        feeding,
        (total, into),
        (residual, vec),
        got_1,
        tokens=[tok],
    )
    own = own_share(along)
    rest_rows = D - CUT // 2
    near_qx = flip(
        lax.dynamic_slice_in_dim(near, CUT + (1 - own) * rest_rows, rest_rows, 0), "dp", along[0]
    )
    res_grad, branch, q_grad, grads, grad_totals, cols_two, tok = branch_back(
        info, into, residual, cot, vec, out_w, ratio, inverse, gate, tokens=[tok]
    )
    far_py, far_qx, grad_totals, tok = sync(far_py, far_qx, grad_totals, tok)
    sum_p = add(near[:CUT], far_py).astype(BF)[None]
    sum_px = scatter_start(sum_p, along)
    far_qy = flip(scatter_end(far_q, far_qx, along), "chan", 2)
    grad_halo = message(grads, grad_totals)
    k_grad, v_grad, pair_grad, tok = window_back(
        info, terms, grads, grad_halo, grad_totals, stacked, halo, vals, tokens=[tok]
    )
    t_got = flip(pair_grad[2:], "chan", 1)
    ups = jnp.concatenate([ups_0, ups_1, ups_2, ups_3], axis=0)
    m_near, m_far, send, pack, tok = mixing_grads(
        info, q_grad, k_grad, v_grad, mixed, normed_one, branch, cols_two, ups, tokens=[tok]
    )
    got = flip(send, "chan", 1)
    t_got, tok = sync(t_got, tok)
    t = add(pair_grad[:2], t_got).astype(BF)
    t_near, t_far = t[:1], flip(t[1:], "chan", 2)
    input_t, pack, tok = input_back(
        q_grad, k_grad, v_grad, qkv_t, x_t, vec, res_grad, pack, tokens=[tok]
    )

    got, tok = sync(got, tok)
    m_far = add(m_far, got[1]).astype(BF)
    near_qx, sum_px, far_qy, m_far, t_far, tok = sync(near_qx, sum_px, far_qy, m_far, t_far, tok)
    m_far = flip(m_far, "chan", 2)
    near_q = lax.dynamic_slice_in_dim(near, CUT + own * rest_rows, rest_rows, 0)
    f_q = (add(near_q, near_qx) + far_qy[0].astype(F32)).astype(BF)
    f = jnp.concatenate([scatter_end(sum_p, sum_px, along)[0], f_q], axis=0)
    f_z = lax.all_to_all(
        jnp.concatenate(
            [f[: CUT // 2].reshape(4, -1, D), f[CUT // 2 :].reshape(4, -1, D)], axis=1
        ),
        "dp",
        0,
        0,
        axis_index_groups=dp_groups(across),
        tiled=True,
    )
    m_near = add(m_near, got[0]).astype(BF)
    half_cols = 2 * WIN
    rest = jnp.pad(pack[:, half_cols:], ((0, 0), (0, half_cols - WIN)))
    pack = jnp.pad(jnp.concatenate([pack[:, :half_cols], rest], axis=0), ((0, 96), (0, 0)))
    t = jnp.concatenate([add(t_near, t_far)[0].astype(BF), pack.astype(BF)], axis=0)
    t_all = scatter_all(t)
    layer_parts = pick(split_rows(layer_t, CHAN), me)
    input_parts = pick(split_rows(input_t, CHAN), me)
    layer_near = exchange_near(layer_parts)
    input_near = exchange_near(input_parts)
    m_far, f_z, layer_near, tok = sync(m_far, f_z, layer_near, tok)
    m = add(m_near, m_far).astype(BF)[None]
    m_x = scatter_start(m, along)
    f = sum_all(f_z)[None]
    cut = CUT // 8
    f_p, f_q = [gather_rest(scatter_rest(v, others), others) for v in (f[:, :cut], f[:, cut:])]
    f = jnp.concatenate([f_p, f_q], axis=1)[0]
    f_z = [flip(f, "dp", k) for k in across]
    layer_far = exchange_far(layer_parts, layer_near)
    m_x, t_all, f, tok = sync(m_x, t_all, f, tok)
    m = scatter_end(m, m_x, along)
    m_z = scatter_start(m, across)
    t = sum_all(t_all)
    *f_z, layer_far, m = sync(*f_z, layer_far, m)
    pieces = pick([f, *f_z], own_share(across))
    f = jnp.concatenate([p[:cut] for p in pieces] + [p[cut:] for p in pieces], axis=0)
    f_x = flip(f, "dp", along[0])
    m_z, t, input_near, f = sync(m_z, t, input_near, f)
    m = gather_rest(scatter_rest(scatter_end(m, m_z, across), others), others)
    m_z = gather_start(m, across)
    layer_out = columns(layer_parts, layer_near, layer_far, me)
    input_far = exchange_far(input_parts, input_near)
    f_x, m, t, layer_out = sync(f_x, m, t, layer_out)
    t_all = gather_all(t)
    low, high = jnp.where(own == 1, f_x, f), jnp.where(own == 1, f, f_x)
    half_cut = CUT // 2
    f_u = jnp.concatenate(
        [low[:half_cut], high[:half_cut], low[half_cut : half_cut + D - CUT]], axis=0
    ).astype(F32)
    f_d = jnp.concatenate([low[half_cut + D - CUT :], high[half_cut:]], axis=0).astype(F32)
    m_z, f_u, f_d, tok = sync(m_z, f_u, f_d, tok)
    m = gather_end(m, m_z, across)
    m_x = gather_start(m, along)
    t_all, input_far, tok = sync(t_all, input_far, tok)
    t = t_all.reshape(-1, half_cols)
    t_y = flip(t, "chan", 2)
    input_grad = columns(input_parts, input_near, input_far, me)
    m_x, t_y, input_grad = sync(m_x, t_y, input_grad)
    pair = jnp.stack([t, t_y])
    beside = flip(pair, "chan", 1)
    m = gather_end(m, m_x, along)[0]
    qkv_out = jnp.swapaxes(m[: 3 * width].reshape(3, width, D).astype(F32), 1, 2)
    out_out = m[3 * width :].astype(F32)
    beside, qkv_out, out_out, tok = sync(beside, qkv_out, out_out, tok)
    table = jnp.stack(pick([pair[0], beside[0], pair[1], beside[1]], me))
    pair_out, small_out, ups_out, tok = unpack_pairs(info, table, pair_bias, tokens=[tok])
    vector = [small_out[k, :width] for k in range(8)]
    return (
        layer_out,
        input_grad,
        vector[0],
        vector[1],
        qkv_out,
        jnp.stack(vector[6:8]),
        pair_out,
        out_out,
        vector[4],
        vector[2],
        vector[3],
        f_u,
        ups_out.reshape(-1),
        f_d,
        vector[5],
    )


def solution(mesh):
    in_specs = (
        P("dp", "chan"),
        P("chan"),
        P("chan"),
        P(None, None, "chan"),
        P(None, "chan"),
        P(),
        P("chan", None),
        P("chan"),
        P("chan"),
        P("chan"),
        P(None, "chan"),
        P("chan"),
        P("chan", None),
        P("chan"),
        P("dp"),
        P("dp", "chan"),
    )
    out_specs = (
        P("dp", "chan"),
        P("dp", "chan"),
        P("chan"),
        P("chan"),
        P(None, None, "chan"),
        P(None, "chan"),
        P(),
        P("chan", None),
        P("chan"),
        P("chan"),
        P("chan"),
        P(None, "chan"),
        P("chan"),
        P("chan", None),
        P("chan"),
    )
    return jax.shard_map(body, mesh=mesh, in_specs=in_specs, out_specs=out_specs, check_vma=False)
```

```python
import functools

import jax
import jax.numpy as jnp
from jax import lax
from jax.experimental import pallas as pl
from jax.experimental.pallas import tpu as pltpu
from jax.sharding import PartitionSpec as P

D = 768
PAIR = 1024
WIN = 256
LEN = 2048
CHAN = 4
EPSILON = 1e-05
BF = jnp.bfloat16
F32 = jnp.float32
SMEM = pltpu.SMEM
MIB = 1024 * 1024
RB = 512
INPUT_COST = 72
CUT = 512
WINDOW_COST = 1000


def flip(values, axis, mask):
    size = lax.axis_size(axis)
    return lax.ppermute(values, axis, [(i, i ^ mask) for i in range(size)])


def dot_f32(left, right, dims):
    return lax.dot_general(left, right, (dims, ((), ())), preferred_element_type=F32)


def mm(left, right):
    return dot_f32(left, right, ((1,), (0,)))


def mm_t(left, right):
    return dot_f32(left, right, ((1,), (1,)))


def t_mm(left, right):
    return dot_f32(left, right, ((0,), (0,)))


def pick(pieces, index):
    low, high = index % 2 == 1, index // 2 == 1
    a, b, c, d = pieces
    a, b = jnp.where(low, b, a), jnp.where(low, a, b)
    c, d = jnp.where(low, d, c), jnp.where(low, c, d)
    a, c = jnp.where(high, c, a), jnp.where(high, a, c)
    b, d = jnp.where(high, d, b), jnp.where(high, b, d)
    return [a, b, c, d]


def call(
    kernel, steps, views, out_views, out_shape, scratch=(), flops=0, heavy=0, mem=18, tokens=()
):
    vm = pl.BlockSpec(memory_space=pltpu.VMEM)
    specs = [pl.BlockSpec(memory_space=SMEM) if v is None else vm for v in views]
    every = list(views) + list(out_views)
    first_out, count = len(views) + len(tokens), len(out_views)

    def unrolled(*refs):
        used = refs[: len(views)] + refs[first_out : first_out + count]
        refs[first_out + count][...] = jnp.zeros((8, 128), F32)
        for step in range(steps):
            parts = [r if v is None else v(r, step) for v, r in zip(every, used)]
            kernel(step, steps, *parts, *refs[first_out + count + 1 :])

    run = pl.pallas_call(
        unrolled,
        in_specs=specs + [vm] * len(tokens),
        out_specs=[vm] * (count + 1),
        out_shape=list(out_shape) + [shape_of((8, 128), F32)],
        scratch_shapes=list(scratch),
        compiler_params=pltpu.CompilerParams(vmem_limit_bytes=mem * MIB),
        cost_estimate=pl.CostEstimate(
            flops=flops, bytes_accessed=flops // 300, transcendentals=heavy
        ),
    )
    return lambda *operands: run(*operands, *tokens)


def whole(ref, step):
    return ref


def rows_of(size):
    return lambda ref, step: ref.at[step * size : (step + 1) * size]


def cols_of(size):
    return lambda ref, step: ref.at[:, step * size : (step + 1) * size]


def shape_of(shape, dtype):
    return jax.ShapeDtypeStruct(shape, dtype)


def live_block(info_ref, step, size):
    ids = lax.broadcasted_iota(jnp.int32, (size, 1), 0) + step * size
    return (ids < info_ref[0]).astype(F32)


def normalize(values):
    row_mean = jnp.mean(values, axis=1, keepdims=True)
    spread = jnp.mean(values * values, axis=1, keepdims=True) - row_mean * row_mean
    inv_scale = lax.rsqrt(spread + EPSILON)
    return (values - row_mean) * inv_scale, inv_scale


def norm_back(grad_out, centred, inv_scale, gain_vals):
    scaled = grad_out * gain_vals
    plain = jnp.mean(scaled, axis=1, keepdims=True)
    crossed = jnp.mean(scaled * centred, axis=1, keepdims=True)
    return inv_scale * (scaled - plain - centred * crossed)


def col_sum(values):
    return jnp.sum(values, axis=0, keepdims=True)


def gelu_pair(u):
    c0, c1 = 0.7978845608, 0.044715
    sq = u * u
    half = 0.5 + 0.5 * jnp.tanh(u * (c0 + c0 * c1 * sq))
    slope = half * (1.0 + (1.0 - half) * (u * (2.0 * c0 + 6.0 * c0 * c1 * sq)))
    return u * half, slope


def add_into(ref, step, values):
    ref[...] = values if step == 0 else ref[...] + values


def vector_kernel(step, count, info, small_ref, vec_ref, up_ref):
    width, me = D // CHAN, info[2]
    for k in range(CHAN):
        cols = slice(k * width, (k + 1) * width)
        own = small_ref[me ^ k].astype(F32)
        pair = small_ref[k - k % 2 + (k % 2 + info[1]) % 2].astype(F32)
        vec_ref[0:2, cols] = own[0:2]
        vec_ref[2:4, cols] = pair[2:4]
        vec_ref[4:8, cols] = own[4:8]
        ups = small_ref[k].astype(F32)
        for t in range(CHAN):
            up_ref[k : k + 1, t * width : (t + 1) * width] = ups[8 + t : 9 + t]


def vectors(info, small, tokens=()):
    return call(
        vector_kernel,
        1,
        [None, whole],
        [whole, whole],
        [shape_of((8, D), F32), shape_of((CHAN, D), F32)],
        mem=16,
        tokens=tokens,
    )(info, small)


def chan_row(info, r):
    return (r - r % 2) + (r % 2 + info[1]) % 2


def project_kernel(
    step, count, info, x_ref, vec, w_0, w_1, w_2, w_3, n_ref, gate_ref, v_ref, s_ref, tot_ref, w_ref
):
    width = D // CHAN
    if step == 0:
        for r, ref in enumerate((w_0, w_1, w_2, w_3)):
            row = pl.multiple_of(chan_row(info, r) * width, width)
            for k in range(3):
                w_ref[k, pl.ds(row, width)] = ref[k * width : (k + 1) * width]
    live = live_block(info, step, RB)
    centred, _ = normalize(x_ref[...].astype(F32).T)
    normed = (centred * vec[0:1] + vec[1:2]).astype(BF)
    n_ref[...] = normed
    gate_ref[...] = jax.nn.sigmoid(mm_t(normed, w_ref[0]) + vec[2:3]).astype(BF)
    keys = live * jnp.exp(mm_t(normed, w_ref[1]))
    vals = mm_t(normed, w_ref[2]) + vec[3:4]
    carried = keys * vals
    v_ref[...] = vals.astype(BF)
    s_ref[:, :D] = carried.astype(BF)
    s_ref[:, D:] = keys.astype(BF)
    add_into(tot_ref, step, jnp.concatenate([col_sum(carried), col_sum(keys)], axis=1))


def project(info, x_t, vec, weights, tokens=()):
    rows = x_t.shape[1]
    return call(
        project_kernel,
        rows // RB,
        [None, cols_of(RB)] + [whole] * 5,
        [rows_of(RB)] * 4 + [whole] * 2,
        [shape_of((rows, D), BF)] * 3
        + [shape_of((rows, 2 * D), BF), shape_of((1, 2 * D), F32), shape_of((3, D, D), BF)],
        flops=6 * rows * D * D,
        heavy=rows * D * 2,
        tokens=tokens,
    )(info, x_t, vec, *weights)


def side_masks():
    row_ids = lax.broadcasted_iota(jnp.int32, (WIN, WIN), 0)
    col_ids = lax.broadcasted_iota(jnp.int32, (WIN, WIN), 1)
    return col_ids > row_ids, col_ids < row_ids


def neighbours(info, step, count, ref, halo_ref):
    half = info[1]
    if step == 0:
        left = jnp.where(half == 1, halo_ref[:WIN], jnp.zeros_like(halo_ref[:WIN]))
    else:
        left = ref[(step - 1) * WIN : step * WIN]
    if step == count - 1:
        right = jnp.where(half == 0, halo_ref[:WIN], jnp.zeros_like(halo_ref[:WIN]))
    else:
        right = ref[(step + 1) * WIN : (step + 2) * WIN]
    return left, ref[step * WIN : (step + 1) * WIN], right


def pair_total(tot_ref, far_ref):
    far = far_ref[WIN : WIN + 16].astype(F32)
    return tot_ref[...] + (far[0:1] + far[1:2])


def pair_cols(ref, step, count, side):
    col = (step + side) % count
    return ref[step * WIN : (step + 1) * WIN, col * WIN : (col + 1) * WIN]


def mix_kernel(
    step, count, info, pair_ref, s_ref, far_ref, tot_ref, gate_ref, x_ref, vec,
    w_0, w_1, w_2, w_3, term_ref, ratio_ref, inv_ref, mixed_ref, res_ref, n_ref, w_ref,
):
    width = D // CHAN
    if step == 0:
        for r, ref in enumerate((w_0, w_1, w_2, w_3)):
            row = pl.multiple_of(chan_row(info, r) * width, width)
            w_ref[pl.ds(row, width)] = ref[3 * width :]
    live = live_block(info, step, WIN)
    before, after_own = side_masks()
    left, own, right = neighbours(info, step, count, s_ref, far_ref)
    grow = [jnp.exp(pair_cols(pair_ref, step, count, k).astype(F32)) - 1.0 for k in (-1, 0, 1)]
    term_l = jnp.where(before, grow[0], 0.0).astype(BF)
    term_o = grow[1].astype(BF)
    term_r = jnp.where(after_own, grow[2], 0.0).astype(BF)
    term_ref[:, :WIN] = term_l
    term_ref[:, WIN : 2 * WIN] = term_o
    term_ref[:, 2 * WIN :] = term_r
    merged = mm(term_l, left) + mm(term_o, own) + mm(term_r, right)
    merged = merged + pair_total(tot_ref, far_ref)
    inverse = 1.0 / merged[:, D:]
    ratio = merged[:, :D] * inverse
    mixed = (live * gate_ref[...].astype(F32) * ratio).astype(BF)
    ratio_ref[...] = ratio.astype(BF)
    inv_ref[...] = inverse.astype(BF)
    mixed_ref[...] = mixed
    residual = x_ref[...].astype(F32).T + live * (mm(mixed, w_ref[...]) + vec[4:5])
    res_ref[...] = residual
    centred, _ = normalize(residual)
    n_ref[...] = (centred * vec[5:6] + vec[6:7]).astype(BF)


def mix(info, pair_bias, stacked, message, totals, gate, x_t, vec, weights, tokens=()):
    rows = x_t.shape[1]
    return call(
        mix_kernel,
        rows // WIN,
        [None, whole, whole, whole, whole, rows_of(WIN), cols_of(WIN)] + [whole] * 5,
        [rows_of(WIN)] * 6 + [whole],
        [
            shape_of((rows, 3 * WIN), BF),
            shape_of((rows, D), BF),
            shape_of((rows, D), BF),
            shape_of((rows, D), BF),
            shape_of((rows, D), F32),
            shape_of((rows, D), BF),
            shape_of((D, D), BF),
        ],
        flops=2 * rows * D * (6 * WIN + D),
        heavy=rows * D * 2,
        tokens=tokens,
    )(info, pair_bias, stacked, message, totals, gate, x_t, vec, *weights)


def feed_kernel(first, final, extra, step, count, info, n_ref, cot_ref, shift_ref, w_ref, *rest):
    rest = list(rest)
    state = [rest.pop(0), rest.pop(0)] if not first else None
    final_refs = [rest.pop(0), rest.pop(0)] if final else None
    extra_ref = rest.pop(0) if extra else None
    sum_ref, into_ref, ups_ref = rest.pop(0), rest.pop(0), rest.pop(0)
    weight_grad = rest.pop(0)
    if first:
        rest.pop(0)[...] = (cot := cot_ref[...].T)
    else:
        cot = cot_ref[...]
    grad_sc, act_sc, hidden_sc = rest
    live = lax.broadcasted_iota(jnp.int32, (n_ref.shape[0], 1), 0) < info[0]
    grad_sc[...] = jnp.where(live, cot, jnp.zeros_like(cot))
    grad = grad_sc[...]
    for f in range(0, D, WIN):
        cols, low = slice(f, f + WIN), slice(D + f, D + f + WIN)
        hidden = mm(n_ref[...], w_ref[:D, cols]) + shift_ref[:, cols]
        act, slope = gelu_pair(hidden)
        act = act.astype(BF)
        hidden_grad = (mm_t(grad, w_ref[low]) * slope).astype(BF)
        act_sc[:, cols] = act
        hidden_sc[:, cols] = hidden_grad
        ups_ref[:, cols] = col_sum(hidden_grad.astype(F32))
        of_up = t_mm(n_ref[...], hidden_grad)
        of_down = t_mm(act, grad)
        if extra:
            of_up = of_up + extra_ref[:D, cols].astype(F32)
            of_down = of_down + extra_ref[low].astype(F32)
        weight_grad[:D, cols] = of_up.astype(BF)
        weight_grad[low] = of_down.astype(BF)
    total = mm(act_sc[...], w_ref[D:])
    into = mm_t(hidden_sc[...], w_ref[:D])
    if not first:
        total, into = total + state[0][...], into + state[1][...]
    into_ref[...] = into
    if final:
        res_ref, vec = final_refs
        out = res_ref[...] + jnp.where(live, total + vec[7:8], 0.0)
        sum_ref[...] = out.T.astype(BF)
    else:
        sum_ref[...] = total


def feed(info, normed, cot, shift, weights, state=None, final=None, extra=None, tokens=()):
    rows = normed.shape[0]
    operands = [info, normed, cot, shift, weights]
    operands += list(state or ()) + list(final or ()) + ([] if extra is None else [extra])
    out_shape = [
        shape_of((rows, D), F32) if final is None else shape_of((D, rows), BF),
        shape_of((rows, D), F32),
        shape_of((1, D), F32),
    ]
    out_shape.append(shape_of((2 * D, D), BF))
    if state is None:
        out_shape.append(shape_of((rows, D), BF))
    flags = (state is None, final is not None, extra is not None)
    return call(
        functools.partial(feed_kernel, *flags),
        1,
        [None] + [whole] * (len(operands) - 1),
        [whole] * len(out_shape),
        out_shape,
        scratch=[pltpu.VMEM((rows, D), BF)] * 3,
        flops=12 * rows * D * D,
        heavy=rows * D,
        mem=18,
        tokens=tokens,
    )(*operands)


def branch_kernel(
    step, count, info, into_ref, res_ref, cot_ref, vec, w_ref, ratio_ref, inv_ref, gate_ref,
    resg_ref, branch_ref, qg_ref, g_ref, tot_ref, cols_ref,
):
    live = live_block(info, step, RB)
    upstream = into_ref[...]
    centred, inv_scale = normalize(res_ref[...])
    cot = cot_ref[...].astype(F32)
    res_grad = cot + norm_back(upstream, centred, inv_scale, vec[5:6])
    resg_ref[...] = res_grad.astype(BF)
    branch = (live * res_grad).astype(BF)
    branch_ref[...] = branch
    mixed_grad = live * mm_t(branch, w_ref[...])
    gate, ratio = gate_ref[...].astype(F32), ratio_ref[...].astype(F32)
    pulled = mixed_grad * gate
    qg_ref[...] = (pulled * ratio * (1.0 - gate)).astype(BF)
    num = pulled * inv_ref[...].astype(F32)
    den = -num * ratio
    g_ref[:, :D] = num.astype(BF)
    g_ref[:, D:] = den.astype(BF)
    add_into(tot_ref, step, jnp.concatenate([col_sum(num), col_sum(den)], axis=1))
    cols = [
        col_sum(upstream * centred),
        col_sum(upstream),
        col_sum(branch.astype(F32)),
        col_sum(live * cot),
        jnp.zeros((4, D), F32),
    ]
    add_into(cols_ref, step, jnp.concatenate(cols, axis=0))


def branch_back(info, into, residual, cot, vec, out_w, ratio, inverse, gate, tokens=()):
    rows = cot.shape[0]
    wide = rows_of(RB)
    return call(
        branch_kernel,
        rows // RB,
        [None, wide, wide, wide, whole, whole, wide, wide, wide],
        [wide, wide, wide, wide, whole, whole],
        [
            shape_of((rows, D), BF),
            shape_of((rows, D), BF),
            shape_of((rows, D), BF),
            shape_of((rows, 2 * D), BF),
            shape_of((1, 2 * D), F32),
            shape_of((8, D), F32),
        ],
        flops=2 * rows * D * D,
        tokens=tokens,
    )(info, into, residual, cot, vec, out_w, ratio, inverse, gate)


def window_kernel(
    step, count, info, t_ref, g_ref, gfar_ref, tot_ref, s_ref, sfar_ref, v_ref,
    kg_ref, vg_ref, pair_ref,
):
    before, after_own = side_masks()
    left, own, right = neighbours(info, step, count, g_ref, gfar_ref)

    def term(block, part):
        block = block % count
        return t_ref[block * WIN : (block + 1) * WIN, part * WIN : (part + 1) * WIN]

    pulled = t_mm(term(step - 1, 2), left) + t_mm(term(step, 1), own)
    pulled = pulled + t_mm(term(step + 1, 0), right) + pair_total(tot_ref, gfar_ref)
    carried_grad, exp_grad = pulled[:, :D], pulled[:, D:]
    left, data, right = neighbours(info, step, count, s_ref, sfar_ref)
    keys = data[:, D:].astype(F32)
    vg_ref[...] = (carried_grad * keys).astype(BF)
    kg_ref[...] = ((exp_grad + carried_grad * v_ref[...].astype(F32)) * keys).astype(BF)
    r = info[2] ^ step
    slot = (r % 2) * 2 + r // 2
    pair_ref[slot, :, :WIN] = mm_t(own, data).astype(BF)
    side = jnp.where(before, mm_t(own, left), 0.0) + jnp.where(after_own, mm_t(own, right), 0.0)
    pair_ref[slot, :, WIN:] = side.astype(BF)


def window_back(info, terms, grads, grad_message, grad_totals, stacked, message, vals, tokens=()):
    rows = vals.shape[0]
    return call(
        window_kernel,
        rows // WIN,
        [None, whole, whole, whole, whole, whole, whole, rows_of(WIN)],
        [rows_of(WIN), rows_of(WIN), whole],
        [shape_of((rows, D), BF)] * 2 + [shape_of((rows // WIN, WIN, 2 * WIN), BF)],
        flops=WINDOW_COST,
        tokens=tokens,
    )(info, terms, grads, grad_message, grad_totals, stacked, message, vals)


def mixing_grads_kernel(
    step, count, info, q_ref, k_ref, v_ref, m_ref, n_ref, b_ref, two_ref, ups_ref,
    keep_near, keep_far, send_ref, pack_ref,
):
    half, me = info[1], info[2]
    keep_refs = (keep_near, keep_far)
    width = D // CHAN
    products = [t_mm(ref[...], n_ref[...]).astype(BF) for ref in (q_ref, k_ref, v_ref)]
    products.append(t_mm(m_ref[...], b_ref[...]).astype(BF))

    def store(core, far, rows, values):
        @pl.when(half == core)
        def _():
            keep_refs[far][rows] = values

        @pl.when(half != core)
        def _():
            send_ref[far, rows] = values

    for k, product in enumerate(products):
        for far in range(2):
            for core in range(2):
                b = 2 * far + core
                rows = slice(k * width, (k + 1) * width)
                store(core, far, rows, product[b * width : (b + 1) * width])

    sums = [col_sum(q_ref[...].astype(F32)), col_sum(v_ref[...].astype(F32))]
    turned = [jnp.concatenate([t[:, D // 2 :], t[:, : D // 2]], axis=1) for t in sums]
    pack_ref[0:2] = jnp.zeros((2, D), F32)
    pack_ref[2:6] = two_ref[0:4]
    for k in range(2):
        pack_ref[6 + k : 7 + k] = jnp.where(me // 2 == 1, turned[k], sums[k])
    for r in range(CHAN):
        pack_ref[pl.ds(8 + (me ^ r), 1)] = ups_ref[r : r + 1]
    pack_ref[12:16] = jnp.zeros((4, D), F32)


def mixing_grads(info, q_grad, k_grad, v_grad, mixed, normed, branch, two, ups, tokens=()):
    rows = normed.shape[0]
    return call(
        mixing_grads_kernel,
        1,
        [None] + [whole] * 8,
        [whole] * 4,
        [shape_of((D, D), BF)] * 2 + [shape_of((2, D, D), BF), shape_of((16, D), F32)],
        flops=8 * rows * D * D,
        mem=18,
        tokens=tokens,
    )(info, q_grad, k_grad, v_grad, mixed, normed, branch, two, ups)


def input_kernel(
    step, count, q_ref, k_ref, v_ref, w_ref, x_ref, vec, resg_ref, pack_ref, out_ref, cols_ref
):
    upstream = mm(q_ref[...], w_ref[0]) + mm(k_ref[...], w_ref[1]) + mm(v_ref[...], w_ref[2])
    centred, inv_scale = normalize(x_ref[...].astype(F32).T)
    grad = resg_ref[...].astype(F32) + norm_back(upstream, centred, inv_scale, vec[0:1])
    out_ref[...] = grad.T.astype(BF)
    if step == 0:
        cols_ref[...] = pack_ref[...]
    cols_ref[0:1] += col_sum(upstream * centred)
    cols_ref[1:2] += col_sum(upstream)


def input_back(q_grad, k_grad, v_grad, weights, x_t, vec, res_grad, pack, tokens=()):
    rows = res_grad.shape[0]
    wide = rows_of(RB)
    return call(
        input_kernel,
        rows // RB,
        [wide, wide, wide, whole, cols_of(RB), whole, wide, whole],
        [cols_of(RB), whole],
        [shape_of((D, rows), BF), shape_of((16, D), F32)],
        flops=INPUT_COST * rows * D * D,
        tokens=tokens,
    )(q_grad, k_grad, v_grad, weights, x_t, vec, res_grad, pack)


def sync(*arrays):
    return lax.optimization_barrier(arrays)


def row_pieces(values, rows):
    return values.reshape(-1, CHAN, rows).swapaxes(0, 1)


def to_rows(pieces):
    pieces = lax.all_to_all(pieces, "chan", 0, 0, tiled=True)
    return pieces.reshape(-1, pieces.shape[2])


def exchange_near(pieces):
    return flip(jnp.stack([pieces[1], pieces[3]]), "chan", 1)


def exchange_far(pieces, near):
    return flip(jnp.stack([pieces[2], near[1]]), "chan", 2)


def columns(pieces, near, far, me):
    return jnp.concatenate(pick([pieces[0], near[0], far[0], far[1]], me), axis=1).T


def split_rows(values, count):
    size = values.shape[0] // count
    return [values[k * size : (k + 1) * size] for k in range(count)]


def take(values, index, size, axis=0):
    return lax.dynamic_slice_in_dim(values, index * size, size, axis)


def unpack_kernel(step, count, info, packed_ref, pair_ref, out_ref, small_ref, ups_ref):
    before, after_own = side_masks()
    grow = [jnp.exp(pair_cols(pair_ref, step, count, k).astype(F32)) for k in (-1, 0, 1)]
    own = packed_ref[step, :WIN, :WIN].astype(F32)
    side = packed_ref[step, :WIN, WIN:].astype(F32)
    squares = [jnp.zeros((WIN, WIN), F32)] * count
    squares[step] = own * grow[1]
    squares[(step - 1) % count] = jnp.where(before, side * grow[0], 0.0)
    squares[(step + 1) % count] = jnp.where(after_own, side * grow[2], 0.0)
    for k in range(count):
        out_ref[:, k * WIN : (k + 1) * WIN] = squares[k]
    if step == count - 1:
        me, width = info[2], D // CHAN
        every = 0.0
        for b in range(CHAN):
            part = packed_ref[b, WIN : WIN + 32].astype(F32)
            every = every + jnp.concatenate([part[:16], part[16:, :WIN]], axis=1)
        mine = every[:8, :width]
        for k in range(1, CHAN):
            mine = jnp.where(me == k, every[:8, k * width : (k + 1) * width], mine)
        ups = every[8:9]
        for k in range(1, CHAN):
            ups = jnp.where(me == k, every[8 + k : 9 + k], ups)
        small_ref[:, :width] = mine
        small_ref[:, width:] = jnp.zeros((8, D - width), F32)
        ups_ref[...] = ups


def unpack_pairs(info, packed, pair_bias, tokens=()):
    size = pair_bias.shape[0]
    return call(
        unpack_kernel,
        size // WIN,
        [None, whole, whole],
        [rows_of(WIN), whole, whole],
        [shape_of((size, size), F32), shape_of((8, D), F32), shape_of((1, D), F32)],
        heavy=size * WIN * 3,
        tokens=tokens,
    )(info, packed, pair_bias)


def dp_stages():
    size = lax.axis_size("dp")
    stages, mask = [[1]], 2
    while mask < size:
        if mask * 2 < size:
            stages.append([mask, mask * 2, mask * 3])
            mask *= 4
        else:
            stages.append([mask])
            mask *= 2
    return stages


def add(first, second):
    return first.astype(F32) + second.astype(F32)


def dp_groups(masks):
    size = lax.axis_size("dp")
    low, count = masks[0], len(masks) + 1
    starts = [i for i in range(size) if (i // low) % count == 0]
    return [[i + low * k for k in range(count)] for i in starts]


def own_share(masks):
    return (lax.axis_index("dp") // masks[0]) % (len(masks) + 1)


def scatter_start(values, masks):
    count = len(masks) + 1
    n, rows, cols = values.shape[0], values.shape[1] // count, values.shape[2]
    if count == 2:
        return flip(take(values, 1 - own_share(masks), rows, 1), "dp", masks[0])
    parts = values.reshape(n, count, rows, cols).swapaxes(0, 1)
    return lax.all_to_all(parts, "dp", 0, 0, axis_index_groups=dp_groups(masks), tiled=True)


def scatter_end(values, got, masks):
    count = len(masks) + 1
    if count == 2:
        return add(take(values, own_share(masks), values.shape[1] // 2, 1), got).astype(BF)
    total = got[0].astype(F32)
    for k in range(1, count):
        total = total + got[k].astype(F32)
    return total.astype(BF)


def gather_start(values, masks):
    count = len(masks) + 1
    if count == 2:
        return flip(values, "dp", masks[0])
    parts = jnp.broadcast_to(values[None], (count, *values.shape))
    return lax.all_to_all(parts, "dp", 0, 0, axis_index_groups=dp_groups(masks), tiled=True)


def gather_end(values, got, masks):
    if len(masks) == 1:
        own = own_share(masks)
        pieces = [jnp.where(own == 1, got, values), jnp.where(own == 1, values, got)]
        return jnp.concatenate(pieces, axis=1)
    return got.swapaxes(0, 1).reshape(values.shape[0], -1, values.shape[2])


def scatter_all(values):
    parts = values.reshape(lax.axis_size("dp"), -1, values.shape[1])
    return lax.all_to_all(parts, "dp", 0, 0, tiled=True)


def sum_all(got):
    total = got[0].astype(F32)
    for k in range(1, got.shape[0]):
        total = total + got[k].astype(F32)
    return total.astype(BF)


def gather_all(values):
    parts = jnp.broadcast_to(values[None], (lax.axis_size("dp"), *values.shape))
    return lax.all_to_all(parts, "dp", 0, 0, tiled=True)


def scatter_rest(values, stages):
    for masks in stages:
        values = scatter_end(values, scatter_start(values, masks), masks)
    return values


def gather_rest(values, stages):
    for masks in reversed(stages):
        values = gather_end(values, gather_start(values, masks), masks)
    return values


def body(
    tokens,
    norm1_gain,
    norm1_bias,
    qkv_weight,
    qv_bias,
    pair_bias,
    out_weight,
    out_bias,
    norm2_gain,
    norm2_bias,
    up_weight,
    up_bias,
    down_weight,
    down_bias,
    lengths,
    cotangent,
):
    me = lax.axis_index("chan")
    place = lax.axis_index("dp") % 4
    half = me % 2
    rows = tokens.shape[0] // CHAN
    width = D // CHAN
    length = lax.dynamic_index_in_dim(lengths, me // 2, 0, keepdims=False)
    info = jnp.stack([jnp.clip(length - half * rows, 0, rows), half, me]).astype(jnp.int32)
    along, across, *others = dp_stages()

    mixing = jnp.concatenate([jnp.swapaxes(qkv_weight, 1, 2).reshape(-1, D), out_weight], axis=0)
    mix_q0 = flip(take(mixing, place, D // 4), "chan", 2)
    mix_near = flip(mixing, "chan", 1)
    feeding = jnp.concatenate([up_weight, down_weight], axis=0)
    feed_near = flip(feeding, "chan", 1)
    token_pieces = row_pieces(tokens.T, rows)
    mix_q0, token_pieces = sync(mix_q0, token_pieces)
    x_t = to_rows(token_pieces)
    mix_q1 = flip(mix_q0, "dp", 1)
    mix_q2 = flip(mix_q0, "dp", 2)
    small = jnp.stack(
        [norm1_gain, norm1_bias, qv_bias[0], qv_bias[1], out_bias, norm2_gain, norm2_bias, down_bias]
    )
    small = jnp.concatenate([small, up_bias.reshape(CHAN, width)], axis=0)
    small = jnp.pad(small, ((0, 4), (0, 0)))
    small = jnp.stack([small] + [flip(small, "chan", r) for r in range(1, CHAN)])
    mix_q1, mix_q2, feeding = sync(mix_q1, mix_q2, feeding)
    mix_q3 = flip(mix_q2, "dp", 1)
    vec, up_shift, tok = vectors(info, small)
    mix_q3, x_t, feeding, tok = sync(mix_q3, x_t, feeding, tok)
    mix_far = jnp.concatenate(pick([mix_q0, mix_q1, mix_q2, mix_q3], place), axis=0)
    mixing = [mixing, mix_near, mix_far, flip(mix_far, "chan", 1)]
    feed_q0 = flip(take(feeding, place, D // 2), "chan", 2)

    def message(values, totals):
        edge = lax.dynamic_slice_in_dim(values, (1 - half) * (rows - WIN), WIN, 0)
        high = totals.astype(BF)
        low = (totals - high.astype(F32)).astype(BF)
        rest = jnp.zeros((14, values.shape[1]), BF)
        return flip(jnp.concatenate([edge, high, low, rest], axis=0), "chan", 1)

    normed_one, gate, vals, stacked, totals, qkv_t, tok = project(
        info, x_t, vec, mixing, tokens=[tok]
    )
    cot_pieces = row_pieces(cotangent.T, rows)
    feed_q0, totals, cot_pieces, tok = sync(feed_q0, totals, cot_pieces, tok)
    halo = message(stacked, totals)
    feed_q1 = flip(feed_q0, "dp", 1)
    feed_q2 = flip(feed_q0, "dp", 2)
    cot_t = to_rows(cot_pieces)
    terms, ratio, inverse, mixed, residual, normed_two, out_w, tok = mix(
        info, pair_bias, stacked, halo, totals, gate, x_t, vec, mixing, tokens=[tok]
    )
    feed_q1, feed_q2, cot_t, tok = sync(feed_q1, feed_q2, cot_t, tok)
    feed_q3 = flip(feed_q2, "dp", 1)

    total, into, ups_1, grad_1, cot, tok = feed(
        info, normed_two, cot_t, up_shift[1:2], feed_near, tokens=[tok]
    )
    got_1 = flip(grad_1, "chan", 1)
    feed_q3, tok = sync(feed_q3, tok)
    feed_far = jnp.concatenate(pick([feed_q0, feed_q1, feed_q2, feed_q3], place), axis=0)
    feed_both = flip(feed_far, "chan", 1)
    total, into, ups_3, grad_3, tok = feed(
        info, normed_two, cot, up_shift[3:4], feed_both, (total, into), tokens=[tok]
    )
    got_3 = flip(grad_3, "chan", 1)
    total, into, ups_2, grad_2, tok = feed(
        info, normed_two, cot, up_shift[2:3], feed_far, (total, into), tokens=[tok]
    )
    far_p = add(grad_2[:CUT], got_3[:CUT]).astype(BF)
    far_q = add(grad_2[CUT:], got_3[CUT:]).astype(BF)[None]
    far_py = flip(far_p, "chan", 2)
    far_qx = scatter_start(far_q, along)
    layer_t, into, ups_0, near, tok = feed(
        info,
        normed_two,
        cot,
        up_shift[0:1],
        feeding,
        (total, into),
        (residual, vec),
        got_1,
        tokens=[tok],
    )
    own = own_share(along)
    rest_rows = D - CUT // 2
    near_qx = flip(
        lax.dynamic_slice_in_dim(near, CUT + (1 - own) * rest_rows, rest_rows, 0), "dp", along[0]
    )
    res_grad, branch, q_grad, grads, grad_totals, cols_two, tok = branch_back(
        info, into, residual, cot, vec, out_w, ratio, inverse, gate, tokens=[tok]
    )
    far_py, far_qx, grad_totals, tok = sync(far_py, far_qx, grad_totals, tok)
    sum_p = add(near[:CUT], far_py).astype(BF)[None]
    sum_px = scatter_start(sum_p, along)
    far_qy = flip(scatter_end(far_q, far_qx, along), "chan", 2)
    grad_halo = message(grads, grad_totals)
    k_grad, v_grad, pair_grad, tok = window_back(
        info, terms, grads, grad_halo, grad_totals, stacked, halo, vals, tokens=[tok]
    )
    t_got = flip(pair_grad[2:], "chan", 1)
    ups = jnp.concatenate([ups_0, ups_1, ups_2, ups_3], axis=0)
    m_near, m_far, send, pack, tok = mixing_grads(
        info, q_grad, k_grad, v_grad, mixed, normed_one, branch, cols_two, ups, tokens=[tok]
    )
    got = flip(send, "chan", 1)
    t_got, tok = sync(t_got, tok)
    t = add(pair_grad[:2], t_got).astype(BF)
    t_near, t_far = t[:1], flip(t[1:], "chan", 2)
    input_t, pack, tok = input_back(
        q_grad, k_grad, v_grad, qkv_t, x_t, vec, res_grad, pack, tokens=[tok]
    )

    got, tok = sync(got, tok)
    m_far = add(m_far, got[1]).astype(BF)
    near_qx, sum_px, far_qy, m_far, t_far, tok = sync(near_qx, sum_px, far_qy, m_far, t_far, tok)
    m_far = flip(m_far, "chan", 2)
    near_q = lax.dynamic_slice_in_dim(near, CUT + own * rest_rows, rest_rows, 0)
    f_q = (add(near_q, near_qx) + far_qy[0].astype(F32)).astype(BF)
    f = jnp.concatenate([scatter_end(sum_p, sum_px, along)[0], f_q], axis=0)
    f_z = lax.all_to_all(
        jnp.concatenate(
            [f[: CUT // 2].reshape(4, -1, D), f[CUT // 2 :].reshape(4, -1, D)], axis=1
        ),
        "dp",
        0,
        0,
        axis_index_groups=dp_groups(across),
        tiled=True,
    )
    m_near = add(m_near, got[0]).astype(BF)
    half_cols = 2 * WIN
    rest = jnp.pad(pack[:, half_cols:], ((0, 0), (0, half_cols - WIN)))
    pack = jnp.pad(jnp.concatenate([pack[:, :half_cols], rest], axis=0), ((0, 32), (0, 0)))
    t = jnp.concatenate([add(t_near, t_far)[0].astype(BF), pack.astype(BF)], axis=0)
    t_all = scatter_all(t)
    layer_parts = pick(split_rows(layer_t, CHAN), me)
    input_parts = pick(split_rows(input_t, CHAN), me)
    layer_near = exchange_near(layer_parts)
    input_near = exchange_near(input_parts)
    m_far, f_z, layer_near, tok = sync(m_far, f_z, layer_near, tok)
    m = add(m_near, m_far).astype(BF)[None]
    m_x = scatter_start(m, along)
    f = sum_all(f_z)[None]
    cut = CUT // 8
    f_p, f_q = [gather_rest(scatter_rest(v, others), others) for v in (f[:, :cut], f[:, cut:])]
    f = jnp.concatenate([f_p, f_q], axis=1)[0]
    f_z = [flip(f, "dp", k) for k in across]
    layer_far = exchange_far(layer_parts, layer_near)
    m_x, t_all, f, tok = sync(m_x, t_all, f, tok)
    m = scatter_end(m, m_x, along)
    m_z = scatter_start(m, across)
    t = sum_all(t_all)
    *f_z, layer_far, m = sync(*f_z, layer_far, m)
    pieces = pick([f, *f_z], own_share(across))
    f = jnp.concatenate([p[:cut] for p in pieces] + [p[cut:] for p in pieces], axis=0)
    f_x = flip(f, "dp", along[0])
    m_z, t, input_near, f = sync(m_z, t, input_near, f)
    m = gather_rest(scatter_rest(scatter_end(m, m_z, across), others), others)
    m_z = gather_start(m, across)
    layer_out = columns(layer_parts, layer_near, layer_far, me)
    input_far = exchange_far(input_parts, input_near)
    f_x, m, t, layer_out = sync(f_x, m, t, layer_out)
    t_all = gather_all(t)
    low, high = jnp.where(own == 1, f_x, f), jnp.where(own == 1, f, f_x)
    half_cut = CUT // 2
    f_u = jnp.concatenate(
        [low[:half_cut], high[:half_cut], low[half_cut : half_cut + D - CUT]], axis=0
    ).astype(F32)
    f_d = jnp.concatenate([low[half_cut + D - CUT :], high[half_cut:]], axis=0).astype(F32)
    m_z, f_u, f_d, tok = sync(m_z, f_u, f_d, tok)
    m = gather_end(m, m_z, across)
    m_x = gather_start(m, along)
    t_all, input_far, tok = sync(t_all, input_far, tok)
    t = t_all.reshape(-1, half_cols)
    t_y = flip(t, "chan", 2)
    input_grad = columns(input_parts, input_near, input_far, me)
    m_x, t_y, input_grad = sync(m_x, t_y, input_grad)
    pair = jnp.stack([t, t_y])
    beside = flip(pair, "chan", 1)
    m = gather_end(m, m_x, along)[0]
    qkv_out = jnp.swapaxes(m[: 3 * width].reshape(3, width, D).astype(F32), 1, 2)
    out_out = m[3 * width :].astype(F32)
    beside, qkv_out, out_out, tok = sync(beside, qkv_out, out_out, tok)
    table = jnp.stack(pick([pair[0], beside[0], pair[1], beside[1]], me))
    pair_out, small_out, ups_out, tok = unpack_pairs(info, table, pair_bias, tokens=[tok])
    vector = [small_out[k, :width] for k in range(8)]
    return (
        layer_out,
        input_grad,
        vector[0],
        vector[1],
        qkv_out,
        jnp.stack(vector[6:8]),
        pair_out,
        out_out,
        vector[4],
        vector[2],
        vector[3],
        f_u,
        ups_out.reshape(-1),
        f_d,
        vector[5],
    )


def solution(mesh):
    in_specs = (
        P("dp", "chan"),
        P("chan"),
        P("chan"),
        P(None, None, "chan"),
        P(None, "chan"),
        P(),
        P("chan", None),
        P("chan"),
        P("chan"),
        P("chan"),
        P(None, "chan"),
        P("chan"),
        P("chan", None),
        P("chan"),
        P("dp"),
        P("dp", "chan"),
    )
    out_specs = (
        P("dp", "chan"),
        P("dp", "chan"),
        P("chan"),
        P("chan"),
        P(None, None, "chan"),
        P(None, "chan"),
        P(),
        P("chan", None),
        P("chan"),
        P("chan"),
        P("chan"),
        P(None, "chan"),
        P("chan"),
        P("chan", None),
        P("chan"),
    )
    return jax.shard_map(body, mesh=mesh, in_specs=in_specs, out_specs=out_specs, check_vma=False)
```

```python
import functools

import jax
import jax.numpy as jnp
from jax import lax
from jax.experimental import pallas as pl
from jax.experimental.pallas import tpu as pltpu
from jax.sharding import PartitionSpec as P

D = 768
PAIR = 1024
WIN = 256
LEN = 2048
CHAN = 4
EPSILON = 1e-05
BF = jnp.bfloat16
F32 = jnp.float32
SMEM = pltpu.SMEM
MIB = 1024 * 1024
RB = 512
INPUT_COST = 72
CUT = 512
WINDOW_COST = 1000


def flip(values, axis, mask):
    size = lax.axis_size(axis)
    return lax.ppermute(values, axis, [(i, i ^ mask) for i in range(size)])


def dot_f32(left, right, dims):
    return lax.dot_general(left, right, (dims, ((), ())), preferred_element_type=F32)


def mm(left, right):
    return dot_f32(left, right, ((1,), (0,)))


def mm_t(left, right):
    return dot_f32(left, right, ((1,), (1,)))


def t_mm(left, right):
    return dot_f32(left, right, ((0,), (0,)))


def pick(pieces, index):
    low, high = index % 2 == 1, index // 2 == 1
    a, b, c, d = pieces
    a, b = jnp.where(low, b, a), jnp.where(low, a, b)
    c, d = jnp.where(low, d, c), jnp.where(low, c, d)
    a, c = jnp.where(high, c, a), jnp.where(high, a, c)
    b, d = jnp.where(high, d, b), jnp.where(high, b, d)
    return [a, b, c, d]


def call(
    kernel, steps, views, out_views, out_shape, scratch=(), flops=0, heavy=0, mem=18, tokens=()
):
    vm = pl.BlockSpec(memory_space=pltpu.VMEM)
    specs = [pl.BlockSpec(memory_space=SMEM) if v is None else vm for v in views]
    every = list(views) + list(out_views)
    first_out, count = len(views) + len(tokens), len(out_views)

    def unrolled(*refs):
        used = refs[: len(views)] + refs[first_out : first_out + count]
        refs[first_out + count][...] = jnp.zeros((8, 128), F32)
        for step in range(steps):
            parts = [r if v is None else v(r, step) for v, r in zip(every, used)]
            kernel(step, steps, *parts, *refs[first_out + count + 1 :])

    run = pl.pallas_call(
        unrolled,
        in_specs=specs + [vm] * len(tokens),
        out_specs=[vm] * (count + 1),
        out_shape=list(out_shape) + [shape_of((8, 128), F32)],
        scratch_shapes=list(scratch),
        compiler_params=pltpu.CompilerParams(vmem_limit_bytes=mem * MIB),
        cost_estimate=pl.CostEstimate(
            flops=flops, bytes_accessed=flops // 300, transcendentals=heavy
        ),
    )
    return lambda *operands: run(*operands, *tokens)


def whole(ref, step):
    return ref


def rows_of(size):
    return lambda ref, step: ref.at[step * size : (step + 1) * size]


def cols_of(size):
    return lambda ref, step: ref.at[:, step * size : (step + 1) * size]


def shape_of(shape, dtype):
    return jax.ShapeDtypeStruct(shape, dtype)


def live_block(info_ref, step, size):
    ids = lax.broadcasted_iota(jnp.int32, (size, 1), 0) + step * size
    return (ids < info_ref[0]).astype(F32)


def normalize(values):
    row_mean = jnp.mean(values, axis=1, keepdims=True)
    spread = jnp.mean(values * values, axis=1, keepdims=True) - row_mean * row_mean
    inv_scale = lax.rsqrt(spread + EPSILON)
    return (values - row_mean) * inv_scale, inv_scale


def norm_back(grad_out, centred, inv_scale, gain_vals):
    scaled = grad_out * gain_vals
    plain = jnp.mean(scaled, axis=1, keepdims=True)
    crossed = jnp.mean(scaled * centred, axis=1, keepdims=True)
    return inv_scale * (scaled - plain - centred * crossed)


def col_sum(values):
    return jnp.sum(values, axis=0, keepdims=True)


def gelu_pair(u):
    c0, c1 = 0.7978845608, 0.044715
    sq = u * u
    half = 0.5 + 0.5 * jnp.tanh(u * (c0 + c0 * c1 * sq))
    slope = half * (1.0 + (1.0 - half) * (u * (2.0 * c0 + 6.0 * c0 * c1 * sq)))
    return u * half, slope


def add_into(ref, step, values):
    ref[...] = values if step == 0 else ref[...] + values


def vector_kernel(step, count, info, small_ref, vec_ref, up_ref):
    width, me = D // CHAN, info[2]
    for k in range(CHAN):
        cols = slice(k * width, (k + 1) * width)
        own = small_ref[me ^ k].astype(F32)
        pair = small_ref[k - k % 2 + (k % 2 + info[1]) % 2].astype(F32)
        vec_ref[0:2, cols] = own[0:2]
        vec_ref[2:4, cols] = pair[2:4]
        vec_ref[4:8, cols] = own[4:8]
        ups = small_ref[k].astype(F32)
        for t in range(CHAN):
            up_ref[k : k + 1, t * width : (t + 1) * width] = ups[8 + t : 9 + t]


def vectors(info, small, tokens=()):
    return call(
        vector_kernel,
        1,
        [None, whole],
        [whole, whole],
        [shape_of((8, D), F32), shape_of((CHAN, D), F32)],
        mem=16,
        tokens=tokens,
    )(info, small)


def chan_row(info, r):
    return (r - r % 2) + (r % 2 + info[1]) % 2


def project_kernel(
    step, count, info, x_ref, vec, w_0, w_1, w_2, w_3, n_ref, gate_ref, v_ref, s_ref, tot_ref, w_ref
):
    width = D // CHAN
    if step == 0:
        for r, ref in enumerate((w_0, w_1, w_2, w_3)):
            row = pl.multiple_of(chan_row(info, r) * width, width)
            for k in range(3):
                w_ref[k, pl.ds(row, width)] = ref[k * width : (k + 1) * width]
    live = live_block(info, step, RB)
    centred, _ = normalize(x_ref[...].astype(F32).T)
    normed = (centred * vec[0:1] + vec[1:2]).astype(BF)
    n_ref[...] = normed
    gate_ref[...] = jax.nn.sigmoid(mm_t(normed, w_ref[0]) + vec[2:3]).astype(BF)
    keys = live * jnp.exp(mm_t(normed, w_ref[1]))
    vals = mm_t(normed, w_ref[2]) + vec[3:4]
    carried = keys * vals
    v_ref[...] = vals.astype(BF)
    s_ref[:, :D] = carried.astype(BF)
    s_ref[:, D:] = keys.astype(BF)
    add_into(tot_ref, step, jnp.concatenate([col_sum(carried), col_sum(keys)], axis=1))


def project(info, x_t, vec, weights, tokens=()):
    rows = x_t.shape[1]
    return call(
        project_kernel,
        rows // RB,
        [None, cols_of(RB)] + [whole] * 5,
        [rows_of(RB)] * 4 + [whole] * 2,
        [shape_of((rows, D), BF)] * 3
        + [shape_of((rows, 2 * D), BF), shape_of((1, 2 * D), F32), shape_of((3, D, D), BF)],
        flops=6 * rows * D * D,
        heavy=rows * D * 2,
        tokens=tokens,
    )(info, x_t, vec, *weights)


def side_masks():
    row_ids = lax.broadcasted_iota(jnp.int32, (WIN, WIN), 0)
    col_ids = lax.broadcasted_iota(jnp.int32, (WIN, WIN), 1)
    return col_ids > row_ids, col_ids < row_ids


def neighbours(info, step, count, ref, halo_ref):
    half = info[1]
    if step == 0:
        left = jnp.where(half == 1, halo_ref[:WIN], jnp.zeros_like(halo_ref[:WIN]))
    else:
        left = ref[(step - 1) * WIN : step * WIN]
    if step == count - 1:
        right = jnp.where(half == 0, halo_ref[:WIN], jnp.zeros_like(halo_ref[:WIN]))
    else:
        right = ref[(step + 1) * WIN : (step + 2) * WIN]
    return left, ref[step * WIN : (step + 1) * WIN], right


def pair_total(tot_ref, far_ref):
    far = far_ref[WIN : WIN + 16].astype(F32)
    return tot_ref[...] + (far[0:1] + far[1:2])


def pair_cols(ref, step, count, side):
    col = (step + side) % count
    return ref[step * WIN : (step + 1) * WIN, col * WIN : (col + 1) * WIN]


def mix_kernel(
    step, count, info, pair_ref, s_ref, far_ref, tot_ref, gate_ref, x_ref, vec,
    w_0, w_1, w_2, w_3, term_ref, ratio_ref, inv_ref, mixed_ref, res_ref, n_ref, w_ref,
):
    width = D // CHAN
    if step == 0:
        for r, ref in enumerate((w_0, w_1, w_2, w_3)):
            row = pl.multiple_of(chan_row(info, r) * width, width)
            w_ref[pl.ds(row, width)] = ref[3 * width :]
    live = live_block(info, step, WIN)
    before, after_own = side_masks()
    left, own, right = neighbours(info, step, count, s_ref, far_ref)
    grow = [jnp.exp(pair_cols(pair_ref, step, count, k).astype(F32)) - 1.0 for k in (-1, 0, 1)]
    term_l = jnp.where(before, grow[0], 0.0).astype(BF)
    term_o = grow[1].astype(BF)
    term_r = jnp.where(after_own, grow[2], 0.0).astype(BF)
    term_ref[:, :WIN] = term_l
    term_ref[:, WIN : 2 * WIN] = term_o
    term_ref[:, 2 * WIN :] = term_r
    merged = mm(term_l, left) + mm(term_o, own) + mm(term_r, right)
    merged = merged + pair_total(tot_ref, far_ref)
    inverse = 1.0 / merged[:, D:]
    ratio = merged[:, :D] * inverse
    mixed = (live * gate_ref[...].astype(F32) * ratio).astype(BF)
    ratio_ref[...] = ratio.astype(BF)
    inv_ref[...] = inverse.astype(BF)
    mixed_ref[...] = mixed
    residual = x_ref[...].astype(F32).T + live * (mm(mixed, w_ref[...]) + vec[4:5])
    res_ref[...] = residual
    centred, _ = normalize(residual)
    n_ref[...] = (centred * vec[5:6] + vec[6:7]).astype(BF)


def mix(info, pair_bias, stacked, message, totals, gate, x_t, vec, weights, tokens=()):
    rows = x_t.shape[1]
    return call(
        mix_kernel,
        rows // WIN,
        [None, whole, whole, whole, whole, rows_of(WIN), cols_of(WIN)] + [whole] * 5,
        [rows_of(WIN)] * 6 + [whole],
        [
            shape_of((rows, 3 * WIN), BF),
            shape_of((rows, D), BF),
            shape_of((rows, D), BF),
            shape_of((rows, D), BF),
            shape_of((rows, D), F32),
            shape_of((rows, D), BF),
            shape_of((D, D), BF),
        ],
        flops=2 * rows * D * (6 * WIN + D),
        heavy=rows * D * 2,
        tokens=tokens,
    )(info, pair_bias, stacked, message, totals, gate, x_t, vec, *weights)


def feed_kernel(first, final, extra, step, count, info, n_ref, cot_ref, shift_ref, w_ref, *rest):
    rest = list(rest)
    state = [rest.pop(0), rest.pop(0)] if not first else None
    final_refs = [rest.pop(0), rest.pop(0)] if final else None
    extra_ref = rest.pop(0) if extra else None
    sum_ref, into_ref, ups_ref = rest.pop(0), rest.pop(0), rest.pop(0)
    weight_grad = rest.pop(0)
    if first:
        rest.pop(0)[...] = (cot := cot_ref[...].T)
    else:
        cot = cot_ref[...]
    grad_sc, act_sc, hidden_sc = rest
    live = lax.broadcasted_iota(jnp.int32, (n_ref.shape[0], 1), 0) < info[0]
    grad_sc[...] = jnp.where(live, cot, jnp.zeros_like(cot))
    grad = grad_sc[...]
    for f in range(0, D, WIN):
        cols, low = slice(f, f + WIN), slice(D + f, D + f + WIN)
        hidden = mm(n_ref[...], w_ref[:D, cols]) + shift_ref[:, cols]
        act, slope = gelu_pair(hidden)
        act = act.astype(BF)
        hidden_grad = (mm_t(grad, w_ref[low]) * slope).astype(BF)
        act_sc[:, cols] = act
        hidden_sc[:, cols] = hidden_grad
        ups_ref[:, cols] = col_sum(hidden_grad.astype(F32))
        of_up = t_mm(n_ref[...], hidden_grad)
        of_down = t_mm(act, grad)
        if extra:
            of_up = of_up + extra_ref[:D, cols].astype(F32)
            of_down = of_down + extra_ref[low].astype(F32)
        weight_grad[:D, cols] = of_up.astype(BF)
        weight_grad[low] = of_down.astype(BF)
    total = mm(act_sc[...], w_ref[D:])
    into = mm_t(hidden_sc[...], w_ref[:D])
    if not first:
        total, into = total + state[0][...], into + state[1][...]
    into_ref[...] = into
    if final:
        res_ref, vec = final_refs
        out = res_ref[...] + jnp.where(live, total + vec[7:8], 0.0)
        sum_ref[...] = out.T.astype(BF)
    else:
        sum_ref[...] = total


def feed(info, normed, cot, shift, weights, state=None, final=None, extra=None, tokens=()):
    rows = normed.shape[0]
    operands = [info, normed, cot, shift, weights]
    operands += list(state or ()) + list(final or ()) + ([] if extra is None else [extra])
    out_shape = [
        shape_of((rows, D), F32) if final is None else shape_of((D, rows), BF),
        shape_of((rows, D), F32),
        shape_of((1, D), F32),
    ]
    out_shape.append(shape_of((2 * D, D), BF))
    if state is None:
        out_shape.append(shape_of((rows, D), BF))
    flags = (state is None, final is not None, extra is not None)
    return call(
        functools.partial(feed_kernel, *flags),
        1,
        [None] + [whole] * (len(operands) - 1),
        [whole] * len(out_shape),
        out_shape,
        scratch=[pltpu.VMEM((rows, D), BF)] * 3,
        flops=12 * rows * D * D,
        heavy=rows * D,
        mem=18,
        tokens=tokens,
    )(*operands)


def branch_kernel(
    step, count, info, into_ref, res_ref, cot_ref, vec, w_ref, ratio_ref, inv_ref, gate_ref,
    resg_ref, branch_ref, qg_ref, g_ref, tot_ref, cols_ref,
):
    live = live_block(info, step, RB)
    upstream = into_ref[...]
    centred, inv_scale = normalize(res_ref[...])
    cot = cot_ref[...].astype(F32)
    res_grad = cot + norm_back(upstream, centred, inv_scale, vec[5:6])
    resg_ref[...] = res_grad.astype(BF)
    branch = (live * res_grad).astype(BF)
    branch_ref[...] = branch
    mixed_grad = live * mm_t(branch, w_ref[...])
    gate, ratio = gate_ref[...].astype(F32), ratio_ref[...].astype(F32)
    pulled = mixed_grad * gate
    qg_ref[...] = (pulled * ratio * (1.0 - gate)).astype(BF)
    num = pulled * inv_ref[...].astype(F32)
    den = -num * ratio
    g_ref[:, :D] = num.astype(BF)
    g_ref[:, D:] = den.astype(BF)
    add_into(tot_ref, step, jnp.concatenate([col_sum(num), col_sum(den)], axis=1))
    cols = [
        col_sum(upstream * centred),
        col_sum(upstream),
        col_sum(branch.astype(F32)),
        col_sum(live * cot),
        jnp.zeros((4, D), F32),
    ]
    add_into(cols_ref, step, jnp.concatenate(cols, axis=0))


def branch_back(info, into, residual, cot, vec, out_w, ratio, inverse, gate, tokens=()):
    rows = cot.shape[0]
    wide = rows_of(RB)
    return call(
        branch_kernel,
        rows // RB,
        [None, wide, wide, wide, whole, whole, wide, wide, wide],
        [wide, wide, wide, wide, whole, whole],
        [
            shape_of((rows, D), BF),
            shape_of((rows, D), BF),
            shape_of((rows, D), BF),
            shape_of((rows, 2 * D), BF),
            shape_of((1, 2 * D), F32),
            shape_of((8, D), F32),
        ],
        flops=2 * rows * D * D,
        tokens=tokens,
    )(info, into, residual, cot, vec, out_w, ratio, inverse, gate)


def window_kernel(
    step, count, info, t_ref, g_ref, gfar_ref, tot_ref, s_ref, sfar_ref, v_ref,
    kg_ref, vg_ref, pair_ref,
):
    before, after_own = side_masks()
    left, own, right = neighbours(info, step, count, g_ref, gfar_ref)

    def term(block, part):
        block = block % count
        return t_ref[block * WIN : (block + 1) * WIN, part * WIN : (part + 1) * WIN]

    pulled = t_mm(term(step - 1, 2), left) + t_mm(term(step, 1), own)
    pulled = pulled + t_mm(term(step + 1, 0), right) + pair_total(tot_ref, gfar_ref)
    carried_grad, exp_grad = pulled[:, :D], pulled[:, D:]
    left, data, right = neighbours(info, step, count, s_ref, sfar_ref)
    keys = data[:, D:].astype(F32)
    vg_ref[...] = (carried_grad * keys).astype(BF)
    kg_ref[...] = ((exp_grad + carried_grad * v_ref[...].astype(F32)) * keys).astype(BF)
    r = info[2] ^ step
    slot = (r % 2) * 2 + r // 2
    pair_ref[slot, :, :WIN] = mm_t(own, data).astype(BF)
    side = jnp.where(before, mm_t(own, left), 0.0) + jnp.where(after_own, mm_t(own, right), 0.0)
    pair_ref[slot, :, WIN:] = side.astype(BF)


def window_back(info, terms, grads, grad_message, grad_totals, stacked, message, vals, tokens=()):
    rows = vals.shape[0]
    return call(
        window_kernel,
        rows // WIN,
        [None, whole, whole, whole, whole, whole, whole, rows_of(WIN)],
        [rows_of(WIN), rows_of(WIN), whole],
        [shape_of((rows, D), BF)] * 2 + [shape_of((rows // WIN, WIN, 2 * WIN), BF)],
        flops=WINDOW_COST,
        tokens=tokens,
    )(info, terms, grads, grad_message, grad_totals, stacked, message, vals)


def mixing_grads_kernel(
    step, count, info, q_ref, k_ref, v_ref, m_ref, n_ref, b_ref, two_ref, ups_ref,
    keep_near, keep_far, send_ref, pack_ref,
):
    half, me = info[1], info[2]
    keep_refs = (keep_near, keep_far)
    width = D // CHAN
    products = [t_mm(ref[...], n_ref[...]).astype(BF) for ref in (q_ref, k_ref, v_ref)]
    products.append(t_mm(m_ref[...], b_ref[...]).astype(BF))

    def store(core, far, rows, values):
        @pl.when(half == core)
        def _():
            keep_refs[far][rows] = values

        @pl.when(half != core)
        def _():
            send_ref[far, rows] = values

    for k, product in enumerate(products):
        for far in range(2):
            for core in range(2):
                b = 2 * far + core
                rows = slice(k * width, (k + 1) * width)
                store(core, far, rows, product[b * width : (b + 1) * width])

    sums = [col_sum(q_ref[...].astype(F32)), col_sum(v_ref[...].astype(F32))]
    turned = [jnp.concatenate([t[:, D // 2 :], t[:, : D // 2]], axis=1) for t in sums]
    pack_ref[0:2] = jnp.zeros((2, D), F32)
    pack_ref[2:6] = two_ref[0:4]
    for k in range(2):
        pack_ref[6 + k : 7 + k] = jnp.where(me // 2 == 1, turned[k], sums[k])
    for r in range(CHAN):
        pack_ref[pl.ds(8 + (me ^ r), 1)] = ups_ref[r : r + 1]
    pack_ref[12:16] = jnp.zeros((4, D), F32)


def mixing_grads(info, q_grad, k_grad, v_grad, mixed, normed, branch, two, ups, tokens=()):
    rows = normed.shape[0]
    return call(
        mixing_grads_kernel,
        1,
        [None] + [whole] * 8,
        [whole] * 4,
        [shape_of((D, D), BF)] * 2 + [shape_of((2, D, D), BF), shape_of((16, D), F32)],
        flops=8 * rows * D * D,
        mem=18,
        tokens=tokens,
    )(info, q_grad, k_grad, v_grad, mixed, normed, branch, two, ups)


def input_kernel(
    step, count, q_ref, k_ref, v_ref, w_ref, x_ref, vec, resg_ref, pack_ref, out_ref, cols_ref
):
    upstream = mm(q_ref[...], w_ref[0]) + mm(k_ref[...], w_ref[1]) + mm(v_ref[...], w_ref[2])
    centred, inv_scale = normalize(x_ref[...].astype(F32).T)
    grad = resg_ref[...].astype(F32) + norm_back(upstream, centred, inv_scale, vec[0:1])
    out_ref[...] = grad.T.astype(BF)
    if step == 0:
        cols_ref[...] = pack_ref[...]
    cols_ref[0:1] += col_sum(upstream * centred)
    cols_ref[1:2] += col_sum(upstream)


def input_back(q_grad, k_grad, v_grad, weights, x_t, vec, res_grad, pack, tokens=()):
    rows = res_grad.shape[0]
    wide = rows_of(RB)
    return call(
        input_kernel,
        rows // RB,
        [wide, wide, wide, whole, cols_of(RB), whole, wide, whole],
        [cols_of(RB), whole],
        [shape_of((D, rows), BF), shape_of((16, D), F32)],
        flops=INPUT_COST * rows * D * D,
        tokens=tokens,
    )(q_grad, k_grad, v_grad, weights, x_t, vec, res_grad, pack)


def sync(*arrays):
    return lax.optimization_barrier(arrays)


def row_pieces(values, rows):
    return values.reshape(-1, CHAN, rows).swapaxes(0, 1)


def to_rows(pieces):
    pieces = lax.all_to_all(pieces, "chan", 0, 0, tiled=True)
    return pieces.reshape(-1, pieces.shape[2])


def exchange_near(pieces):
    return flip(jnp.stack([pieces[1], pieces[3]]), "chan", 1)


def exchange_far(pieces, near):
    return flip(jnp.stack([pieces[2], near[1]]), "chan", 2)


def columns(pieces, near, far, me):
    return jnp.concatenate(pick([pieces[0], near[0], far[0], far[1]], me), axis=1).T


def split_rows(values, count):
    size = values.shape[0] // count
    return [values[k * size : (k + 1) * size] for k in range(count)]


def take(values, index, size, axis=0):
    return lax.dynamic_slice_in_dim(values, index * size, size, axis)


def unpack_kernel(step, count, info, packed_ref, pair_ref, out_ref, small_ref, ups_ref):
    before, after_own = side_masks()
    grow = [jnp.exp(pair_cols(pair_ref, step, count, k).astype(F32)) for k in (-1, 0, 1)]
    own = packed_ref[step, :WIN, :WIN].astype(F32)
    side = packed_ref[step, :WIN, WIN:].astype(F32)
    squares = [jnp.zeros((WIN, WIN), F32)] * count
    squares[step] = own * grow[1]
    squares[(step - 1) % count] = jnp.where(before, side * grow[0], 0.0)
    squares[(step + 1) % count] = jnp.where(after_own, side * grow[2], 0.0)
    for k in range(count):
        out_ref[:, k * WIN : (k + 1) * WIN] = squares[k]
    if step == count - 1:
        me, width = info[2], D // CHAN
        every = 0.0
        for b in range(CHAN):
            part = packed_ref[b, WIN : WIN + 32].astype(F32)
            every = every + jnp.concatenate([part[:16], part[16:, :WIN]], axis=1)
        mine = every[:8, :width]
        for k in range(1, CHAN):
            mine = jnp.where(me == k, every[:8, k * width : (k + 1) * width], mine)
        ups = every[8:9]
        for k in range(1, CHAN):
            ups = jnp.where(me == k, every[8 + k : 9 + k], ups)
        small_ref[:, :width] = mine
        small_ref[:, width:] = jnp.zeros((8, D - width), F32)
        ups_ref[...] = ups


def unpack_pairs(info, packed, pair_bias, tokens=()):
    size = pair_bias.shape[0]
    return call(
        unpack_kernel,
        size // WIN,
        [None, whole, whole],
        [rows_of(WIN), whole, whole],
        [shape_of((size, size), F32), shape_of((8, D), F32), shape_of((1, D), F32)],
        heavy=size * WIN * 3,
        tokens=tokens,
    )(info, packed, pair_bias)


def dp_stages():
    size = lax.axis_size("dp")
    stages, mask = [[1]], 2
    while mask < size:
        if mask * 2 < size:
            stages.append([mask, mask * 2, mask * 3])
            mask *= 4
        else:
            stages.append([mask])
            mask *= 2
    return stages


def add(first, second):
    return first.astype(F32) + second.astype(F32)


def dp_groups(masks):
    size = lax.axis_size("dp")
    low, count = masks[0], len(masks) + 1
    starts = [i for i in range(size) if (i // low) % count == 0]
    return [[i + low * k for k in range(count)] for i in starts]


def own_share(masks):
    return (lax.axis_index("dp") // masks[0]) % (len(masks) + 1)


def scatter_start(values, masks):
    count = len(masks) + 1
    n, rows, cols = values.shape[0], values.shape[1] // count, values.shape[2]
    if count == 2:
        return flip(take(values, 1 - own_share(masks), rows, 1), "dp", masks[0])
    parts = values.reshape(n, count, rows, cols).swapaxes(0, 1)
    return lax.all_to_all(parts, "dp", 0, 0, axis_index_groups=dp_groups(masks), tiled=True)


def scatter_end(values, got, masks):
    count = len(masks) + 1
    if count == 2:
        return add(take(values, own_share(masks), values.shape[1] // 2, 1), got).astype(BF)
    total = got[0].astype(F32)
    for k in range(1, count):
        total = total + got[k].astype(F32)
    return total.astype(BF)


def gather_start(values, masks):
    count = len(masks) + 1
    if count == 2:
        return flip(values, "dp", masks[0])
    parts = jnp.broadcast_to(values[None], (count, *values.shape))
    return lax.all_to_all(parts, "dp", 0, 0, axis_index_groups=dp_groups(masks), tiled=True)


def gather_end(values, got, masks):
    if len(masks) == 1:
        own = own_share(masks)
        pieces = [jnp.where(own == 1, got, values), jnp.where(own == 1, values, got)]
        return jnp.concatenate(pieces, axis=1)
    return got.swapaxes(0, 1).reshape(values.shape[0], -1, values.shape[2])


def scatter_all(values):
    parts = values.reshape(lax.axis_size("dp"), -1, values.shape[1])
    return lax.all_to_all(parts, "dp", 0, 0, tiled=True)


def sum_all(got):
    total = got[0].astype(F32)
    for k in range(1, got.shape[0]):
        total = total + got[k].astype(F32)
    return total.astype(BF)


def gather_all(values):
    parts = jnp.broadcast_to(values[None], (lax.axis_size("dp"), *values.shape))
    return lax.all_to_all(parts, "dp", 0, 0, tiled=True)


def scatter_rest(values, stages):
    for masks in stages:
        values = scatter_end(values, scatter_start(values, masks), masks)
    return values


def gather_rest(values, stages):
    for masks in reversed(stages):
        values = gather_end(values, gather_start(values, masks), masks)
    return values


def body(
    tokens,
    norm1_gain,
    norm1_bias,
    qkv_weight,
    qv_bias,
    pair_bias,
    out_weight,
    out_bias,
    norm2_gain,
    norm2_bias,
    up_weight,
    up_bias,
    down_weight,
    down_bias,
    lengths,
    cotangent,
):
    me = lax.axis_index("chan")
    place = lax.axis_index("dp") % 4
    half = me % 2
    rows = tokens.shape[0] // CHAN
    width = D // CHAN
    length = lax.dynamic_index_in_dim(lengths, me // 2, 0, keepdims=False)
    info = jnp.stack([jnp.clip(length - half * rows, 0, rows), half, me]).astype(jnp.int32)
    along, across, *others = dp_stages()

    mixing = jnp.concatenate([jnp.swapaxes(qkv_weight, 1, 2).reshape(-1, D), out_weight], axis=0)
    mix_q0 = flip(take(mixing, place, D // 4), "chan", 2)
    mix_near = flip(mixing, "chan", 1)
    feeding = jnp.concatenate([up_weight, down_weight], axis=0)
    feed_near = flip(feeding, "chan", 1)
    token_pieces = row_pieces(tokens.T, rows)
    mix_q0, token_pieces = sync(mix_q0, token_pieces)
    x_t = to_rows(token_pieces)
    mix_q1 = flip(mix_q0, "dp", 1)
    mix_q2 = flip(mix_q0, "dp", 2)
    small = jnp.stack(
        [norm1_gain, norm1_bias, qv_bias[0], qv_bias[1], out_bias, norm2_gain, norm2_bias, down_bias]
    )
    small = jnp.concatenate([small, up_bias.reshape(CHAN, width)], axis=0)
    small = jnp.pad(small, ((0, 4), (0, 0)))
    small = jnp.stack([small] + [flip(small, "chan", r) for r in range(1, CHAN)])
    mix_q1, mix_q2, feeding = sync(mix_q1, mix_q2, feeding)
    mix_q3 = flip(mix_q2, "dp", 1)
    vec, up_shift, tok = vectors(info, small)
    mix_q3, x_t, feeding, tok = sync(mix_q3, x_t, feeding, tok)
    mix_far = jnp.concatenate(pick([mix_q0, mix_q1, mix_q2, mix_q3], place), axis=0)
    mixing = [mixing, mix_near, mix_far, flip(mix_far, "chan", 1)]
    feed_q0 = flip(take(feeding, place, D // 2), "chan", 2)

    def message(values, totals):
        edge = lax.dynamic_slice_in_dim(values, (1 - half) * (rows - WIN), WIN, 0)
        high = totals.astype(BF)
        low = (totals - high.astype(F32)).astype(BF)
        rest = jnp.zeros((14, values.shape[1]), BF)
        return flip(jnp.concatenate([edge, high, low, rest], axis=0), "chan", 1)

    normed_one, gate, vals, stacked, totals, qkv_t, tok = project(
        info, x_t, vec, mixing, tokens=[tok]
    )
    cot_pieces = row_pieces(cotangent.T, rows)
    feed_q0, totals, cot_pieces, tok = sync(feed_q0, totals, cot_pieces, tok)
    halo = message(stacked, totals)
    feed_q1 = flip(feed_q0, "dp", 1)
    feed_q2 = flip(feed_q0, "dp", 2)
    cot_t = to_rows(cot_pieces)
    terms, ratio, inverse, mixed, residual, normed_two, out_w, tok = mix(
        info, pair_bias, stacked, halo, totals, gate, x_t, vec, mixing, tokens=[tok]
    )
    feed_q1, feed_q2, cot_t, tok = sync(feed_q1, feed_q2, cot_t, tok)
    feed_q3 = flip(feed_q2, "dp", 1)

    total, into, ups_1, grad_1, cot, tok = feed(
        info, normed_two, cot_t, up_shift[1:2], feed_near, tokens=[tok]
    )
    got_1 = flip(grad_1, "chan", 1)
    feed_q3, tok = sync(feed_q3, tok)
    feed_far = jnp.concatenate(pick([feed_q0, feed_q1, feed_q2, feed_q3], place), axis=0)
    feed_both = flip(feed_far, "chan", 1)
    total, into, ups_3, grad_3, tok = feed(
        info, normed_two, cot, up_shift[3:4], feed_both, (total, into), tokens=[tok]
    )
    got_3 = flip(grad_3, "chan", 1)
    total, into, ups_2, grad_2, tok = feed(
        info, normed_two, cot, up_shift[2:3], feed_far, (total, into), tokens=[tok]
    )
    far_p = add(grad_2[:CUT], got_3[:CUT]).astype(BF)
    far_q = add(grad_2[CUT:], got_3[CUT:]).astype(BF)[None]
    far_py = flip(far_p, "chan", 2)
    far_qx = scatter_start(far_q, along)
    layer_t, into, ups_0, near, tok = feed(
        info,
        normed_two,
        cot,
        up_shift[0:1],
        feeding,
        (total, into),
        (residual, vec),
        got_1,
        tokens=[tok],
    )
    own = own_share(along)
    rest_rows = D - CUT // 2
    near_qx = flip(
        lax.dynamic_slice_in_dim(near, CUT + (1 - own) * rest_rows, rest_rows, 0), "dp", along[0]
    )
    res_grad, branch, q_grad, grads, grad_totals, cols_two, tok = branch_back(
        info, into, residual, cot, vec, out_w, ratio, inverse, gate, tokens=[tok]
    )
    far_py, far_qx, grad_totals, tok = sync(far_py, far_qx, grad_totals, tok)
    sum_p = add(near[:CUT], far_py).astype(BF)[None]
    sum_px = scatter_start(sum_p, along)
    far_qy = flip(scatter_end(far_q, far_qx, along), "chan", 2)
    grad_halo = message(grads, grad_totals)
    k_grad, v_grad, pair_grad, tok = window_back(
        info, terms, grads, grad_halo, grad_totals, stacked, halo, vals, tokens=[tok]
    )
    t_got = flip(pair_grad[2:], "chan", 1)
    ups = jnp.concatenate([ups_0, ups_1, ups_2, ups_3], axis=0)
    m_near, m_far, send, pack, tok = mixing_grads(
        info, q_grad, k_grad, v_grad, mixed, normed_one, branch, cols_two, ups, tokens=[tok]
    )
    got = flip(send, "chan", 1)
    t_got, tok = sync(t_got, tok)
    t = add(pair_grad[:2], t_got).astype(BF)
    t_near, t_far = t[:1], flip(t[1:], "chan", 2)
    input_t, pack, tok = input_back(
        q_grad, k_grad, v_grad, qkv_t, x_t, vec, res_grad, pack, tokens=[tok]
    )

    got, tok = sync(got, tok)
    m_far = add(m_far, got[1]).astype(BF)
    near_qx, sum_px, far_qy, m_far, t_far, tok = sync(near_qx, sum_px, far_qy, m_far, t_far, tok)
    m_far = flip(m_far, "chan", 2)
    near_q = lax.dynamic_slice_in_dim(near, CUT + own * rest_rows, rest_rows, 0)
    f_q = (add(near_q, near_qx) + far_qy[0].astype(F32)).astype(BF)
    f = jnp.concatenate([scatter_end(sum_p, sum_px, along)[0], f_q], axis=0)
    f_z = lax.all_to_all(
        jnp.concatenate(
            [f[: CUT // 2].reshape(4, -1, D), f[CUT // 2 :].reshape(4, -1, D)], axis=1
        ),
        "dp",
        0,
        0,
        axis_index_groups=dp_groups(across),
        tiled=True,
    )
    m_near = add(m_near, got[0]).astype(BF)
    half_cols = 2 * WIN
    rest = jnp.pad(pack[:, half_cols:], ((0, 0), (0, half_cols - WIN)))
    pack = jnp.pad(jnp.concatenate([pack[:, :half_cols], rest], axis=0), ((0, 32), (0, 0)))
    t = jnp.concatenate([add(t_near, t_far)[0].astype(BF), pack.astype(BF)], axis=0)
    t_all = scatter_all(t)
    layer_parts = pick(split_rows(layer_t, CHAN), me)
    input_parts = pick(split_rows(input_t, CHAN), me)
    layer_near = exchange_near(layer_parts)
    input_near = exchange_near(input_parts)
    m_far, f_z, layer_near, tok = sync(m_far, f_z, layer_near, tok)
    m = add(m_near, m_far).astype(BF)[None]
    m_x = scatter_start(m, along)
    f = sum_all(f_z)[None]
    cut = CUT // 8
    f_p, f_q = [gather_rest(scatter_rest(v, others), others) for v in (f[:, :cut], f[:, cut:])]
    f = jnp.concatenate([f_p, f_q], axis=1)[0]
    f_z = [flip(f, "dp", k) for k in across]
    layer_far = exchange_far(layer_parts, layer_near)
    m_x, t_all, f, tok = sync(m_x, t_all, f, tok)
    m = scatter_end(m, m_x, along)
    m_z = scatter_start(m, across)
    t = sum_all(t_all)
    *f_z, layer_far, m = sync(*f_z, layer_far, m)
    pieces = pick([f, *f_z], own_share(across))
    f = jnp.concatenate([p[:cut] for p in pieces] + [p[cut:] for p in pieces], axis=0)
    f_x = flip(f, "dp", along[0])
    m_z, t, input_near, f = sync(m_z, t, input_near, f)
    m = gather_rest(scatter_rest(scatter_end(m, m_z, across), others), others)
    m_z = gather_start(m, across)
    layer_out = columns(layer_parts, layer_near, layer_far, me)
    input_far = exchange_far(input_parts, input_near)
    f_x, m, t, layer_out = sync(f_x, m, t, layer_out)
    t_all = gather_all(t)
    m_z, tok = sync(m_z, tok)
    m = gather_end(m, m_z, across)
    m_x = gather_start(m, along)
    t_all, input_far, tok = sync(t_all, input_far, tok)
    low, high = jnp.where(own == 1, f_x, f), jnp.where(own == 1, f, f_x)
    half_cut = CUT // 2
    f_u = jnp.concatenate(
        [low[:half_cut], high[:half_cut], low[half_cut : half_cut + D - CUT]], axis=0
    ).astype(F32)
    f_d = jnp.concatenate([low[half_cut + D - CUT :], high[half_cut:]], axis=0).astype(F32)
    t = t_all.reshape(-1, half_cols)
    t_y = flip(t, "chan", 2)
    input_grad = columns(input_parts, input_near, input_far, me)
    m_x, t_y, input_grad, f_u, f_d = sync(m_x, t_y, input_grad, f_u, f_d)
    pair = jnp.stack([t, t_y])
    beside = flip(pair, "chan", 1)
    m = gather_end(m, m_x, along)[0]
    qkv_out = jnp.swapaxes(m[: 3 * width].reshape(3, width, D).astype(F32), 1, 2)
    out_out = m[3 * width :].astype(F32)
    beside, qkv_out, out_out, tok = sync(beside, qkv_out, out_out, tok)
    table = jnp.stack(pick([pair[0], beside[0], pair[1], beside[1]], me))
    pair_out, small_out, ups_out, tok = unpack_pairs(info, table, pair_bias, tokens=[tok])
    vector = [small_out[k, :width] for k in range(8)]
    return (
        layer_out,
        input_grad,
        vector[0],
        vector[1],
        qkv_out,
        jnp.stack(vector[6:8]),
        pair_out,
        out_out,
        vector[4],
        vector[2],
        vector[3],
        f_u,
        ups_out.reshape(-1),
        f_d,
        vector[5],
    )


def solution(mesh):
    in_specs = (
        P("dp", "chan"),
        P("chan"),
        P("chan"),
        P(None, None, "chan"),
        P(None, "chan"),
        P(),
        P("chan", None),
        P("chan"),
        P("chan"),
        P("chan"),
        P(None, "chan"),
        P("chan"),
        P("chan", None),
        P("chan"),
        P("dp"),
        P("dp", "chan"),
    )
    out_specs = (
        P("dp", "chan"),
        P("dp", "chan"),
        P("chan"),
        P("chan"),
        P(None, None, "chan"),
        P(None, "chan"),
        P(),
        P("chan", None),
        P("chan"),
        P("chan"),
        P("chan"),
        P(None, "chan"),
        P("chan"),
        P("chan", None),
        P("chan"),
    )
    return jax.shard_map(body, mesh=mesh, in_specs=in_specs, out_specs=out_specs, check_vma=False)
```
